32 devices in a mesh: row: 4 (over y, x), seq: 8 (over z, core).
Axes of the slice: x: 2, y: 2, z: 4, core: 2. Of those that a mesh axis runs over, the one named last changes fastest.
Arguments:
- tokens: bfloat16 [16, 2048, 2048], P('row', 'seq'), may hold values from -6 to 6
- lengths: int32 [16], P('row'), may hold values from 64 to 2048, as said below
- cotangent: bfloat16 [16, 2048, 2048], P('row', 'seq'), may hold values from -6 to 6
- w_qkv: bfloat16 [2048, 1536], P(('row', 'seq')), may hold values from -0.125 to 0.125
- w_out: bfloat16 [2048, 1024], P(('row', 'seq')), may hold values from -1.5 to 1.5
- w_gateup: bfloat16 [2048, 2048], P(('row', 'seq')), may hold values from -0.125 to 0.125
- w_down: bfloat16 [2048, 1024], P(('row', 'seq')), may hold values from -0.1875 to 0.1875
- norm_attn: bfloat16 [2048], P(('row', 'seq')), may hold values from 0.5 to 1.5
- norm_ffn: bfloat16 [2048], P(('row', 'seq')), may hold values from 0.5 to 1.5
- q_gain: bfloat16 [64], replicated, may hold values from 0.099609375 to 1.8984375
- k_gain: bfloat16 [64], replicated, may hold values from 0.099609375 to 1.8984375
Outputs:
- output: bfloat16 [16, 2048, 2048], P('row', 'seq')
- grad_tokens: bfloat16 [16, 2048, 2048], P('row', 'seq')
- grad_qkv: float32 [2048, 1536], P(('row', 'seq'))
- grad_out: float32 [2048, 1024], P(('row', 'seq'))
- grad_gateup: float32 [2048, 2048], P(('row', 'seq'))
- grad_down: float32 [2048, 1024], P(('row', 'seq'))
- grad_norm_attn: float32 [2048], P(('row', 'seq'))
- grad_norm_ffn: float32 [2048], P(('row', 'seq'))
- grad_q_gain: float32 [64], replicated
- grad_k_gain: float32 [64], replicated
The draws below stay inside these ranges and needn't reach their ends.
Inputs may be any that keep to these rules, and one draw needn't show every extreme that they name: `lengths`: each aligned block of 4 entries (the sequences of one index of row) holds at least one entry equal to 2048; the others are heavy-tailed.
All inputs are finite; a program needn't handle non-finite values.
Results may differ from the reference program's by a relative error of at most 0.033.
Values may be sent and summed in bfloat16 or wider, within the bound.
No kernel may reach another device: no remote copies, remote signals or barrier semaphores. Data moves between devices by JAX's collectives and lax.ppermute only.
A program may use at most 448 MiB of HBM per device.

```python
from functools import partial
import jax
import jax.numpy as jnp
from jax import lax

D = 2048
HEADS = 16
KV_HEADS = 4
HD = 64
FF = 1024
LEN = 2048
MIN_LEN = 64
SEQS_DEV = 4
SEQS = 16
QW = 1024
KVW = 256


def draw_lengths(key, part):
    key = jax.random.fold_in(key, 11)
    key_expo, key_base, key_slot = jax.random.split(key, 3)
    exponent = jax.random.randint(key_expo, (SEQS,), 0, 6)
    base_len = MIN_LEN * 2 ** exponent + jax.random.randint(key_base, (SEQS,), 0, MIN_LEN)
    slot_pick = jax.random.randint(key_slot, (SEQS // SEQS_DEV,), 0, SEQS_DEV)
    full_slot = jnp.repeat(slot_pick, SEQS_DEV) == jnp.arange(SEQS) % SEQS_DEV
    return jnp.where(full_slot, LEN, jnp.minimum(base_len, LEN)).astype(jnp.int32)


def levels(key, shape, cuts, low, largest):
    factor_of = 1.0
    for position, shards_of in cuts:
        draws = jax.random.uniform(jax.random.fold_in(jax.random.fold_in(key, 6), position), (shards_of,), jnp.float32, low / len(cuts), largest / len(cuts))
        factor_of = factor_of * jnp.repeat(jnp.exp(draws), shape[position] // shards_of).reshape((-1,) + (1,) * (len(shape) - 1 - position))
    return factor_of


def centred(stream_key, extent, deviation, most, pieces=(), kind=jnp.bfloat16):
    gain = levels(stream_key, extent, pieces, -0.22, 0.18) if pieces else 1.0
    array = jax.random.normal(stream_key, extent, jnp.float32) * deviation * gain
    return jnp.minimum(jnp.maximum(array, -most), most).astype(kind)


def setup_inputs(seed: int = 0) -> dict:
    keys = jax.random.split(jax.random.key(seed), 12)
    return {
        "tokens": centred(keys[0], (SEQS, LEN, D), 1.0, 6.0, ((0, 4), (1, 8))),
        "lengths": draw_lengths(jax.random.fold_in(keys[11], 71), 0),
        "cotangent": centred(keys[2], (SEQS, LEN, D), 1.0, 6.0, ((0, 4), (1, 8))),
        "w_qkv": centred(keys[3], (D, QW + 2 * KVW), D ** -0.5, 0.125, ((0, 32),)),
        "w_out": centred(keys[4], (D, QW), (max(QW // 64, 1)) ** -0.5, 1.5, ((0, 32),)),
        "w_gateup": centred(keys[5], (D, 2 * FF), D ** -0.5, 0.125, ((0, 32),)),
        "w_down": centred(keys[6], (D, FF), FF ** -0.5, 0.1875, ((0, 32),)),
        "norm_attn": jnp.clip(1.0 + 0.1 * jax.random.normal(keys[7], (D,), jnp.float32), 0.5, 1.5).astype(jnp.bfloat16),
        "norm_ffn": jnp.clip(1.0 + 0.1 * jax.random.normal(keys[8], (D,), jnp.float32), 0.5, 1.5).astype(jnp.bfloat16),
        "q_gain": jnp.clip(1.0 + 0.18 * jax.random.normal(keys[9], (HD,), jnp.float32), 0.099609375, 1.8984375).astype(jnp.bfloat16),
        "k_gain": jnp.clip(1.0 + 0.18 * jax.random.normal(keys[10], (HD,), jnp.float32), 0.099609375, 1.8984375).astype(jnp.bfloat16),
    }


norm_eps = 1e-06
theta_base = 10000.0
neg_big = -1e+30

@jax.custom_vjp
def low(v):
    return lax.optimization_barrier(v.astype(jnp.bfloat16)).astype(jnp.float32)

@jax.custom_vjp
def low_back(v):
    return v

def low_keep(v):
    return (low(v), None)

def low_pass(kept, grad):
    return (grad,)

def back_keep(v):
    return (v, None)

def back_low(kept, grad):
    return (low(grad),)
low.defvjp(low_keep, low_pass)
low_back.defvjp(back_keep, back_low)

def both_ways(values):
    return low_back(low(values))

def rms_norm(values, gain_vec):
    return values * lax.rsqrt(lax.optimization_barrier(jnp.mean(values * values, axis=-1, keepdims=True)) + norm_eps) * gain_vec

def rotate(values, cosine_table, sine_table):
    half_dim = values.shape[-1] // 2
    first_half = values[..., :half_dim]
    second_half = values[..., half_dim:]
    return jnp.concatenate([first_half * cosine_table - second_half * sine_table, second_half * cosine_table + first_half * sine_table], axis=-1)

def highest(left, right):
    return jnp.dot(left, right, precision=lax.Precision.HIGHEST, preferred_element_type=jnp.float32)

def sequence_layer(weights, inputs):
    w_qkv, w_out, w_gateup, w_down, norm_attn, norm_ffn, q_gain, k_gain = weights
    tokens, length = inputs
    group_size = HEADS // KV_HEADS
    half_dim = HD // 2
    positions = jnp.arange(LEN, dtype=jnp.float32)
    inverse = theta_base ** (-jnp.arange(half_dim, dtype=jnp.float32) * 2.0 / HD)
    angles = positions[:, None] * inverse[None, :]
    cosine_table = jnp.cos(angles)[:, None, :]
    sine_table = jnp.sin(angles)[:, None, :]
    normed = low(rms_norm(tokens, norm_attn))
    projected = low_back(highest(normed, w_qkv))
    query_all = projected[:, :QW].reshape(LEN, HEADS, HD)
    key_all = projected[:, QW:QW + KVW].reshape(LEN, KV_HEADS, HD)
    value_all = both_ways(projected[:, QW + KVW:].reshape(LEN, KV_HEADS, HD))
    query_all = both_ways(rotate(rms_norm(query_all, q_gain), cosine_table, sine_table))
    query_all = query_all.reshape(LEN, KV_HEADS, group_size, HD)
    key_all = both_ways(rotate(rms_norm(key_all, k_gain), cosine_table, sine_table))
    block_rows = min(512, LEN)
    key_pos = jnp.arange(LEN, dtype=jnp.int32)

    def attend(block_index):
        query_block = lax.dynamic_slice_in_dim(query_all, (block_index * block_rows).astype(jnp.int32), block_rows, 0)
        query_pos = (block_index * block_rows).astype(jnp.int32) + jnp.arange(block_rows, dtype=jnp.int32)
        scores = jnp.einsum('qkgd,nkd->qkgn', query_block, key_all, precision=lax.Precision.HIGHEST)
        scores = low_back(scores * HD ** (-0.5))
        allowed = (key_pos[None, :] <= query_pos[:, None]) & (key_pos[None, :] < length)
        scores = jnp.where(allowed[:, None, None, :], scores, neg_big)
        probabilities = low(jax.nn.softmax(scores, axis=-1))
        mixed_block = jnp.einsum('qkgn,nkd->qkgd', probabilities, value_all, precision=lax.Precision.HIGHEST)
        return mixed_block.reshape(block_rows, QW)
    attended = lax.map(jax.checkpoint(attend), jnp.arange(LEN // block_rows, dtype=jnp.int32))
    attended = both_ways(attended.reshape(LEN, QW))
    middle = tokens + low_back(highest(attended, w_out.T))
    normed_ffn = low(rms_norm(middle, norm_ffn))
    gate_up = low_back(highest(normed_ffn, w_gateup))
    hidden = low(jax.nn.silu(gate_up[:, :FF]) * gate_up[:, FF:])
    return middle + low_back(highest(hidden, w_down.T))

def reference(tokens, lengths, cotangent, w_qkv, w_out, w_gateup, w_down, norm_attn, norm_ffn, q_gain, k_gain):
    weights = tuple((array_in.astype(jnp.float32) for array_in in (w_qkv, w_out, w_gateup, w_down, norm_attn, norm_ffn, q_gain, k_gain)))

    def forward(inputs_f, weight_set):
        return lax.map(jax.checkpoint(partial(sequence_layer, weight_set)), (inputs_f, lengths))
    output, pullback = jax.vjp(forward, tokens.astype(jnp.float32), weights)
    row_valid = (jnp.arange(LEN, dtype=jnp.int32)[None, :] < lengths[:, None]).astype(jnp.float32)
    grad_in, grad_weights = pullback(cotangent.astype(jnp.float32) * row_valid[:, :, None])
    return (output.astype(jnp.bfloat16), grad_in.astype(jnp.bfloat16), grad_weights[0], grad_weights[1], grad_weights[2], grad_weights[3], grad_weights[4], grad_weights[5], grad_weights[6], grad_weights[7])
```

```python
import functools
import math

import jax
import jax.numpy as jnp
from jax import lax
from jax.experimental import pallas as pl
from jax.experimental.pallas import tpu as pltpu
from jax.sharding import PartitionSpec as P

norm_eps = 1e-06
theta_base = 10000.0
both = ("row", "seq")
f32 = jnp.float32
bf16 = jnp.bfloat16
vmem_cap = 56 * 1024 * 1024
NN = (((1,), (0,)), ((), ()))
NT = (((1,), (1,)), ((), ()))
TN = (((0,), (0,)), ((), ()))


def mm(left, right, dims=NN):
    return lax.dot_general(left, right, dims, preferred_element_type=f32)


def params(n_grid):
    return pltpu.CompilerParams(
        dimension_semantics=("arbitrary",) * n_grid, vmem_limit_bytes=vmem_cap
    )


def lane_iota(shape):
    return lax.broadcasted_iota(jnp.int32, shape, len(shape) - 1)


def group_matrix(head_dim, value):
    i = lax.broadcasted_iota(jnp.int32, (128, 128), 0) // head_dim
    j = lax.broadcasted_iota(jnp.int32, (128, 128), 1) // head_dim
    return jnp.where(i == j, value, 0.0).astype(bf16)


def group_sum(values, matrix):
    high = values.astype(bf16)
    low = (values - high.astype(f32)).astype(bf16)
    return mm(high, matrix) + mm(low, matrix)


def turn(values, cos_ref, sa_ref, sb_ref):
    return (
        values * cos_ref[...]
        + pltpu.roll(values, 96, 1) * sa_ref[...]
        + pltpu.roll(values, 32, 1) * sb_ref[...]
    )


def turn_back(values, cos_ref, sa_ref, sb_ref):
    return (
        values * cos_ref[...]
        - pltpu.roll(values, 96, 1) * sa_ref[...]
        - pltpu.roll(values, 32, 1) * sb_ref[...]
    )


def project_kernel(
    normed_slabs,
    head_dim,
    with_scale,
    tok_ref,
    w_ref,
    gain_ref,
    cos_ref,
    sa_ref,
    sb_ref,
    *rest,
):
    if with_scale:
        heads_ref, raw_ref, scale_ref = rest
        x = tok_ref[...].astype(f32)
        scale = lax.rsqrt(jnp.mean(x * x, axis=-1, keepdims=True) + norm_eps)
        scale_ref[...] = jnp.broadcast_to(scale, scale_ref.shape)
    else:
        scale_in_ref, heads_ref, raw_ref = rest
        scale = scale_in_ref[:, :1]
    projected = mm(tok_ref[...], w_ref[...]) * scale
    mean_matrix = group_matrix(head_dim, 1.0 / head_dim)
    raw_ref[...] = projected[:, : raw_ref.shape[1]].astype(bf16)
    for slab in range(heads_ref.shape[1] // 128):
        lanes = slice(128 * slab, 128 * slab + 128)
        part = projected[:, lanes]
        if slab < normed_slabs:
            inverse = lax.rsqrt(group_sum(part * part, mean_matrix) + norm_eps)
            part = turn(part * inverse * gain_ref[...], cos_ref, sa_ref, sb_ref)
        heads_ref[:, lanes] = part.astype(bf16)


def project(tokens, weight, gain, tables, normed, head_dim, scale=None):
    rows, width = tokens.shape
    out_width = weight.shape[1]
    span = tables[0].shape[0]
    row_block = lambda n: pl.BlockSpec((span, n), lambda i: (i, 0))
    fixed = lambda a: pl.BlockSpec(a.shape, lambda i: (0,) * a.ndim)
    args = [tokens, weight, gain, *tables]
    in_specs = [row_block(width), fixed(weight), fixed(gain)] + [fixed(t) for t in tables]
    out_shape = [
        jax.ShapeDtypeStruct((rows, out_width), bf16),
        jax.ShapeDtypeStruct((rows, normed), bf16),
    ]
    out_specs = [row_block(out_width), row_block(normed)]
    if scale is None:
        out_shape.append(jax.ShapeDtypeStruct((rows, 128), f32))
        out_specs.append(row_block(128))
    else:
        args.append(scale)
        in_specs.append(row_block(128))
    return pl.pallas_call(
        functools.partial(project_kernel, normed // 128, head_dim, scale is None),
        grid=(rows // span,),
        in_specs=in_specs,
        out_specs=out_specs,
        out_shape=out_shape,
        compiler_params=params(1),
        cost_estimate=pl.CostEstimate(
            flops=2 * rows * width * out_width,
            bytes_accessed=2 * (rows * (width + 2 * out_width) + width * out_width),
            transcendentals=rows * normed,
        ),
    )(*args)


def placed_pair(slab, parity, low):
    values = slab.astype(f32)
    rolled = pltpu.roll(values, 64, 1)
    first = jnp.where(low, jnp.where(parity == 0, values, rolled), 0.0)
    second = jnp.where(low, 0.0, jnp.where(parity == 0, rolled, values))
    return first, second


def stacked(ref):
    return jnp.concatenate([ref[0, :, :128], ref[0, :, 128:]], axis=0)


def key_blocks(info_ref, seq, base, chunk_len, span, block, backward):
    offset = info_ref[0]
    length = info_ref[1 + seq]
    whole = jnp.clip(jnp.minimum(offset + 1, length) - base, 0, chunk_len) // block
    reach = jnp.clip(jnp.minimum(offset + span, length) - base, 0, chunk_len)
    count = (reach + block - 1) // block
    alive = base >= 0
    if backward:
        alive = alive & (offset < length)
    return jnp.where(alive, whole, 0), jnp.where(alive, count, 0)


def attend_kernel(block, n_chunks, with_acc, finish, info_ref, q_ref, *refs):
    keys, refs = refs[:n_chunks], refs[n_chunks:]
    values, refs = refs[:n_chunks], refs[n_chunks:]
    if with_acc:
        acc_in, refs = refs[0], refs[1:]
    if finish:
        out_ref, log_ref, acc = refs
    else:
        (acc,) = refs
        acc = acc.at[0, 0]
    seq = pl.program_id(0)
    parity = lax.rem(pl.program_id(1), 2)
    span = q_ref.shape[1]
    low = lane_iota((block, 128)) < 64
    ones_low = jnp.where(low, 1.0, 0.0).astype(bf16)
    ones_high = jnp.where(low, 0.0, 1.0).astype(bf16)
    queries = stacked(q_ref)
    acc[...] = acc_in[0, 0] if with_acc else jnp.zeros(acc.shape, f32)

    for chunk in range(n_chunks):
        base = info_ref[1 + pl.num_programs(0) + chunk]
        chunk_len = keys[chunk].shape[1]
        whole, count = key_blocks(info_ref, seq, base, chunk_len, span, block, False)

        def step(index, masked, chunk=chunk, base=base):
            rows = pl.ds(pl.multiple_of(index * block, block), block)
            k0, k1 = placed_pair(keys[chunk][0, rows, :], parity, low)
            v0, v1 = placed_pair(values[chunk][0, rows, :], parity, low)
            k_pair = jnp.concatenate([k0, k1], axis=0).astype(bf16)
            v_pair = jnp.concatenate(
                [
                    jnp.concatenate([v0.astype(bf16), ones_low], axis=1),
                    jnp.concatenate([v1.astype(bf16), ones_high], axis=1),
                ],
                axis=0,
            )
            weights = jnp.exp2(mm(queries, k_pair, NT))
            if masked:
                shape = (2 * span, 2 * block)
                q_pos = info_ref[0] + lax.rem(lax.broadcasted_iota(jnp.int32, shape, 0), span)
                k_pos = base + index * block + lax.rem(lane_iota(shape), block)
                ok = (k_pos <= q_pos) & (k_pos < info_ref[1 + seq])
                weights = jnp.where(ok, weights, 0.0)
            acc[...] += mm(weights.astype(bf16), v_pair)

        @pl.loop(0, whole)
        def _(index):
            step(index, False)

        @pl.loop(whole, count)
        def _(index):
            step(index, True)

    if finish:
        totals = acc[:, 128:]
        heads = (acc[:, :128] / totals).astype(bf16)
        logs = jnp.log2(totals)
        out_ref[0, :, :128] = heads[:span]
        out_ref[0, :, 128:] = heads[span:]
        log_ref[0, :, :128] = logs[:span]
        log_ref[0, :, 128:] = logs[span:]


def attend(info, queries, chunks, acc=None, finish=True):
    seqs, span, width = queries.shape
    kv_heads = width // 256
    q_spec = pl.BlockSpec((1, span, 256), lambda b, h, *_: (b, 0, h))
    acc_spec = pl.BlockSpec((1, 1, 2 * span, 256), lambda b, h, *_: (b, h, 0, 0))
    acc_shape = jax.ShapeDtypeStruct((seqs, kv_heads, 2 * span, 256), f32)
    block = min(256, chunks[0].shape[1])
    key_specs = [
        pl.BlockSpec((1, c.shape[1], 128), lambda b, h, *_: (b, 0, h // 2)) for c in chunks
    ]
    value_specs = [
        pl.BlockSpec((1, c.shape[1], 128), lambda b, h, *_: (b, 0, kv_heads // 2 + h // 2))
        for c in chunks
    ]
    args = [queries, *chunks, *chunks]
    in_specs = [q_spec, *key_specs, *value_specs]
    if acc is not None:
        args.append(acc)
        in_specs.append(acc_spec)
    if finish:
        out_shape = [
            jax.ShapeDtypeStruct(queries.shape, bf16),
            jax.ShapeDtypeStruct(queries.shape, f32),
        ]
        out_specs = [q_spec, q_spec]
        scratch = [pltpu.VMEM((2 * span, 256), f32)]
    else:
        out_shape, out_specs, scratch = acc_shape, acc_spec, []
    keys = sum(c.shape[1] for c in chunks)
    return pl.pallas_call(
        functools.partial(attend_kernel, block, len(chunks), acc is not None, finish),
        grid_spec=pltpu.PrefetchScalarGridSpec(
            num_scalar_prefetch=1,
            grid=(seqs, kv_heads),
            in_specs=in_specs,
            out_specs=out_specs,
            scratch_shapes=scratch,
        ),
        out_shape=out_shape,
        compiler_params=params(2),
        cost_estimate=pl.CostEstimate(
            flops=4 * 4 * seqs * span * width * keys,
            bytes_accessed=4 * seqs * (span * width * 3 + keys * width // 2),
            transcendentals=seqs * span * width // 64 * keys,
        ),
    )(info, *args)


def attend_back_kernel(block, with_acc, finish, info_ref, q_ref, do_ref, o_ref, log_ref, k_ref, v_ref, *refs):
    if with_acc:
        acc_in, refs = refs[0], refs[1:]
    dk_ref, dv_ref, dq_ref, *refs = refs
    acc, q_wide, do_wide = refs
    seq = pl.program_id(0)
    parity = lax.rem(pl.program_id(1), 2)
    span = q_ref.shape[1]
    chunk_len = k_ref.shape[1]
    base = info_ref[1 + pl.num_programs(0)]
    whole, count = key_blocks(info_ref, seq, base, chunk_len, span, block, True)
    low = lane_iota((block, 128)) < 64
    half_lane = lax.rem(lane_iota((block, 128)), 64)
    pick_low = jnp.where(low & (half_lane < 2), 1.0, 0.0)
    pick_high = jnp.where(low | (half_lane >= 2), 0.0, 1.0)

    @pl.when(parity == 0)
    def _():
        dk_ref[...] = jnp.zeros(dk_ref.shape, dk_ref.dtype)
        dv_ref[...] = jnp.zeros(dv_ref.shape, dv_ref.dtype)

    acc[...] = acc_in[0, 0] if with_acc else jnp.zeros(acc.shape, f32)

    @pl.when(count > 0)
    def _():
        lane = lax.rem(lane_iota((2 * span, 128)), 64)

        def split(values):
            high = values.astype(bf16).astype(f32)
            rest = values - high
            return jnp.where(lane == 0, high, jnp.where(lane == 1, rest, 0.0)).astype(bf16)

        heads = stacked(do_ref)
        dots = group_sum(
            heads.astype(f32) * stacked(o_ref).astype(f32), group_matrix(64, 1.0)
        )
        do_wide[:, :128] = heads
        do_wide[:, 128:] = split(-dots)
        q_wide[:, :128] = stacked(q_ref)
        q_wide[:, 128:] = split(-stacked(log_ref))

        def step(index, masked):
            rows = pl.ds(pl.multiple_of(index * block, block), block)
            k0, k1 = placed_pair(k_ref[0, rows, :], parity, low)
            v0, v1 = placed_pair(v_ref[0, rows, :], parity, low)
            k_pair = jnp.concatenate([k0, k1], axis=0)
            k_turned = jnp.transpose(k_pair).astype(bf16)
            picks = jnp.concatenate([pick_low, pick_high], axis=0).astype(bf16)
            k_wide = jnp.concatenate([k_pair.astype(bf16), picks], axis=1)
            v_wide = jnp.concatenate(
                [jnp.concatenate([v0, v1], axis=0).astype(bf16), picks], axis=1
            )
            weights = jnp.exp2(mm(k_wide, q_wide[...], NT))
            if masked:
                shape = (2 * block, 2 * span)
                q_pos = info_ref[0] + lax.rem(lane_iota(shape), span)
                k_pos = base + index * block + lax.rem(
                    lax.broadcasted_iota(jnp.int32, shape, 0), block
                )
                ok = (k_pos <= q_pos) & (k_pos < info_ref[1 + seq])
                weights = jnp.where(ok, weights, 0.0)
            grads = (weights * mm(v_wide, do_wide[...], NT)).astype(bf16)
            both_v = mm(weights.astype(bf16), do_wide[:, :128])
            both_k = mm(grads, q_wide[:, :128]) * math.log(2.0)
            acc[...] += mm(k_turned, grads)

            def joined(pair):
                total = jnp.where(low, pair[:block] + pltpu.roll(pair[block:], 64, 1), 0.0)
                return jnp.where(parity == 0, total, pltpu.roll(total, 64, 1))

            dk_ref[0, rows, :] += joined(both_k).astype(dk_ref.dtype)
            dv_ref[0, rows, :] += joined(both_v).astype(dv_ref.dtype)

        @pl.loop(0, whole)
        def _(index):
            step(index, False)

        @pl.loop(whole, count)
        def _(index):
            step(index, True)

    if finish:
        turned = jnp.transpose(acc[...]) * 0.125
        dq_ref[0, :, :128] = turned[:span].astype(dq_ref.dtype)
        dq_ref[0, :, 128:] = turned[span:].astype(dq_ref.dtype)
    else:
        dq_ref[0, 0] = acc[...]


def attend_back(info, queries, grad_out, out, logs, chunk, acc=None, finish=True):
    seqs, span, width = queries.shape
    kv_heads = width // 256
    chunk_len = chunk.shape[1]
    q_spec = pl.BlockSpec((1, span, 256), lambda b, h, *_: (b, 0, h))
    acc_spec = pl.BlockSpec((1, 1, 128, 2 * span), lambda b, h, *_: (b, h, 0, 0))
    acc_shape = jax.ShapeDtypeStruct((seqs, kv_heads, 128, 2 * span), f32)
    block = min(256, chunk_len)
    key_spec = pl.BlockSpec((1, chunk_len, 128), lambda b, h, *_: (b, 0, h // 2))
    value_spec = pl.BlockSpec(
        (1, chunk_len, 128), lambda b, h, *_: (b, 0, kv_heads // 2 + h // 2)
    )
    args = [queries, grad_out, out, logs, chunk, chunk]
    in_specs = [q_spec] * 4 + [key_spec, value_spec]
    if acc is not None:
        args.append(acc)
        in_specs.append(acc_spec)
    grad_shape = jax.ShapeDtypeStruct((seqs, chunk_len, width // 4), bf16)
    if finish:
        dq_shape, dq_spec = jax.ShapeDtypeStruct(queries.shape, bf16), q_spec
    else:
        dq_shape, dq_spec = acc_shape, acc_spec
    return pl.pallas_call(
        functools.partial(attend_back_kernel, block, acc is not None, finish),
        grid_spec=pltpu.PrefetchScalarGridSpec(
            num_scalar_prefetch=1,
            grid=(seqs, kv_heads),
            in_specs=in_specs,
            out_specs=[key_spec, key_spec, dq_spec],
            scratch_shapes=[
                pltpu.VMEM((128, 2 * span), f32),
                pltpu.VMEM((2 * span, 256), bf16),
                pltpu.VMEM((2 * span, 256), bf16),
            ],
        ),
        out_shape=[grad_shape, grad_shape, dq_shape],
        compiler_params=params(2),
        cost_estimate=pl.CostEstimate(
            flops=10 * 4 * seqs * span * width * chunk_len,
            bytes_accessed=4 * seqs * (span * width * 4 + chunk_len * width),
            transcendentals=seqs * span * width // 64 * chunk_len,
        ),
    )(info, *args)


def unproject_kernel(
    head_dim,
    n_q,
    n_k,
    dq_ref,
    dk_ref,
    dv_ref,
    qraw_ref,
    kraw_ref,
    scale_ref,
    qg_ref,
    kg_ref,
    cos_ref,
    sa_ref,
    sb_ref,
    out_ref,
    gq_ref,
    gk_ref,
):
    @pl.when(pl.program_id(0) == 0)
    def _():
        gq_ref[...] = jnp.zeros(gq_ref.shape, f32)
        gk_ref[...] = jnp.zeros(gk_ref.shape, f32)

    scale = scale_ref[:, :1]
    mean_matrix = group_matrix(head_dim, 1.0 / head_dim)
    for slab in range(n_q + n_k):
        is_q = slab < n_q
        index = slab if is_q else slab - n_q
        lanes = slice(128 * index, 128 * index + 128)
        raw = (qraw_ref if is_q else kraw_ref)[:, lanes].astype(f32)
        grad = (dq_ref if is_q else dk_ref)[:, lanes].astype(f32)
        gain = (qg_ref if is_q else kg_ref)[...]
        inverse = lax.rsqrt(group_sum(raw * raw, mean_matrix) + norm_eps)
        unit = raw * inverse
        turned = turn_back(grad, cos_ref, sa_ref, sb_ref)
        gain_part = jnp.sum(turned * unit, axis=0, keepdims=True)
        if is_q:
            gq_ref[...] += jnp.broadcast_to(gain_part, gq_ref.shape)
        else:
            gk_ref[...] += jnp.broadcast_to(gain_part, gk_ref.shape)
        inner = turned * gain
        mean = group_sum(inner * unit, mean_matrix)
        out = inverse * (inner - unit * mean) * scale
        out_ref[:, 128 * slab : 128 * slab + 128] = out.astype(bf16)
    v_start = 128 * (n_q + n_k)
    out_ref[:, v_start:] = (dv_ref[...].astype(f32) * scale).astype(bf16)


def unproject(dq, dk, dv, qraw, kraw, scale, q_gain, k_gain, tables, head_dim):
    rows, q_width = dq.shape
    kv_width = dk.shape[1]
    span = tables[0].shape[0]
    row_block = lambda a: pl.BlockSpec((span, a.shape[1]), lambda i: (i, 0))
    fixed = lambda a: pl.BlockSpec(a.shape, lambda i: (0,) * a.ndim)
    total = q_width + 2 * kv_width
    gain_shape = jax.ShapeDtypeStruct((8, 128), f32)
    return pl.pallas_call(
        functools.partial(unproject_kernel, head_dim, q_width // 128, kv_width // 128),
        grid=(rows // span,),
        in_specs=[row_block(a) for a in (dq, dk, dv, qraw, kraw, scale)]
        + [fixed(a) for a in (q_gain, k_gain, *tables)],
        out_specs=[
            pl.BlockSpec((span, total), lambda i: (i, 0)),
            pl.BlockSpec((8, 128), lambda i: (0, 0)),
            pl.BlockSpec((8, 128), lambda i: (0, 0)),
        ],
        out_shape=[jax.ShapeDtypeStruct((rows, total), bf16), gain_shape, gain_shape],
        compiler_params=params(1),
        cost_estimate=pl.CostEstimate(
            flops=8 * 128 * rows * total,
            bytes_accessed=6 * rows * total,
            transcendentals=rows * total,
        ),
    )(dq, dk, dv, qraw, kraw, scale, q_gain, k_gain, *tables)


def shards(
    tokens, lengths, cotangent, w_qkv, w_out, w_gateup, w_down, norm_attn, norm_ffn, q_gain, k_gain
):
    seq_count, span_len, model_width = tokens.shape
    row_count = seq_count * span_len
    head_dim = q_gain.shape[0]
    half_dim = head_dim // 2
    query_width = w_out.shape[1]
    kv_width = (w_qkv.shape[1] - query_width) // 2
    hidden_width = w_down.shape[1]
    log2_scale = math.log2(math.e) * head_dim ** (-0.5)

    offset = lax.axis_index("seq") * span_len
    positions = offset + jnp.arange(span_len, dtype=jnp.int32)
    inverse = theta_base ** (-jnp.arange(half_dim, dtype=f32) * 2.0 / head_dim)
    angles = positions.astype(f32)[:, None] * inverse[None, :]
    cosine, sine = jnp.cos(angles), jnp.sin(angles)
    nothing = jnp.zeros_like(sine)
    tables = (
        jnp.concatenate([cosine] * 4, axis=1),
        jnp.concatenate([-sine, nothing] * 2, axis=1),
        jnp.concatenate([nothing, sine] * 2, axis=1),
    )
    q_gain_f = jnp.concatenate([q_gain.astype(f32)] * 2)[None, :]
    k_gain_f = jnp.concatenate([k_gain.astype(f32)] * 2)[None, :]

    attn_gain = norm_attn.astype(f32)[:, None]
    ffn_gain = norm_ffn.astype(f32)[:, None]
    qkv_shard = (w_qkv.astype(f32) * attn_gain).astype(bf16)
    gateup_shard = (w_gateup.astype(f32) * ffn_gain).astype(bf16)

    gather = lambda w: lax.all_gather(w, both, axis=0, tiled=True)
    qkv_full = gather(qkv_shard)
    q_full, kv_full = qkv_full[:, :query_width], qkv_full[:, query_width:]
    out_full = gather(w_out)
    gateup_full = gather(gateup_shard)
    down_full = gather(w_down)

    rows_in = tokens.reshape(row_count, model_width)
    kv, k_raw, scale1 = project(rows_in, kv_full, k_gain_f, tables, kv_width, head_dim)
    q, q_raw = project(
        rows_in, q_full, q_gain_f * log2_scale, tables, query_width, head_dim, scale1
    )
    q = q.reshape(seq_count, span_len, query_width)
    kv = kv.reshape(seq_count, span_len, 2 * kv_width)
    kv_all = lax.all_gather(kv, "seq", axis=1, tiled=True)
    info = jnp.concatenate(
        [offset[None].astype(jnp.int32), lengths, jnp.zeros((1,), jnp.int32)]
    )
    heads, logs = attend(info, q, [kv_all])
    attended = heads.reshape(row_count, query_width)

    inputs = rows_in.astype(f32)
    middle = inputs + mm(attended, out_full, NT)
    middle_low = middle.astype(bf16)
    scale2 = lax.rsqrt(jnp.mean(middle * middle, axis=-1, keepdims=True) + norm_eps)
    gate_up = mm(middle_low, gateup_full) * scale2
    gate, up = gate_up[:, :hidden_width], gate_up[:, hidden_width:]
    sig = jax.nn.sigmoid(gate)
    silu = gate * sig
    hidden = (silu * up).astype(bf16)
    output = (middle + mm(hidden, down_full, NT)).astype(bf16)

    valid = (positions[None, :] < lengths[:, None]).reshape(row_count, 1)
    cot = jnp.where(valid, cotangent.reshape(row_count, model_width), 0)
    grad_down = mm(cot, hidden, TN)
    grad_hidden = mm(cot, down_full)
    grad_gate = grad_hidden * up * (sig * (1.0 + gate * (1.0 - sig)))
    grad_up = grad_hidden * silu
    grad_gu = (jnp.concatenate([grad_gate, grad_up], axis=1) * scale2).astype(bf16)
    grad_gateup = mm(middle_low, grad_gu, TN)
    back2 = mm(grad_gu, gateup_full, NT)
    unit2 = middle * scale2
    grad_middle = (
        cot.astype(f32) + back2 - unit2 * jnp.mean(back2 * unit2, axis=-1, keepdims=True)
    )
    grad_branch = grad_middle.astype(bf16)
    grad_out = mm(grad_branch, attended, TN)
    grad_heads = mm(grad_branch, out_full).astype(bf16)
    grad_heads = grad_heads.reshape(seq_count, span_len, query_width)

    dk, dv, dq = attend_back(info, q, grad_heads, heads, logs, kv_all)
    dkv = lax.psum_scatter(
        jnp.concatenate([dk, dv], axis=-1), "seq", scatter_dimension=1, tiled=True
    )
    dkv = dkv.reshape(row_count, 2 * kv_width)
    grad_proj, gq, gk = unproject(
        dq.reshape(row_count, query_width),
        dkv[:, :kv_width],
        dkv[:, kv_width:],
        q_raw,
        k_raw,
        scale1,
        q_gain_f,
        k_gain_f,
        tables,
        head_dim,
    )
    grad_qkv = mm(rows_in, grad_proj, TN)
    back1 = mm(grad_proj, qkv_full, NT)
    unit1 = inputs * scale1[:, :1]
    grad_tokens = (
        grad_middle + back1 - unit1 * jnp.mean(back1 * unit1, axis=-1, keepdims=True)
    ).astype(bf16)

    scatter = lambda g: lax.psum_scatter(
        g.astype(bf16), both, scatter_dimension=0, tiled=True
    ).astype(f32)
    sum_down = scatter(grad_down)
    sum_gateup = scatter(grad_gateup)
    sum_out = scatter(grad_out)
    sum_qkv = scatter(grad_qkv)
    gains = lax.psum(jnp.concatenate([gq[:1], gk[:1]], axis=0), both)
    gains = gains[:, :head_dim] + gains[:, head_dim:]
    return (
        output.reshape(tokens.shape),
        grad_tokens.reshape(tokens.shape),
        sum_qkv * attn_gain,
        sum_out,
        sum_gateup * ffn_gain,
        sum_down,
        jnp.sum(sum_qkv * w_qkv.astype(f32), axis=1),
        jnp.sum(sum_gateup * w_gateup.astype(f32), axis=1),
        gains[0],
        gains[1],
    )


def solution(mesh):
    rows = P("row", "seq", None)
    weight = P(both, None)
    vector = P(both)
    return jax.shard_map(
        shards,
        mesh=mesh,
        in_specs=(rows, P("row"), rows, weight, weight, weight, weight, vector, vector, P(), P()),
        out_specs=(rows, rows, weight, weight, weight, weight, vector, vector, P(), P()),
        check_vma=False,
    )
```

```python
import functools
import math

import jax
import jax.numpy as jnp
from jax import lax
from jax.experimental import pallas as pl
from jax.experimental.pallas import tpu as pltpu
from jax.sharding import PartitionSpec as P

norm_eps = 1e-06
theta_base = 10000.0
both = ("row", "seq")
f32 = jnp.float32
bf16 = jnp.bfloat16
vmem_cap = 56 * 1024 * 1024
any_spec = pl.BlockSpec(memory_space=pl.ANY)
NN = (((1,), (0,)), ((), ()))
NT = (((1,), (1,)), ((), ()))
TN = (((0,), (0,)), ((), ()))


def mm(left, right, dims=NN):
    return lax.dot_general(left, right, dims, preferred_element_type=f32)


def params(n_grid):
    return pltpu.CompilerParams(
        dimension_semantics=("arbitrary",) * n_grid, vmem_limit_bytes=vmem_cap
    )


def lane_iota(shape):
    return lax.broadcasted_iota(jnp.int32, shape, len(shape) - 1)


def group_matrix(head_dim, value):
    i = lax.broadcasted_iota(jnp.int32, (128, 128), 0) // head_dim
    j = lax.broadcasted_iota(jnp.int32, (128, 128), 1) // head_dim
    return jnp.where(i == j, value, 0.0).astype(bf16)


def group_sum(values, matrix):
    high = values.astype(bf16)
    low = (values - high.astype(f32)).astype(bf16)
    return mm(high, matrix) + mm(low, matrix)


def turn(values, cos_ref, sa_ref, sb_ref):
    return (
        values * cos_ref[...]
        + pltpu.roll(values, 96, 1) * sa_ref[...]
        + pltpu.roll(values, 32, 1) * sb_ref[...]
    )


def turn_back(values, cos_ref, sa_ref, sb_ref):
    return (
        values * cos_ref[...]
        - pltpu.roll(values, 96, 1) * sa_ref[...]
        - pltpu.roll(values, 32, 1) * sb_ref[...]
    )


class Grid:
    def __init__(self, rows, seqs):
        self.rows, self.seqs, self.depth = rows, seqs, seqs // 2
        self.row = lax.axis_index("row")
        seq = lax.axis_index("seq")
        self.level, self.core = seq // 2, lax.rem(seq, 2)
        self.seq = seq
        bits = [1 << k for k in range(rows.bit_length() - 1)]
        self.orders = (bits, bits[::-1])
        self.place = jnp.stack([self.row, self.level, self.core]).astype(jnp.int32)

    def move(self, value, where):
        pairs = []
        for row in range(self.rows):
            for seq in range(self.seqs):
                target = where(row, seq)
                if target is not None:
                    pairs.append((row * self.seqs + seq, target[0] * self.seqs + target[1]))
        return lax.ppermute(value, both, pairs)

    def across(self, value, mask):
        return self.move(value, lambda r, s: (r ^ mask, s))

    def partner(self, value):
        return self.move(value, lambda r, s: (r, s ^ 1))

    def around(self, value):
        return self.move(value, lambda r, s: (r, (s + 2) % self.seqs))

    def up(self, value):
        return self.move(value, lambda r, s: (r, s + 2) if s + 2 < self.seqs else None)

    def down(self, value):
        return self.move(value, lambda r, s: (r, s - 2) if s >= 2 else None)

    def masks(self, half):
        found = [0]
        for bit in self.orders[half]:
            found = found + [m ^ bit for m in found]
        return found

    def gather(self, shard):
        steps = [shard]
        for _ in range(1, self.depth):
            steps.append(self.around(steps[-1]))
        middle = self.depth // 2
        mine = []
        for half, part in enumerate((steps[:middle], steps[middle:])):
            held = jnp.stack(part)[None]
            for bit in self.orders[half]:
                held = jnp.concatenate([held, self.across(held, bit)], axis=0)
            mine.append(held)
        return mine + [self.partner(held) for held in mine]

    def everywhere(self, value):
        for bit in self.orders[0]:
            value = value + self.across(value, bit)
        bit = 1
        while bit < self.seqs:
            value = value + self.move(value, lambda r, s, bit=bit: (r, s ^ bit))
            bit *= 2
        return value

    def scatter(self, mine, theirs):
        ends = []
        for half in range(2):
            parts = [mine[half].astype(f32), self.partner(theirs[half]).astype(f32)]
            for bit in reversed(self.orders[half]):
                count = parts[0].shape[0] // 2
                sent = sum(p[count:] for p in parts).astype(bf16)
                parts = [p[:count] for p in parts] + [self.across(sent, bit).astype(f32)]
            ends.append(sum(p[0] for p in parts))
        levels = jnp.concatenate(ends, axis=0)

        def at(step):
            index = lax.rem(self.level - step + 2 * self.depth, self.depth)
            return lax.dynamic_index_in_dim(levels, index, 0, keepdims=False)

        total = at(1)
        for step in range(2, self.depth + 1):
            total = self.around(total.astype(bf16)).astype(f32) + at(step)
        return total


def loads(grid, place_ref, pieces, target, sems, columns=None, at_column=0):
    row, level, core = place_ref[0], place_ref[1], place_ref[2]
    shard = pieces[0].shape[2]
    if columns is None:
        columns = (0, pieces[0].shape[3])
    width = columns[1] - columns[0]
    copies = []
    for which, ref in enumerate(pieces):
        half = which % 2
        whose = core if which < 2 else 1 - core
        first = 0 if half == 0 else grid.depth // 2
        for m, mask in enumerate(grid.masks(half)):
            for h in range(ref.shape[1]):
                at_level = lax.rem(level - (first + h) + grid.depth, grid.depth)
                start = ((row ^ mask) * grid.seqs + at_level * 2 + whose) * shard
                copies.append(
                    pltpu.make_async_copy(
                        ref.at[m, h, :, columns[0] : columns[1]],
                        target.at[
                            pl.ds(pl.multiple_of(start, shard), shard),
                            at_column : at_column + width,
                        ],
                        sems.at[len(copies)],
                    )
                )
    return copies


def n_loads(grid):
    return grid.rows * grid.seqs


def project_kernel(grid, normed_slabs, head_dim, with_scale, place_ref, tok_ref, *rest):
    pieces, rest = rest[:4], rest[4:]
    gain_ref, cos_ref, sa_ref, sb_ref, *rest = rest
    if with_scale:
        heads_ref, raw_ref, scale_ref, weight, sems = rest
    else:
        scale_in_ref, heads_ref, raw_ref, weight, sems = rest

    @pl.when(pl.program_id(0) == 0)
    def _():
        copies = loads(grid, place_ref, pieces, weight, sems)
        for copy in copies:
            copy.start()
        for copy in copies:
            copy.wait()

    if with_scale:
        x = tok_ref[...].astype(f32)
        scale = lax.rsqrt(jnp.mean(x * x, axis=-1, keepdims=True) + norm_eps)
        scale_ref[...] = jnp.broadcast_to(scale, scale_ref.shape)
    else:
        scale = scale_in_ref[:, :1]
    projected = mm(tok_ref[...], weight[...]) * scale
    mean_matrix = group_matrix(head_dim, 1.0 / head_dim)
    raw_ref[...] = projected[:, : raw_ref.shape[1]].astype(bf16)
    for slab in range(heads_ref.shape[1] // 128):
        lanes = slice(128 * slab, 128 * slab + 128)
        part = projected[:, lanes]
        if slab < normed_slabs:
            inverse = lax.rsqrt(group_sum(part * part, mean_matrix) + norm_eps)
            part = turn(part * inverse * gain_ref[...], cos_ref, sa_ref, sb_ref)
        heads_ref[:, lanes] = part.astype(bf16)


def project(grid, tokens, pieces, gain, tables, normed, head_dim, scale=None):
    rows, width = tokens.shape
    out_width = pieces[0].shape[3]
    span = tables[0].shape[0]
    row_block = lambda n: pl.BlockSpec((span, n), lambda i, *_: (i, 0))
    fixed = lambda a: pl.BlockSpec(a.shape, lambda i, *_: (0,) * a.ndim)
    args = [tokens, *pieces, gain, *tables]
    in_specs = [row_block(width)] + [any_spec] * 4 + [fixed(a) for a in (gain, *tables)]
    out_shape = [
        jax.ShapeDtypeStruct((rows, out_width), bf16),
        jax.ShapeDtypeStruct((rows, normed), bf16),
    ]
    out_specs = [row_block(out_width), row_block(normed)]
    if scale is None:
        out_shape.append(jax.ShapeDtypeStruct((rows, 128), f32))
        out_specs.append(row_block(128))
    else:
        args.append(scale)
        in_specs.append(row_block(128))
    return pl.pallas_call(
        functools.partial(project_kernel, grid, normed // 128, head_dim, scale is None),
        grid_spec=pltpu.PrefetchScalarGridSpec(
            num_scalar_prefetch=1,
            grid=(rows // span,),
            in_specs=in_specs,
            out_specs=out_specs,
            scratch_shapes=[
                pltpu.VMEM((width, out_width), bf16),
                pltpu.SemaphoreType.DMA((n_loads(grid),)),
            ],
        ),
        out_shape=out_shape,
        compiler_params=params(1),
        cost_estimate=pl.CostEstimate(
            flops=4 * rows * width * out_width,
            bytes_accessed=2 * (rows * (width + 2 * out_width) + width * out_width),
            transcendentals=rows * normed,
        ),
    )(grid.place, *args)


def placed_pair(slab, parity, low):
    values = slab.astype(f32)
    rolled = pltpu.roll(values, 64, 1)
    first = jnp.where(low, jnp.where(parity == 0, values, rolled), 0.0)
    second = jnp.where(low, 0.0, jnp.where(parity == 0, rolled, values))
    return first, second


def stacked(ref):
    return jnp.concatenate([ref[0, :, :128], ref[0, :, 128:]], axis=0)


def block_state(info_ref, seq, base, block, span):
    offset = info_ref[0]
    length = info_ref[1 + seq]
    some = (base >= 0) & (base < jnp.minimum(offset + span, length))
    whole = some & (base + block <= jnp.minimum(offset + 1, length))
    return whole, some & jnp.logical_not(whole)


def allowed(info_ref, seq, base, shape, key_axis, block, span):
    q_pos = info_ref[0] + lax.rem(
        lax.broadcasted_iota(jnp.int32, shape, 1 - key_axis), span
    )
    k_pos = base + lax.rem(lax.broadcasted_iota(jnp.int32, shape, key_axis), block)
    return (k_pos <= q_pos) & (k_pos < info_ref[1 + seq])


def attend_kernel(n_chunks, with_acc, finish, info_ref, q_ref, *refs):
    keys, refs = refs[:n_chunks], refs[n_chunks:]
    values, refs = refs[:n_chunks], refs[n_chunks:]
    if with_acc:
        acc_in, refs = refs[0], refs[1:]
    if finish:
        out_ref, log_ref, acc = refs
    else:
        (acc,) = refs
        acc = acc.at[0, 0]
    seq = pl.program_id(0)
    parity = lax.rem(pl.program_id(1), 2)
    span = q_ref.shape[1]
    block = keys[0].shape[1]
    acc[...] = acc_in[0, 0] if with_acc else jnp.zeros(acc.shape, f32)

    for chunk in range(n_chunks):
        base = info_ref[1 + pl.num_programs(0) + chunk]
        whole, partly = block_state(info_ref, seq, base, block, span)

        def step(masked, chunk=chunk, base=base):
            low = lane_iota((block, 128)) < 64
            ones_low = jnp.where(low, 1.0, 0.0).astype(bf16)
            ones_high = jnp.where(low, 0.0, 1.0).astype(bf16)
            k0, k1 = placed_pair(keys[chunk][0], parity, low)
            v0, v1 = placed_pair(values[chunk][0], parity, low)
            k_pair = jnp.concatenate([k0, k1], axis=0).astype(bf16)
            v_pair = jnp.concatenate(
                [
                    jnp.concatenate([v0.astype(bf16), ones_low], axis=1),
                    jnp.concatenate([v1.astype(bf16), ones_high], axis=1),
                ],
                axis=0,
            )
            weights = jnp.exp2(mm(stacked(q_ref), k_pair, NT))
            if masked:
                ok = allowed(info_ref, seq, base, weights.shape, 1, block, span)
                weights = jnp.where(ok, weights, 0.0)
            acc[...] += mm(weights.astype(bf16), v_pair)

        @pl.when(whole)
        def _():
            step(False)

        @pl.when(partly)
        def _():
            step(True)

    if finish:
        totals = acc[:, 128:]
        heads = (acc[:, :128] / totals).astype(bf16)
        logs = jnp.log2(totals)
        out_ref[0, :, :128] = heads[:span]
        out_ref[0, :, 128:] = heads[span:]
        log_ref[0, :, :128] = logs[:span]
        log_ref[0, :, 128:] = logs[span:]


def attend(info, bases, queries, chunks, acc=None, finish=True):
    seqs, span, width = queries.shape
    kv_heads = width // 256
    block = chunks[0].shape[1]
    q_spec = pl.BlockSpec((1, span, 256), lambda b, h, *_: (b, 0, h))
    acc_spec = pl.BlockSpec((1, 1, 2 * span, 256), lambda b, h, *_: (b, h, 0, 0))
    acc_shape = jax.ShapeDtypeStruct((seqs, kv_heads, 2 * span, 256), f32)
    key_spec = pl.BlockSpec((1, block, 128), lambda b, h, *_: (b, 0, h // 2))
    value_spec = pl.BlockSpec((1, block, 128), lambda b, h, *_: (b, 0, kv_heads // 2 + h // 2))
    args = [queries, *chunks, *chunks]
    in_specs = [q_spec] + [key_spec] * len(chunks) + [value_spec] * len(chunks)
    if acc is not None:
        args.append(acc)
        in_specs.append(acc_spec)
    if finish:
        out_shape = [
            jax.ShapeDtypeStruct(queries.shape, bf16),
            jax.ShapeDtypeStruct(queries.shape, f32),
        ]
        out_specs = [q_spec, q_spec]
        scratch = [pltpu.VMEM((2 * span, 256), f32)]
    else:
        out_shape, out_specs, scratch = acc_shape, acc_spec, []
    keys = block * len(chunks)
    return pl.pallas_call(
        functools.partial(attend_kernel, len(chunks), acc is not None, finish),
        grid_spec=pltpu.PrefetchScalarGridSpec(
            num_scalar_prefetch=1,
            grid=(seqs, kv_heads),
            in_specs=in_specs,
            out_specs=out_specs,
            scratch_shapes=scratch,
        ),
        out_shape=out_shape,
        compiler_params=params(2),
        cost_estimate=pl.CostEstimate(
            flops=4 * 4 * seqs * span * width * keys,
            bytes_accessed=4 * seqs * (span * width * 3 + keys * width // 2),
            transcendentals=seqs * span * width // 64 * keys,
        ),
    )(jnp.concatenate([info, bases]), *args)


def attend_back_kernel(n_chunks, with_acc, finish, info_ref, q_ref, do_ref, o_ref, log_ref, *refs):
    keys, refs = refs[:n_chunks], refs[n_chunks:]
    values, refs = refs[:n_chunks], refs[n_chunks:]
    if with_acc:
        acc_in, refs = refs[0], refs[1:]
    grads_out, refs = refs[:n_chunks], refs[n_chunks:]
    dq_ref, acc, q_wide, do_wide = refs
    seq, head = pl.program_id(0), pl.program_id(1)
    n_heads = pl.num_programs(1)
    parity = lax.rem(head, 2)
    span = q_ref.shape[1]
    block = keys[0].shape[1]
    alive = info_ref[0] < info_ref[1 + seq]

    @pl.when(head == 0)
    def _():
        for ref in grads_out:
            ref[...] = jnp.zeros(ref.shape, ref.dtype)

    acc[...] = acc_in[0, 0] if with_acc else jnp.zeros(acc.shape, f32)

    @pl.when(alive)
    def _():
        lane = lax.rem(lane_iota((2 * span, 128)), 64)

        def split(values):
            high = values.astype(bf16).astype(f32)
            rest = values - high
            return jnp.where(lane == 0, high, jnp.where(lane == 1, rest, 0.0)).astype(bf16)

        heads = stacked(do_ref)
        dots = group_sum(heads.astype(f32) * stacked(o_ref).astype(f32), group_matrix(64, 1.0))
        do_wide[:, :128] = heads
        do_wide[:, 128:] = split(-dots)
        q_wide[:, :128] = stacked(q_ref)
        q_wide[:, 128:] = split(-stacked(log_ref))

    for chunk in range(n_chunks):
        base = info_ref[1 + pl.num_programs(0) + chunk]
        whole, partly = block_state(info_ref, seq, base, block, span)

        def step(masked, chunk=chunk, base=base):
            low = lane_iota((block, 128)) < 64
            half_lane = lax.rem(lane_iota((block, 128)), 64)
            pick_low = jnp.where(low & (half_lane < 2), 1.0, 0.0)
            pick_high = jnp.where(low | (half_lane >= 2), 0.0, 1.0)
            picks = jnp.concatenate([pick_low, pick_high], axis=0).astype(bf16)
            k0, k1 = placed_pair(keys[chunk][0], parity, low)
            v0, v1 = placed_pair(values[chunk][0], parity, low)
            k_pair = jnp.concatenate([k0, k1], axis=0)
            k_turned = jnp.transpose(k_pair).astype(bf16)
            k_wide = jnp.concatenate([k_pair.astype(bf16), picks], axis=1)
            v_wide = jnp.concatenate(
                [jnp.concatenate([v0, v1], axis=0).astype(bf16), picks], axis=1
            )
            weights = jnp.exp2(mm(k_wide, q_wide[...], NT))
            if masked:
                ok = allowed(info_ref, seq, base, weights.shape, 0, block, span)
                weights = jnp.where(ok, weights, 0.0)
            grads = (weights * mm(v_wide, do_wide[...], NT)).astype(bf16)
            both_v = mm(weights.astype(bf16), do_wide[:, :128])
            both_k = mm(grads, q_wide[:, :128]) * math.log(2.0)
            acc[...] += mm(k_turned, grads)

            def joined(pair):
                total = jnp.where(low, pair[:block] + pltpu.roll(pair[block:], 64, 1), 0.0)
                return jnp.where(parity == 0, total, pltpu.roll(total, 64, 1))

            lanes = pl.multiple_of(head // 2 * 128, 128)
            more = pl.multiple_of((n_heads + head) // 2 * 128, 128)
            out = grads_out[chunk]
            out[0, :, pl.ds(lanes, 128)] += joined(both_k).astype(out.dtype)
            out[0, :, pl.ds(more, 128)] += joined(both_v).astype(out.dtype)

        @pl.when(whole & alive)
        def _():
            step(False)

        @pl.when(partly & alive)
        def _():
            step(True)

    if finish:
        turned = jnp.transpose(acc[...]) * 0.125
        dq_ref[0, :, :128] = turned[:span].astype(dq_ref.dtype)
        dq_ref[0, :, 128:] = turned[span:].astype(dq_ref.dtype)
    else:
        dq_ref[0, 0] = acc[...]


def attend_back(info, bases, queries, grad_out, out, logs, chunks, acc=None, finish=True):
    seqs, span, width = queries.shape
    kv_heads = width // 256
    block = chunks[0].shape[1]
    n = len(chunks)
    q_spec = pl.BlockSpec((1, span, 256), lambda b, h, *_: (b, 0, h))
    acc_spec = pl.BlockSpec((1, 1, 128, 2 * span), lambda b, h, *_: (b, h, 0, 0))
    acc_shape = jax.ShapeDtypeStruct((seqs, kv_heads, 128, 2 * span), f32)
    key_spec = pl.BlockSpec((1, block, 128), lambda b, h, *_: (b, 0, h // 2))
    value_spec = pl.BlockSpec((1, block, 128), lambda b, h, *_: (b, 0, kv_heads // 2 + h // 2))
    grad_spec = pl.BlockSpec((1, block, width // 2), lambda b, h, *_: (b, 0, 0))
    args = [queries, grad_out, out, logs, *chunks, *chunks]
    in_specs = [q_spec] * 4 + [key_spec] * n + [value_spec] * n
    if acc is not None:
        args.append(acc)
        in_specs.append(acc_spec)
    grad_shape = jax.ShapeDtypeStruct((seqs, block, width // 2), bf16)
    if finish:
        dq_shape, dq_spec = jax.ShapeDtypeStruct(queries.shape, bf16), q_spec
    else:
        dq_shape, dq_spec = acc_shape, acc_spec
    return pl.pallas_call(
        functools.partial(attend_back_kernel, n, acc is not None, finish),
        grid_spec=pltpu.PrefetchScalarGridSpec(
            num_scalar_prefetch=1,
            grid=(seqs, kv_heads),
            in_specs=in_specs,
            out_specs=[grad_spec] * n + [dq_spec],
            scratch_shapes=[
                pltpu.VMEM((128, 2 * span), f32),
                pltpu.VMEM((2 * span, 256), bf16),
                pltpu.VMEM((2 * span, 256), bf16),
            ],
        ),
        out_shape=[grad_shape] * n + [dq_shape],
        compiler_params=params(2),
        cost_estimate=pl.CostEstimate(
            flops=10 * 4 * seqs * span * width * block * n,
            bytes_accessed=4 * seqs * (span * width * 4 + block * n * width),
            transcendentals=seqs * span * width // 64 * block * n,
        ),
    )(jnp.concatenate([info, bases]), *args)


def unproject_kernel(
    head_dim,
    n_q,
    n_k,
    dq_ref,
    dk_ref,
    dv_ref,
    qraw_ref,
    kraw_ref,
    scale_ref,
    qg_ref,
    kg_ref,
    cos_ref,
    sa_ref,
    sb_ref,
    out_ref,
    gq_ref,
    gk_ref,
):
    @pl.when(pl.program_id(0) == 0)
    def _():
        gq_ref[...] = jnp.zeros(gq_ref.shape, f32)
        gk_ref[...] = jnp.zeros(gk_ref.shape, f32)

    scale = scale_ref[:, :1]
    mean_matrix = group_matrix(head_dim, 1.0 / head_dim)
    for slab in range(n_q + n_k):
        is_q = slab < n_q
        index = slab if is_q else slab - n_q
        lanes = slice(128 * index, 128 * index + 128)
        raw = (qraw_ref if is_q else kraw_ref)[:, lanes].astype(f32)
        grad = (dq_ref if is_q else dk_ref)[:, lanes].astype(f32)
        gain = (qg_ref if is_q else kg_ref)[...]
        inverse = lax.rsqrt(group_sum(raw * raw, mean_matrix) + norm_eps)
        unit = raw * inverse
        turned = turn_back(grad, cos_ref, sa_ref, sb_ref)
        gain_part = jnp.sum(turned * unit, axis=0, keepdims=True)
        if is_q:
            gq_ref[...] += jnp.broadcast_to(gain_part, gq_ref.shape)
        else:
            gk_ref[...] += jnp.broadcast_to(gain_part, gk_ref.shape)
        inner = turned * gain
        mean = group_sum(inner * unit, mean_matrix)
        out = inverse * (inner - unit * mean) * scale
        out_ref[:, 128 * slab : 128 * slab + 128] = out.astype(bf16)
    v_start = 128 * (n_q + n_k)
    out_ref[:, v_start:] = (dv_ref[...].astype(f32) * scale).astype(bf16)


def unproject(dq, dk, dv, qraw, kraw, scale, q_gain, k_gain, tables, head_dim):
    rows, q_width = dq.shape
    kv_width = dk.shape[1]
    span = tables[0].shape[0]
    row_block = lambda a: pl.BlockSpec((span, a.shape[1]), lambda i: (i, 0))
    fixed = lambda a: pl.BlockSpec(a.shape, lambda i: (0,) * a.ndim)
    total = q_width + 2 * kv_width
    gain_shape = jax.ShapeDtypeStruct((8, 128), f32)
    return pl.pallas_call(
        functools.partial(unproject_kernel, head_dim, q_width // 128, kv_width // 128),
        grid=(rows // span,),
        in_specs=[row_block(a) for a in (dq, dk, dv, qraw, kraw, scale)]
        + [fixed(a) for a in (q_gain, k_gain, *tables)],
        out_specs=[
            pl.BlockSpec((span, total), lambda i: (i, 0)),
            pl.BlockSpec((8, 128), lambda i: (0, 0)),
            pl.BlockSpec((8, 128), lambda i: (0, 0)),
        ],
        out_shape=[jax.ShapeDtypeStruct((rows, total), bf16), gain_shape, gain_shape],
        compiler_params=params(1),
        cost_estimate=pl.CostEstimate(
            flops=8 * 128 * rows * total,
            bytes_accessed=6 * rows * total,
            transcendentals=rows * total,
        ),
    )(dq, dk, dv, qraw, kraw, scale, q_gain, k_gain, *tables)


def feed_kernel(
    grid,
    span,
    split,
    info_ref,
    place_ref,
    tok_ref,
    heads_ref,
    cot_ref,
    *rest,
):
    pieces, rest = rest[:4], rest[4:]
    out_ref, hidden_ref, mid_ref, dgu_ref, dmid_ref, dheads_ref, *rest = rest
    w_out, w_gu, w_down, out_sems, gu_sems, down_sems = rest
    a, b = split

    @pl.when(pl.program_id(0) == 0)
    def _():
        copies = (
            loads(grid, place_ref, pieces, w_out, out_sems, (0, a))
            + loads(grid, place_ref, pieces, w_down, down_sems, (a, 2 * a))
            + loads(grid, place_ref, pieces, w_gu, gu_sems, (2 * a, 2 * a + b))
        )
        for copy in copies:
            copy.start()
        for copy in copies:
            copy.wait()

    rows = tok_ref.shape[0]
    middle = tok_ref[...].astype(f32) + mm(heads_ref[...], w_out[...], NT)
    middle_low = middle.astype(bf16)
    mid_ref[...] = middle_low
    scale = lax.rsqrt(jnp.mean(middle * middle, axis=-1, keepdims=True) + norm_eps)
    gate_up = mm(middle_low, w_gu[...]) * scale
    half = gate_up.shape[1] // 2
    gate, up = gate_up[:, :half], gate_up[:, half:]
    sig = 1.0 / (1.0 + jnp.exp(-gate))
    silu = gate * sig
    hidden = silu * up
    hidden_low = hidden.astype(bf16)
    out_ref[...] = (middle + mm(hidden_low, w_down[...], NT)).astype(bf16)

    first = pl.program_id(0) * (rows // span)
    count = rows // span
    longest = info_ref[1 + first]
    for k in range(1, count):
        longest = jnp.maximum(longest, info_ref[1 + first + k])
    alive = info_ref[0] < longest

    @pl.when(alive)
    def _():
        position = lax.broadcasted_iota(jnp.int32, (span, 1), 0) + info_ref[0]
        valid = jnp.concatenate(
            [(position < info_ref[1 + first + k]).astype(f32) for k in range(count)], axis=0
        )
        hidden_ref[...] = (hidden * valid).astype(bf16)
        cot = cot_ref[...].astype(f32) * valid
        grad_hidden = mm(cot.astype(bf16), w_down[...])
        grad_gate = grad_hidden * up * (sig * (1.0 + gate * (1.0 - sig))) * scale
        grad_up = grad_hidden * silu * scale
        grad_gu = jnp.concatenate([grad_gate.astype(bf16), grad_up.astype(bf16)], axis=1)
        dgu_ref[...] = grad_gu
        back = mm(grad_gu, w_gu[...], NT)
        unit = middle * scale
        grad_mid = cot + back - unit * jnp.mean(back * unit, axis=-1, keepdims=True)
        grad_mid = grad_mid.astype(bf16)
        dmid_ref[...] = grad_mid
        dheads_ref[...] = mm(grad_mid, w_out[...]).astype(bf16)

    @pl.when(jnp.logical_not(alive))
    def _():
        for ref in (hidden_ref, dgu_ref, dmid_ref, dheads_ref):
            ref[...] = jnp.zeros(ref.shape, ref.dtype)


def feed(grid, info, tokens, heads, cotangent, pieces, split, span):
    rows, width = tokens.shape
    a, b = split
    tile = max(span, min(256, rows))
    block = lambda n: pl.BlockSpec((tile, n), lambda i, *_: (i, 0))
    shape = lambda n: jax.ShapeDtypeStruct((rows, n), bf16)
    n = n_loads(grid)
    outs = (width, a, width, b, width, a)
    macs = width * (2 * a + b)
    return pl.pallas_call(
        functools.partial(feed_kernel, grid, span, split),
        grid_spec=pltpu.PrefetchScalarGridSpec(
            num_scalar_prefetch=2,
            grid=(rows // tile,),
            in_specs=[block(width), block(a), block(width)] + [any_spec] * 4,
            out_specs=[block(n) for n in outs],
            scratch_shapes=[
                pltpu.VMEM((width, a), bf16),
                pltpu.VMEM((width, b), bf16),
                pltpu.VMEM((width, a), bf16),
                pltpu.SemaphoreType.DMA((n,)),
                pltpu.SemaphoreType.DMA((n,)),
                pltpu.SemaphoreType.DMA((n,)),
            ],
        ),
        out_shape=[shape(n) for n in outs],
        compiler_params=params(1),
        cost_estimate=pl.CostEstimate(
            flops=6 * rows * macs,
            bytes_accessed=2 * (rows * (sum(outs) + 2 * width + a) + macs),
            transcendentals=rows * a,
        ),
    )(info, grid.place, tokens, heads, cotangent, *pieces)


def last_kernel(grid, span, info_ref, place_ref, tok_ref, dproj_ref, dmid_ref, scale_ref, *rest):
    q_pieces, kv_pieces, rest = rest[:4], rest[4:8], rest[8:]
    out_ref, weight, q_sems, kv_sems = rest
    q_width = q_pieces[0].shape[3]

    @pl.when(pl.program_id(0) == 0)
    def _():
        copies = loads(grid, place_ref, q_pieces, weight, q_sems)
        copies += loads(grid, place_ref, kv_pieces, weight, kv_sems, None, q_width)
        for copy in copies:
            copy.start()
        for copy in copies:
            copy.wait()

    back = mm(dproj_ref[...], weight[...], NT)
    unit = tok_ref[...].astype(f32) * scale_ref[:, :1]
    grad = dmid_ref[...].astype(f32) + back
    grad = grad - unit * jnp.mean(back * unit, axis=-1, keepdims=True)
    out_ref[...] = grad.astype(bf16)


def last(grid, info, tokens, grad_proj, grad_mid, scale, q_pieces, kv_pieces, span):
    rows, width = tokens.shape
    tile = max(span, min(256, rows))
    block = lambda a: pl.BlockSpec((tile, a.shape[1]), lambda i, *_: (i, 0))
    total = grad_proj.shape[1]
    return pl.pallas_call(
        functools.partial(last_kernel, grid, span),
        grid_spec=pltpu.PrefetchScalarGridSpec(
            num_scalar_prefetch=2,
            grid=(rows // tile,),
            in_specs=[block(a) for a in (tokens, grad_proj, grad_mid, scale)] + [any_spec] * 8,
            out_specs=block(tokens),
            scratch_shapes=[
                pltpu.VMEM((width, total), bf16),
                pltpu.SemaphoreType.DMA((n_loads(grid),)),
                pltpu.SemaphoreType.DMA((n_loads(grid),)),
            ],
        ),
        out_shape=jax.ShapeDtypeStruct(tokens.shape, bf16),
        compiler_params=params(1),
        cost_estimate=pl.CostEstimate(
            flops=4 * rows * width * total,
            bytes_accessed=2 * (rows * (3 * width + total) + width * total),
            transcendentals=0,
        ),
    )(info, grid.place, tokens, grad_proj, grad_mid, scale, *q_pieces, *kv_pieces)


def weight_kernel(grid, shard, place_ref, left_ref, right_ref, *rest):
    *outs, acc = rest
    acc[...] = mm(left_ref[...], right_ref[...], TN)
    core = place_ref[2]
    middle = grid.depth // 2
    for level in range(grid.depth):
        half, at = level // middle, level % middle
        for whose, ref in ((core, outs[half]), (1 - core, outs[2 + half])):
            start = pl.multiple_of((level * 2 + whose) * shard, shard)
            ref[0, at] = acc[pl.ds(start, shard), :].astype(bf16)


def weight_grad(grid, left, right):
    rows, features = left.shape
    width = right.shape[1]
    part = features // grid.rows
    shard = part // grid.seqs
    masks = grid.masks(0)
    other = grid.masks(1)
    where = [other.index(m) for m in masks]
    shape = jax.ShapeDtypeStruct((grid.rows, grid.depth // 2, shard, width), bf16)
    piece = (1, grid.depth // 2, shard, width)

    def second(i, *_):
        at = 0
        for k, w in enumerate(where):
            at = jnp.where(i == k, w, at)
        return (at, 0, 0, 0)

    first = lambda i, *_: (i, 0, 0, 0)
    outs = pl.pallas_call(
        functools.partial(weight_kernel, grid, shard),
        grid_spec=pltpu.PrefetchScalarGridSpec(
            num_scalar_prefetch=1,
            grid=(grid.rows,),
            in_specs=[
                pl.BlockSpec((rows, part), lambda i, place: (0, place[0] ^ i)),
                pl.BlockSpec((rows, width), lambda i, place: (0, 0)),
            ],
            out_specs=[pl.BlockSpec(piece, first), pl.BlockSpec(piece, second)] * 2,
            scratch_shapes=[pltpu.VMEM((part, width), f32)],
        ),
        out_shape=[shape] * 4,
        compiler_params=params(1),
        cost_estimate=pl.CostEstimate(
            flops=4 * rows * features * width,
            bytes_accessed=2 * (rows * (features + width) + features * width),
            transcendentals=0,
        ),
    )(grid.place, left, right)
    return outs[:2], outs[2:]


def shards(
    n_rows,
    n_seqs,
    tokens,
    lengths,
    cotangent,
    w_qkv,
    w_out,
    w_gateup,
    w_down,
    norm_attn,
    norm_ffn,
    q_gain,
    k_gain,
):
    grid = Grid(n_rows, n_seqs)
    seq_count, span_len, model_width = tokens.shape
    row_count = seq_count * span_len
    head_dim = q_gain.shape[0]
    half_dim = head_dim // 2
    query_width = w_out.shape[1]
    kv_width = (w_qkv.shape[1] - query_width) // 2
    log2_scale = math.log2(math.e) * head_dim ** (-0.5)

    offset = (grid.seq * span_len).astype(jnp.int32)
    positions = offset + jnp.arange(span_len, dtype=jnp.int32)
    inverse = theta_base ** (-jnp.arange(half_dim, dtype=f32) * 2.0 / head_dim)
    angles = positions.astype(f32)[:, None] * inverse[None, :]
    cosine, sine = jnp.cos(angles), jnp.sin(angles)
    nothing = jnp.zeros_like(sine)
    tables = (
        jnp.concatenate([cosine] * 4, axis=1),
        jnp.concatenate([-sine, nothing] * 2, axis=1),
        jnp.concatenate([nothing, sine] * 2, axis=1),
    )
    q_gain_f = jnp.concatenate([q_gain.astype(f32)] * 2)[None, :]
    k_gain_f = jnp.concatenate([k_gain.astype(f32)] * 2)[None, :]
    info = jnp.concatenate([offset[None], lengths])

    attn_gain = norm_attn.astype(f32)[:, None]
    ffn_gain = norm_ffn.astype(f32)[:, None]
    qkv_shard = (w_qkv.astype(f32) * attn_gain).astype(bf16)
    gateup_shard = (w_gateup.astype(f32) * ffn_gain).astype(bf16)

    kv_pieces = grid.gather(qkv_shard[:, query_width:])
    q_pieces = grid.gather(qkv_shard[:, :query_width])
    feed_pieces = grid.gather(jnp.concatenate([w_out, w_down, gateup_shard], axis=1))

    rows_in = tokens.reshape(row_count, model_width)
    kv, k_raw, scale1 = project(grid, rows_in, kv_pieces, k_gain_f, tables, kv_width, head_dim)
    q, q_raw = project(
        grid, rows_in, q_pieces, q_gain_f * log2_scale, tables, query_width, head_dim, scale1
    )
    q = q.reshape(seq_count, span_len, query_width)
    kv = kv.reshape(seq_count, span_len, 2 * kv_width)

    reach = [kv]
    for _ in range(1, grid.depth):
        reach.append(grid.up(reach[-1]))
    chunks, bases = [], []
    for step, own in enumerate(reach):
        chunks.append((own, grid.partner(own)))
        level = grid.level - step
        start = jnp.stack([level * 2 + grid.core, level * 2 + 1 - grid.core]) * span_len
        bases.append(jnp.where(level >= 0, start, -1).astype(jnp.int32))
    near = [c for pair in chunks[:-1] for c in pair]
    near_bases = jnp.concatenate(bases[:-1])
    acc = attend(info, near_bases, q, near, None, False)
    heads, logs = attend(info, bases[-1], q, list(chunks[-1]), acc, True)
    attended = heads.reshape(row_count, query_width)

    output, hidden, middle, grad_gu, grad_mid, grad_heads = feed(
        grid,
        info,
        rows_in,
        attended,
        cotangent.reshape(row_count, model_width),
        feed_pieces,
        (query_width, w_gateup.shape[1]),
        span_len,
    )
    grad_heads = grad_heads.reshape(seq_count, span_len, query_width)

    *far_grads, acc_q = attend_back(
        info, bases[-1], q, grad_heads, heads, logs, list(chunks[-1]), None, False
    )
    sum_down = grid.scatter(*weight_grad(grid, cotangent.reshape(row_count, model_width), hidden))
    *near_grads, grad_q = attend_back(
        info, near_bases, q, grad_heads, heads, logs, near, acc_q, True
    )
    sum_gateup = grid.scatter(*weight_grad(grid, middle, grad_gu))
    sum_out = grid.scatter(*weight_grad(grid, grad_mid, attended))

    pairs = [near_grads[2 * k : 2 * k + 2] for k in range(grid.depth - 1)] + [far_grads]
    grad_kv = None
    for own, other in reversed(pairs):
        here = own.astype(f32) + grid.partner(other).astype(f32)
        grad_kv = here if grad_kv is None else here + grid.down(grad_kv.astype(bf16)).astype(f32)
    grad_kv = grad_kv.astype(bf16).reshape(row_count, 2 * kv_width)

    grad_proj, gq, gk = unproject(
        grad_q.reshape(row_count, query_width),
        grad_kv[:, :kv_width],
        grad_kv[:, kv_width:],
        q_raw,
        k_raw,
        scale1,
        q_gain_f,
        k_gain_f,
        tables,
        head_dim,
    )
    sum_qkv = grid.scatter(*weight_grad(grid, rows_in, grad_proj))
    grad_tokens = last(
        grid, info, rows_in, grad_proj, grad_mid, scale1, q_pieces, kv_pieces, span_len
    )
    gains = grid.everywhere(jnp.concatenate([gq[:1], gk[:1]], axis=0))
    gains = gains[:, :head_dim] + gains[:, head_dim:]
    return (
        output.reshape(tokens.shape),
        grad_tokens.reshape(tokens.shape),
        sum_qkv * attn_gain,
        sum_out,
        sum_gateup * ffn_gain,
        sum_down,
        jnp.sum(sum_qkv * w_qkv.astype(f32), axis=1),
        jnp.sum(sum_gateup * w_gateup.astype(f32), axis=1),
        gains[0],
        gains[1],
    )


def solution(mesh):
    rows = P("row", "seq", None)
    weight = P(both, None)
    vector = P(both)
    return jax.shard_map(
        functools.partial(shards, mesh.shape["row"], mesh.shape["seq"]),
        mesh=mesh,
        in_specs=(rows, P("row"), rows, weight, weight, weight, weight, vector, vector, P(), P()),
        out_specs=(rows, rows, weight, weight, weight, weight, vector, vector, P(), P()),
        check_vma=False,
    )
```

```python
import functools
import math

import jax
import jax.numpy as jnp
from jax import lax
from jax.experimental import pallas as pl
from jax.experimental.pallas import tpu as pltpu
from jax.sharding import PartitionSpec as P

norm_eps = 1e-06
theta_base = 10000.0
both = ("row", "seq")
f32 = jnp.float32
bf16 = jnp.bfloat16
vmem_cap = 56 * 1024 * 1024
any_spec = pl.BlockSpec(memory_space=pl.ANY)
NN = (((1,), (0,)), ((), ()))
NT = (((1,), (1,)), ((), ()))
TN = (((0,), (0,)), ((), ()))


def mm(left, right, dims=NN):
    return lax.dot_general(left, right, dims, preferred_element_type=f32)


def after(value, *earlier):
    return lax.optimization_barrier((value, *earlier))[0]


def params(n_grid):
    return pltpu.CompilerParams(
        dimension_semantics=("arbitrary",) * n_grid, vmem_limit_bytes=vmem_cap
    )


def lane_iota(shape):
    return lax.broadcasted_iota(jnp.int32, shape, len(shape) - 1)


def group_matrix(head_dim, value):
    i = lax.broadcasted_iota(jnp.int32, (128, 128), 0) // head_dim
    j = lax.broadcasted_iota(jnp.int32, (128, 128), 1) // head_dim
    return jnp.where(i == j, value, 0.0).astype(bf16)


def group_sum(values, matrix):
    high = values.astype(bf16)
    low = (values - high.astype(f32)).astype(bf16)
    return mm(high, matrix) + mm(low, matrix)


def turn(values, cos_ref, sa_ref, sb_ref):
    return (
        values * cos_ref[...]
        + pltpu.roll(values, 96, 1) * sa_ref[...]
        + pltpu.roll(values, 32, 1) * sb_ref[...]
    )


def turn_back(values, cos_ref, sa_ref, sb_ref):
    return (
        values * cos_ref[...]
        - pltpu.roll(values, 96, 1) * sa_ref[...]
        - pltpu.roll(values, 32, 1) * sb_ref[...]
    )


class Grid:
    def __init__(self, rows, seqs):
        self.rows, self.seqs, self.depth = rows, seqs, seqs // 2
        self.row = lax.axis_index("row")
        seq = lax.axis_index("seq")
        self.level, self.core = seq // 2, lax.rem(seq, 2)
        self.seq = seq
        bits = [1 << k for k in range(rows.bit_length() - 1)]
        self.orders = (bits, bits[::-1])
        self.place = jnp.stack([self.row, self.level, self.core]).astype(jnp.int32)

    def move(self, value, where):
        pairs = []
        for row in range(self.rows):
            for seq in range(self.seqs):
                target = where(row, seq)
                if target is not None:
                    pairs.append((row * self.seqs + seq, target[0] * self.seqs + target[1]))
        return lax.ppermute(value, both, pairs)

    def across(self, value, mask):
        return self.move(value, lambda r, s: (r ^ mask, s))

    def partner(self, value):
        return self.move(value, lambda r, s: (r, s ^ 1))

    def around(self, value):
        return self.move(value, lambda r, s: (r, (s + 2) % self.seqs))

    def up(self, value):
        return self.move(value, lambda r, s: (r, s + 2) if s + 2 < self.seqs else None)

    def down(self, value):
        return self.move(value, lambda r, s: (r, s - 2) if s >= 2 else None)

    def masks(self, half):
        found = [0]
        for bit in self.orders[half]:
            found = found + [m ^ bit for m in found]
        return found

    def ring(self, shard, waits=()):
        steps = [shard]
        for hop in range(self.depth - 1):
            held = steps[-1]
            if hop < len(waits):
                held = after(held, *waits[hop])
            steps.append(self.around(held))
        return steps

    def spread(self, steps, waits=()):
        middle = self.depth // 2
        held = [jnp.stack(steps[:middle])[None], jnp.stack(steps[middle:])[None]]
        pieces = []
        arrived = []
        for stage in range(len(self.orders[0])):
            for half in range(2):
                if stage < len(waits):
                    held[half] = after(held[half], *waits[stage])
            found = [self.across(held[half], self.orders[half][stage]) for half in range(2)]
            arrived.append(found)
            if stage == len(self.orders[0]) - 1:
                pieces = [held[0], found[0], held[1], found[1]]
            else:
                held = [jnp.concatenate([held[k], found[k]], axis=0) for k in range(2)]
        return pieces, arrived

    def with_partner(self, pieces, merge):
        if merge:
            pieces = [jnp.stack(pieces)]
        return pieces + [self.partner(p) for p in pieces]

    def everywhere(self, value):
        for bit in self.orders[0]:
            value = value + self.across(value, bit)
        bit = 1
        while bit < self.seqs:
            value = value + self.move(value, lambda r, s, bit=bit: (r, s ^ bit))
            bit *= 2
        return value


class Order:
    def __init__(self):
        self.kernel = None
        self.waits = []

    def pin(self, *values):
        self.waits += values

    def enter(self, value):
        return after(value, *self.waits) if self.waits else value

    def leave(self, value):
        self.kernel = value
        self.waits = [value]

    def late(self, value):
        return after(value, self.kernel)


class Sum:
    def __init__(self, grid, order, parts):
        mine, self.theirs = parts
        self.grid = grid
        self.order = order
        self.halves = [[mine[half]] for half in range(2)]
        self.stage = 0
        self.flight = []
        self.row_stages = len(grid.orders[0])
        self.total = None

    def at(self, step):
        depth = self.grid.depth
        index = lax.rem(self.grid.level - step + 2 * depth, depth)
        return lax.dynamic_index_in_dim(self.levels, index, 0, keepdims=False)

    def land(self):
        came, self.flight = [self.order.late(c) for c in self.flight], []
        if came:
            if self.stage == 1:
                for half in range(2):
                    self.halves[half].append(came[0][half])
            elif self.stage <= 1 + self.row_stages:
                for half in range(2):
                    self.halves[half].append(came[half])
            else:
                self.total = came[0].astype(f32) + self.at(self.stage - self.row_stages)
        return came

    def go(self):
        grid, late = self.grid, self.order.late
        self.land()
        if self.stage == 0:
            sent = [self.theirs]
            self.flight = [grid.partner(self.theirs)]
        elif self.stage <= self.row_stages:
            sent = []
            for half in range(2):
                parts = self.halves[half]
                bit = grid.orders[half][::-1][self.stage - 1]
                count = parts[0].shape[0] // 2
                if half == 0:
                    kept, given = slice(0, count), slice(count, None)
                else:
                    kept, given = slice(0, None, 2), slice(1, None, 2)
                value = sum(p[given].astype(f32) for p in parts).astype(bf16)
                self.halves[half] = [p[kept] for p in parts]
                sent.append(late(value))
                self.flight.append(grid.across(sent[half], bit))
        elif self.stage < self.row_stages + grid.depth:
            if self.total is None:
                self.levels = jnp.concatenate(
                    [sum(p[0].astype(f32) for p in parts) for parts in self.halves], axis=0
                )
                self.total = self.at(1)
            sent = [late(self.total.astype(bf16))]
            self.flight = [grid.around(sent[0])]
        else:
            return []
        self.stage += 1
        return sent

    def finish(self):
        while self.go():
            pass
        return self.total


def loads(grid, place_ref, pieces, target, sems, columns=None, at_column=0):
    row, level, core = place_ref[0], place_ref[1], place_ref[2]
    shard, columns_all = pieces[0].shape[-2:]
    if columns is None:
        columns = (0, columns_all)
    width = columns[1] - columns[0]
    merged = len(pieces) == 2
    copies = []
    for which in range(8):
        ref = pieces[which // 4].at[which % 4] if merged else pieces[which]
        half = which // 2 % 2
        whose = core if which < 4 else 1 - core
        first = 0 if half == 0 else grid.depth // 2
        masks = grid.masks(half)
        masks = masks[len(masks) // 2 :] if which % 2 else masks[: len(masks) // 2]
        for m, mask in enumerate(masks):
            for h in range(ref.shape[1]):
                at_level = lax.rem(level - (first + h) + grid.depth, grid.depth)
                start = ((row ^ mask) * grid.seqs + at_level * 2 + whose) * shard
                copies.append(
                    pltpu.make_async_copy(
                        ref.at[m, h, :, columns[0] : columns[1]],
                        target.at[
                            pl.ds(pl.multiple_of(start, shard), shard),
                            at_column : at_column + width,
                        ],
                        sems.at[len(copies)],
                    )
                )
    return copies


def n_loads(grid):
    return grid.rows * grid.seqs


def project_kernel(grid, normed_slabs, head_dim, with_scale, place_ref, tok_ref, *rest):
    pieces, rest = rest[:2], rest[2:]
    gain_ref, cos_ref, sa_ref, sb_ref, *rest = rest
    if with_scale:
        heads_ref, raw_ref, scale_ref, weight, sems = rest
    else:
        scale_in_ref, heads_ref, raw_ref, weight, sems = rest

    @pl.when(pl.program_id(0) == 0)
    def _():
        copies = loads(grid, place_ref, pieces, weight, sems)
        for copy in copies:
            copy.start()
        for copy in copies:
            copy.wait()

    if with_scale:
        x = tok_ref[...].astype(f32)
        scale = lax.rsqrt(jnp.mean(x * x, axis=-1, keepdims=True) + norm_eps)
        scale_ref[...] = jnp.broadcast_to(scale, scale_ref.shape)
    else:
        scale = scale_in_ref[:, :1]
    projected = mm(tok_ref[...], weight[...]) * scale
    mean_matrix = group_matrix(head_dim, 1.0 / head_dim)
    raw_ref[...] = projected[:, : raw_ref.shape[1]].astype(bf16)
    for slab in range(heads_ref.shape[1] // 128):
        lanes = slice(128 * slab, 128 * slab + 128)
        part = projected[:, lanes]
        if slab < normed_slabs:
            inverse = lax.rsqrt(group_sum(part * part, mean_matrix) + norm_eps)
            part = turn(part * inverse * gain_ref[...], cos_ref, sa_ref, sb_ref)
        heads_ref[:, lanes] = part.astype(bf16)


def project(grid, tokens, pieces, gain, tables, normed, head_dim, scale=None):
    rows, width = tokens.shape
    out_width = pieces[0].shape[-1]
    span = tables[0].shape[0]
    row_block = lambda n: pl.BlockSpec((span, n), lambda i, *_: (i, 0))
    fixed = lambda a: pl.BlockSpec(a.shape, lambda i, *_: (0,) * a.ndim)
    args = [tokens, *pieces, gain, *tables]
    in_specs = [row_block(width)] + [any_spec] * 2 + [fixed(a) for a in (gain, *tables)]
    out_shape = [
        jax.ShapeDtypeStruct((rows, out_width), bf16),
        jax.ShapeDtypeStruct((rows, normed), bf16),
    ]
    out_specs = [row_block(out_width), row_block(normed)]
    if scale is None:
        out_shape.append(jax.ShapeDtypeStruct((rows, 128), f32))
        out_specs.append(row_block(128))
    else:
        args.append(scale)
        in_specs.append(row_block(128))
    return pl.pallas_call(
        functools.partial(project_kernel, grid, normed // 128, head_dim, scale is None),
        grid_spec=pltpu.PrefetchScalarGridSpec(
            num_scalar_prefetch=1,
            grid=(rows // span,),
            in_specs=in_specs,
            out_specs=out_specs,
            scratch_shapes=[
                pltpu.VMEM((width, out_width), bf16),
                pltpu.SemaphoreType.DMA((n_loads(grid),)),
            ],
        ),
        out_shape=out_shape,
        compiler_params=params(1),
        cost_estimate=pl.CostEstimate(
            flops=4 * rows * width * out_width,
            bytes_accessed=2 * (rows * (width + 2 * out_width) + width * out_width),
            transcendentals=rows * normed,
        ),
    )(grid.place, *args)


def placed_pair(slab, parity, low):
    values = slab.astype(f32)
    rolled = pltpu.roll(values, 64, 1)
    here, there = (rolled, values) if parity else (values, rolled)
    return jnp.where(low, here, 0.0), jnp.where(low, 0.0, there)


def block_state(info_ref, seq, base, block, span):
    offset = info_ref[0]
    length = info_ref[1 + seq]
    some = (base >= 0) & (base < jnp.minimum(offset + span, length))
    whole = some & (base + block <= jnp.minimum(offset + 1, length))
    return whole, some & jnp.logical_not(whole)


def allowed(info_ref, seq, base, shape, key_axis, block, span):
    q_pos = info_ref[0] + lax.rem(
        lax.broadcasted_iota(jnp.int32, shape, 1 - key_axis), span
    )
    k_pos = base + lax.rem(lax.broadcasted_iota(jnp.int32, shape, key_axis), block)
    return (k_pos <= q_pos) & (k_pos < info_ref[1 + seq])


def chunk_copies(chunks, buffer, sems, info_ref, seq, n_seqs, slot, span, then, backward=False):
    for i, chunk in enumerate(chunks):
        base = info_ref[1 + n_seqs + i]
        needed = (base >= 0) & (base < jnp.minimum(info_ref[0] + span, info_ref[1 + seq]))
        if backward:
            needed = needed & (info_ref[0] < info_ref[1 + seq])

        @pl.when(needed)
        def _(i=i, chunk=chunk):
            then(pltpu.make_async_copy(chunk.at[seq], buffer.at[slot, i], sems.at[slot, i]))


def fetch_chunks(chunks, buffer, sems, info_ref, span, backward=False):
    seq, n_seqs = pl.program_id(0), pl.num_programs(0)
    slot = lax.rem(seq, 2)
    common = (chunks, buffer, sems, info_ref)

    @pl.when(seq == 0)
    def _():
        chunk_copies(*common, seq, n_seqs, slot, span, lambda c: c.start(), backward)

    @pl.when(seq + 1 < n_seqs)
    def _():
        chunk_copies(*common, seq + 1, n_seqs, 1 - slot, span, lambda c: c.start(), backward)

    chunk_copies(*common, seq, n_seqs, slot, span, lambda c: c.wait(), backward)
    return slot


def stacked_at(ref, head):
    first = head * 256
    return jnp.concatenate(
        [ref[0, :, first : first + 128], ref[0, :, first + 128 : first + 256]], axis=0
    )


def unstack_to(ref, head, value):
    first = head * 256
    span = ref.shape[1]
    ref[0, :, first : first + 128] = value[:span].astype(ref.dtype)
    ref[0, :, first + 128 : first + 256] = value[span:].astype(ref.dtype)


def split_lanes(values):
    lane = lax.rem(lane_iota(values.shape), 64)
    high = values.astype(bf16).astype(f32)
    rest = values - high
    return jnp.where(lane == 0, high, jnp.where(lane == 1, rest, 0.0)).astype(bf16)


def attend_kernel(n, with_acc, finish, info_ref, q_ref, *refs):
    chunks, refs = refs[:n], refs[n:]
    if with_acc:
        acc_in, refs = refs[0], refs[1:]
    if finish:
        out_ref, log_ref, buffer, sems, acc = refs
    else:
        acc_out, buffer, sems, acc = refs
    seq, n_seqs = pl.program_id(0), pl.num_programs(0)
    span = q_ref.shape[1]
    n_heads = q_ref.shape[2] // 256
    slot = fetch_chunks(chunks, buffer, sems, info_ref, span)

    def one_head(head):
        parity = head % 2
        k_lanes = slice(head // 2 * 128, head // 2 * 128 + 128)
        v_lanes = slice((n_heads + head) // 2 * 128, (n_heads + head) // 2 * 128 + 128)
        acc[...] = acc_in[0, head] if with_acc else jnp.zeros(acc.shape, f32)

        @pl.loop(0, n)
        def _(chunk):
            base = info_ref[1 + n_seqs + chunk]
            whole, partly = block_state(info_ref, seq, base, span, span)

            def step(masked):
                low = lane_iota((span, 128)) < 64
                ones_low = jnp.where(low, 1.0, 0.0).astype(bf16)
                ones_high = jnp.where(low, 0.0, 1.0).astype(bf16)
                k0, k1 = placed_pair(buffer[slot, chunk, :, k_lanes], parity, low)
                v0, v1 = placed_pair(buffer[slot, chunk, :, v_lanes], parity, low)
                k_pair = jnp.concatenate([k0, k1], axis=0).astype(bf16)
                v_pair = jnp.concatenate(
                    [
                        jnp.concatenate([v0.astype(bf16), ones_low], axis=1),
                        jnp.concatenate([v1.astype(bf16), ones_high], axis=1),
                    ],
                    axis=0,
                )
                weights = jnp.exp2(mm(stacked_at(q_ref, head), k_pair, NT))
                if masked:
                    ok = allowed(info_ref, seq, base, weights.shape, 1, span, span)
                    weights = jnp.where(ok, weights, 0.0)
                acc[...] += mm(weights.astype(bf16), v_pair)

            @pl.when(whole)
            def _():
                step(False)

            @pl.when(partly)
            def _():
                step(True)

        if finish:
            totals = acc[:, 128:]
            unstack_to(out_ref, head, acc[:, :128] / totals)
            unstack_to(log_ref, head, split_lanes(-jnp.log2(totals)))
        else:
            acc_out[0, head] = acc[...]

    for head in range(n_heads):
        one_head(head)


def attend(info, bases, queries, chunks, acc=None, finish=True):
    seqs, span, width = queries.shape
    n_heads = width // 256
    n = len(chunks)
    q_spec = pl.BlockSpec((1, span, width), lambda b, *_: (b, 0, 0))
    acc_spec = pl.BlockSpec((1, n_heads, 2 * span, 256), lambda b, *_: (b, 0, 0, 0))
    acc_shape = jax.ShapeDtypeStruct((seqs, n_heads, 2 * span, 256), f32)
    args = [queries, *chunks]
    in_specs = [q_spec] + [any_spec] * n
    if acc is not None:
        args.append(acc)
        in_specs.append(acc_spec)
    if finish:
        out_shape = [jax.ShapeDtypeStruct(queries.shape, bf16)] * 2
        out_specs = [q_spec, q_spec]
    else:
        out_shape, out_specs = acc_shape, acc_spec
    return pl.pallas_call(
        functools.partial(attend_kernel, n, acc is not None, finish),
        grid_spec=pltpu.PrefetchScalarGridSpec(
            num_scalar_prefetch=1,
            grid=(seqs,),
            in_specs=in_specs,
            out_specs=out_specs,
            scratch_shapes=[
                pltpu.VMEM((2, n, span, chunks[0].shape[2]), bf16),
                pltpu.SemaphoreType.DMA((2, n)),
                pltpu.VMEM((2 * span, 256), f32),
            ],
        ),
        out_shape=out_shape,
        compiler_params=params(1),
        cost_estimate=pl.CostEstimate(
            flops=4 * 4 * seqs * span * width * span * n,
            bytes_accessed=4 * seqs * (span * width * 3 + n * span * width // 2),
            transcendentals=seqs * span * width // 64 * span * n,
        ),
    )(jnp.concatenate([info, bases]), *args)


def attend_back_kernel(n, with_acc, finish, info_ref, q_ref, do_ref, o_ref, log_ref, *refs):
    chunks, refs = refs[:n], refs[n:]
    if with_acc:
        acc_in, refs = refs[0], refs[1:]
    grads_out, dq_ref, buffer, sems, acc, q_wide, do_wide = refs
    seq, n_seqs = pl.program_id(0), pl.num_programs(0)
    span = q_ref.shape[1]
    n_heads = q_ref.shape[2] // 256
    alive = info_ref[0] < info_ref[1 + seq]
    slot = fetch_chunks(chunks, buffer, sems, info_ref, span, True)
    grads_out[...] = jnp.zeros(grads_out.shape, grads_out.dtype)

    def one_head(head):
        parity = head % 2
        k_lanes = slice(head // 2 * 128, head // 2 * 128 + 128)
        v_lanes = slice((n_heads + head) // 2 * 128, (n_heads + head) // 2 * 128 + 128)
        acc[...] = acc_in[0, head] if with_acc else jnp.zeros(acc.shape, f32)

        @pl.when(alive)
        def _():
            heads = stacked_at(do_ref, head)
            dots = group_sum(
                heads.astype(f32) * stacked_at(o_ref, head).astype(f32), group_matrix(64, 1.0)
            )
            do_wide[:, :128] = heads
            do_wide[:, 128:] = split_lanes(-dots)
            q_wide[:, :128] = stacked_at(q_ref, head)
            q_wide[:, 128:] = stacked_at(log_ref, head)

            @pl.loop(0, n)
            def _(chunk):
                base = info_ref[1 + n_seqs + chunk]
                whole, partly = block_state(info_ref, seq, base, span, span)

                def step(masked):
                    low = lane_iota((span, 128)) < 64
                    half_lane = lax.rem(lane_iota((span, 128)), 64)
                    pick_low = jnp.where(low & (half_lane < 2), 1.0, 0.0)
                    pick_high = jnp.where(low | (half_lane >= 2), 0.0, 1.0)
                    picks = jnp.concatenate([pick_low, pick_high], axis=0).astype(bf16)
                    k0, k1 = placed_pair(buffer[slot, chunk, :, k_lanes], parity, low)
                    v0, v1 = placed_pair(buffer[slot, chunk, :, v_lanes], parity, low)
                    k_pair = jnp.concatenate([k0, k1], axis=0)
                    k_turned = jnp.transpose(k_pair).astype(bf16)
                    k_wide = jnp.concatenate([k_pair.astype(bf16), picks], axis=1)
                    v_wide = jnp.concatenate(
                        [jnp.concatenate([v0, v1], axis=0).astype(bf16), picks], axis=1
                    )
                    weights = jnp.exp2(mm(k_wide, q_wide[...], NT))
                    if masked:
                        ok = allowed(info_ref, seq, base, weights.shape, 0, span, span)
                        weights = jnp.where(ok, weights, 0.0)
                    grads = (weights * mm(v_wide, do_wide[...], NT)).astype(bf16)
                    both_v = mm(weights.astype(bf16), do_wide[:, :128])
                    both_k = mm(grads, q_wide[:, :128]) * math.log(2.0)
                    acc[...] += mm(k_turned, grads)

                    def joined(pair):
                        total = jnp.where(low, pair[:span] + pltpu.roll(pair[span:], 64, 1), 0.0)
                        return pltpu.roll(total, 64, 1) if parity else total

                    dtype = grads_out.dtype
                    grads_out[chunk, 0, :, k_lanes] += joined(both_k).astype(dtype)
                    grads_out[chunk, 0, :, v_lanes] += joined(both_v).astype(dtype)

                @pl.when(whole)
                def _():
                    step(False)

                @pl.when(partly)
                def _():
                    step(True)

        if finish:
            unstack_to(dq_ref, head, jnp.transpose(acc[...]) * 0.125)
        else:
            dq_ref[0, head] = acc[...]

    for head in range(n_heads):
        one_head(head)


def attend_back(info, bases, queries, grad_out, out, logs, chunks, acc=None, finish=True):
    seqs, span, width = queries.shape
    n_heads = width // 256
    n = len(chunks)
    q_spec = pl.BlockSpec((1, span, width), lambda b, *_: (b, 0, 0))
    acc_spec = pl.BlockSpec((1, n_heads, 128, 2 * span), lambda b, *_: (b, 0, 0, 0))
    acc_shape = jax.ShapeDtypeStruct((seqs, n_heads, 128, 2 * span), f32)
    args = [queries, grad_out, out, logs, *chunks]
    in_specs = [q_spec] * 4 + [any_spec] * n
    if acc is not None:
        args.append(acc)
        in_specs.append(acc_spec)
    kv_width = chunks[0].shape[2]
    if finish:
        dq_shape, dq_spec = jax.ShapeDtypeStruct(queries.shape, bf16), q_spec
    else:
        dq_shape, dq_spec = acc_shape, acc_spec
    grads, dq = pl.pallas_call(
        functools.partial(attend_back_kernel, n, acc is not None, finish),
        grid_spec=pltpu.PrefetchScalarGridSpec(
            num_scalar_prefetch=1,
            grid=(seqs,),
            in_specs=in_specs,
            out_specs=[
                pl.BlockSpec((n, 1, span, kv_width), lambda b, *_: (0, b, 0, 0)),
                dq_spec,
            ],
            scratch_shapes=[
                pltpu.VMEM((2, n, span, kv_width), bf16),
                pltpu.SemaphoreType.DMA((2, n)),
                pltpu.VMEM((128, 2 * span), f32),
                pltpu.VMEM((2 * span, 256), bf16),
                pltpu.VMEM((2 * span, 256), bf16),
            ],
        ),
        out_shape=[jax.ShapeDtypeStruct((n, seqs, span, kv_width), bf16), dq_shape],
        compiler_params=params(1),
        cost_estimate=pl.CostEstimate(
            flops=10 * 4 * seqs * span * width * span * n,
            bytes_accessed=4 * seqs * (span * width * 4 + span * n * width),
            transcendentals=seqs * span * width // 64 * span * n,
        ),
    )(jnp.concatenate([info, bases]), *args)
    return [grads[i] for i in range(n)] + [dq]


def unproject_kernel(
    head_dim,
    info_ref,
    grad_ref,
    raw_ref,
    scale_ref,
    gain_ref,
    cos_ref,
    sa_ref,
    sb_ref,
    out_ref,
    sum_ref,
):
    @pl.when(pl.program_id(0) == 0)
    def _():
        sum_ref[...] = jnp.zeros(sum_ref.shape, f32)

    alive = info_ref[0] < info_ref[1 + pl.program_id(0)]

    @pl.when(jnp.logical_not(alive))
    def _():
        out_ref[...] = jnp.zeros(out_ref.shape, out_ref.dtype)

    @pl.when(alive)
    def _():
        scale = scale_ref[:, :1]
        mean_matrix = group_matrix(head_dim, 1.0 / head_dim)
        normed = raw_ref.shape[1]
        for slab in range(normed // 128):
            lanes = slice(128 * slab, 128 * slab + 128)
            raw = raw_ref[:, lanes].astype(f32)
            inverse = lax.rsqrt(group_sum(raw * raw, mean_matrix) + norm_eps)
            unit = raw * inverse
            turned = turn_back(grad_ref[:, lanes].astype(f32), cos_ref, sa_ref, sb_ref)
            sum_ref[...] += jnp.broadcast_to(
                jnp.sum(turned * unit, axis=0, keepdims=True), sum_ref.shape
            )
            inner = turned * gain_ref[...]
            mean = group_sum(inner * unit, mean_matrix)
            out_ref[:, lanes] = (inverse * (inner - unit * mean) * scale).astype(bf16)
        if normed < grad_ref.shape[1]:
            out_ref[:, normed:] = (grad_ref[:, normed:].astype(f32) * scale).astype(bf16)


def unproject(info, grad, raw, scale, gain, tables, head_dim):
    rows, width = grad.shape
    span = tables[0].shape[0]
    row_block = lambda a: pl.BlockSpec((span, a.shape[1]), lambda i, *_: (i, 0))
    fixed = lambda a: pl.BlockSpec(a.shape, lambda i, *_: (0,) * a.ndim)
    return pl.pallas_call(
        functools.partial(unproject_kernel, head_dim),
        grid_spec=pltpu.PrefetchScalarGridSpec(
            num_scalar_prefetch=1,
            grid=(rows // span,),
            in_specs=[row_block(a) for a in (grad, raw, scale)]
            + [fixed(a) for a in (gain, *tables)],
            out_specs=[row_block(grad), pl.BlockSpec((8, 128), lambda i, *_: (0, 0))],
        ),
        out_shape=[
            jax.ShapeDtypeStruct((rows, width), bf16),
            jax.ShapeDtypeStruct((8, 128), f32),
        ],
        compiler_params=params(1),
        cost_estimate=pl.CostEstimate(
            flops=8 * 128 * rows * width,
            bytes_accessed=6 * rows * width,
            transcendentals=rows * width,
        ),
    )(info, grad, raw, scale, gain, *tables)


def feed_kernel(
    grid,
    span,
    split,
    info_ref,
    place_ref,
    tok_ref,
    heads_ref,
    cot_ref,
    *rest,
):
    pieces, rest = rest[:8], rest[8:]
    out_ref, hidden_ref, mid_ref, dgu_ref, dmid_ref, dheads_ref, *rest = rest
    w_out, w_gu, w_down, out_sems, gu_sems, down_sems = rest
    a, b = split

    @pl.when(pl.program_id(0) == 0)
    def _():
        copies = (
            loads(grid, place_ref, pieces, w_out, out_sems, (0, a))
            + loads(grid, place_ref, pieces, w_gu, gu_sems, (2 * a, 2 * a + b))
            + loads(grid, place_ref, pieces, w_down, down_sems, (a, 2 * a))
        )
        for copy in copies:
            copy.start()
        for copy in copies:
            copy.wait()

    rows = tok_ref.shape[0]
    middle = tok_ref[...].astype(f32) + mm(heads_ref[...], w_out[...], NT)
    middle_low = middle.astype(bf16)
    mid_ref[...] = middle_low
    scale = lax.rsqrt(jnp.mean(middle * middle, axis=-1, keepdims=True) + norm_eps)
    gate_up = mm(middle_low, w_gu[...]) * scale
    half = gate_up.shape[1] // 2
    gate, up = gate_up[:, :half], gate_up[:, half:]
    sig = 1.0 / (1.0 + jnp.exp(-gate))
    silu = gate * sig
    hidden = silu * up
    hidden_low = hidden.astype(bf16)
    out_ref[...] = (middle + mm(hidden_low, w_down[...], NT)).astype(bf16)

    first = pl.program_id(0) * (rows // span)
    count = rows // span
    longest = info_ref[1 + first]
    for k in range(1, count):
        longest = jnp.maximum(longest, info_ref[1 + first + k])
    alive = info_ref[0] < longest

    @pl.when(alive)
    def _():
        position = lax.broadcasted_iota(jnp.int32, (span, 1), 0) + info_ref[0]
        valid = jnp.concatenate(
            [(position < info_ref[1 + first + k]).astype(f32) for k in range(count)], axis=0
        )
        hidden_ref[...] = (hidden * valid).astype(bf16)
        cot = cot_ref[...].astype(f32) * valid
        grad_hidden = mm(cot.astype(bf16), w_down[...])
        grad_gate = grad_hidden * up * (sig * (1.0 + gate * (1.0 - sig))) * scale
        grad_up = grad_hidden * silu * scale
        grad_gu = jnp.concatenate([grad_gate.astype(bf16), grad_up.astype(bf16)], axis=1)
        dgu_ref[...] = grad_gu
        back = mm(grad_gu, w_gu[...], NT)
        unit = middle * scale
        grad_mid = cot + back - unit * jnp.mean(back * unit, axis=-1, keepdims=True)
        grad_mid = grad_mid.astype(bf16)
        dmid_ref[...] = grad_mid
        dheads_ref[...] = mm(grad_mid, w_out[...]).astype(bf16)

    @pl.when(jnp.logical_not(alive))
    def _():
        for ref in (hidden_ref, dgu_ref, dmid_ref, dheads_ref):
            ref[...] = jnp.zeros(ref.shape, ref.dtype)


def feed(grid, info, tokens, heads, cotangent, pieces, split, span):
    rows, width = tokens.shape
    a, b = split
    tile = max(span, min(256, rows))
    block = lambda n: pl.BlockSpec((tile, n), lambda i, *_: (i, 0))
    shape = lambda n: jax.ShapeDtypeStruct((rows, n), bf16)
    n = n_loads(grid)
    outs = (width, a, width, b, width, a)
    macs = width * (2 * a + b)
    return pl.pallas_call(
        functools.partial(feed_kernel, grid, span, split),
        grid_spec=pltpu.PrefetchScalarGridSpec(
            num_scalar_prefetch=2,
            grid=(rows // tile,),
            in_specs=[block(width), block(a), block(width)] + [any_spec] * 8,
            out_specs=[block(n) for n in outs],
            scratch_shapes=[
                pltpu.VMEM((width, a), bf16),
                pltpu.VMEM((width, b), bf16),
                pltpu.VMEM((width, a), bf16),
                pltpu.SemaphoreType.DMA((n,)),
                pltpu.SemaphoreType.DMA((n,)),
                pltpu.SemaphoreType.DMA((n,)),
            ],
        ),
        out_shape=[shape(n) for n in outs],
        compiler_params=params(1),
        cost_estimate=pl.CostEstimate(
            flops=6 * rows * macs,
            bytes_accessed=2 * (rows * (sum(outs) + 2 * width + a) + macs),
            transcendentals=rows * a,
        ),
    )(info, grid.place, tokens, heads, cotangent, *pieces)


def load_all(copies):
    for copy in copies:
        copy.start()
    for copy in copies:
        copy.wait()


def query_back_kernel(grid, info_ref, place_ref, grad_ref, *rest):
    pieces, (out_ref, weight, sems) = rest[:2], rest[2:]

    @pl.when(pl.program_id(0) == 0)
    def _():
        load_all(loads(grid, place_ref, pieces, weight, sems))

    @pl.when(info_ref[0] < info_ref[1 + pl.program_id(0)])
    def _():
        out_ref[...] = mm(grad_ref[...], weight[...], NT)


def query_back(grid, info, grad, pieces, width, span):
    rows, inner = grad.shape
    return pl.pallas_call(
        functools.partial(query_back_kernel, grid),
        grid_spec=pltpu.PrefetchScalarGridSpec(
            num_scalar_prefetch=2,
            grid=(rows // span,),
            in_specs=[pl.BlockSpec((span, inner), lambda i, *_: (i, 0))] + [any_spec] * 2,
            out_specs=pl.BlockSpec((span, width), lambda i, *_: (i, 0)),
            scratch_shapes=[
                pltpu.VMEM((width, inner), bf16),
                pltpu.SemaphoreType.DMA((n_loads(grid),)),
            ],
        ),
        out_shape=jax.ShapeDtypeStruct((rows, width), f32),
        compiler_params=params(1),
        cost_estimate=pl.CostEstimate(
            flops=2 * rows * width * inner,
            bytes_accessed=2 * (rows * (2 * width + inner) + width * inner),
            transcendentals=0,
        ),
    )(info, grid.place, grad, *pieces)


def last_kernel(grid, info_ref, place_ref, tok_ref, grad_ref, back_ref, dmid_ref, scale_ref, *rest):
    pieces, (out_ref, weight, sems) = rest[:2], rest[2:]

    @pl.when(pl.program_id(0) == 0)
    def _():
        load_all(loads(grid, place_ref, pieces, weight, sems))

    alive = info_ref[0] < info_ref[1 + pl.program_id(0)]

    @pl.when(alive)
    def _():
        back = back_ref[...] + mm(grad_ref[...], weight[...], NT)
        unit = tok_ref[...].astype(f32) * scale_ref[:, :1]
        grad = dmid_ref[...].astype(f32) + back
        grad = grad - unit * jnp.mean(back * unit, axis=-1, keepdims=True)
        out_ref[...] = grad.astype(bf16)

    @pl.when(jnp.logical_not(alive))
    def _():
        out_ref[...] = jnp.zeros(out_ref.shape, out_ref.dtype)


def last(grid, info, tokens, grad_kv, back, grad_mid, scale, pieces, span):
    rows, width = tokens.shape
    block = lambda a: pl.BlockSpec((span, a.shape[1]), lambda i, *_: (i, 0))
    inner = grad_kv.shape[1]
    args = (tokens, grad_kv, back, grad_mid, scale)
    return pl.pallas_call(
        functools.partial(last_kernel, grid),
        grid_spec=pltpu.PrefetchScalarGridSpec(
            num_scalar_prefetch=2,
            grid=(rows // span,),
            in_specs=[block(a) for a in args] + [any_spec] * 2,
            out_specs=block(tokens),
            scratch_shapes=[
                pltpu.VMEM((width, inner), bf16),
                pltpu.SemaphoreType.DMA((n_loads(grid),)),
            ],
        ),
        out_shape=jax.ShapeDtypeStruct(tokens.shape, bf16),
        compiler_params=params(1),
        cost_estimate=pl.CostEstimate(
            flops=2 * rows * width * inner,
            bytes_accessed=2 * (rows * (5 * width + inner) + width * inner),
            transcendentals=0,
        ),
    )(info, grid.place, *args, *pieces)


def weight_kernel(grid, shard, span, n_pairs, place_ref, info_ref, *refs):
    lefts, rights = refs[:n_pairs], refs[n_pairs : 2 * n_pairs]
    mine_ref, theirs_ref, acc = refs[2 * n_pairs :]
    core = place_ref[2]
    middle = grid.depth // 2
    n_seqs = lefts[0].shape[0] // span
    shortest = info_ref[1]
    for seq in range(1, n_seqs):
        shortest = jnp.minimum(shortest, info_ref[1 + seq])
    all_alive = info_ref[0] < shortest
    column = 0
    for left, right in zip(lefts, rights):
        width = right.shape[1]

        @pl.when(all_alive)
        def _(left=left, right=right, width=width):
            acc[:, :width] = mm(left[...], right[...], TN)

        @pl.when(jnp.logical_not(all_alive))
        def _(left=left, right=right, width=width):
            acc[:, :width] = jnp.zeros((acc.shape[0], width), f32)
            for seq in range(n_seqs):
                rows = slice(seq * span, (seq + 1) * span)

                @pl.when(info_ref[0] < info_ref[1 + seq])
                def _(rows=rows):
                    acc[:, :width] += mm(left[rows, :], right[rows, :], TN)

        for level in range(grid.depth):
            half, at = level // middle, level % middle
            for whose, ref in ((core, mine_ref), (1 - core, theirs_ref)):
                start = pl.multiple_of((level * 2 + whose) * shard, shard)
                ref[half, 0, at, :, column : column + width] = acc[
                    pl.ds(start, shard), :width
                ].astype(bf16)
        column += width


def weight_grad(grid, info, span, *pairs):
    lefts, rights = [p[0] for p in pairs], [p[1] for p in pairs]
    rows, features = lefts[0].shape
    widths = [r.shape[1] for r in rights]
    total = sum(widths)
    part = features // grid.rows
    shard = part // grid.seqs
    middle = grid.depth // 2
    shape = jax.ShapeDtypeStruct((2, grid.rows, middle, shard, total), bf16)
    piece = pl.BlockSpec((2, 1, middle, shard, total), lambda i, *_: (0, i, 0, 0, 0))
    return pl.pallas_call(
        functools.partial(weight_kernel, grid, shard, span, len(pairs)),
        grid_spec=pltpu.PrefetchScalarGridSpec(
            num_scalar_prefetch=2,
            grid=(grid.rows,),
            in_specs=[pl.BlockSpec((rows, part), lambda i, place, info: (0, place[0] ^ i))]
            * len(pairs)
            + [pl.BlockSpec(r.shape, lambda i, *_: (0, 0)) for r in rights],
            out_specs=[piece, piece],
            scratch_shapes=[pltpu.VMEM((part, max(widths)), f32)],
        ),
        out_shape=[shape, shape],
        compiler_params=params(1),
        cost_estimate=pl.CostEstimate(
            flops=2 * rows * features * total,
            bytes_accessed=2 * (rows * (features * len(pairs) + total) + features * total),
            transcendentals=0,
        ),
    )(grid.place, info, *lefts, *rights)


def shards(
    n_rows,
    n_seqs,
    tokens,
    lengths,
    cotangent,
    w_qkv,
    w_out,
    w_gateup,
    w_down,
    norm_attn,
    norm_ffn,
    q_gain,
    k_gain,
):
    grid = Grid(n_rows, n_seqs)
    seq_count, span_len, model_width = tokens.shape
    row_count = seq_count * span_len
    head_dim = q_gain.shape[0]
    half_dim = head_dim // 2
    query_width = w_out.shape[1]
    kv_width = (w_qkv.shape[1] - query_width) // 2
    log2_scale = math.log2(math.e) * head_dim ** (-0.5)

    offset = (grid.seq * span_len).astype(jnp.int32)
    positions = offset + jnp.arange(span_len, dtype=jnp.int32)
    inverse = theta_base ** (-jnp.arange(half_dim, dtype=f32) * 2.0 / head_dim)
    angles = positions.astype(f32)[:, None] * inverse[None, :]
    cosine, sine = jnp.cos(angles), jnp.sin(angles)
    nothing = jnp.zeros_like(sine)
    tables = (
        jnp.concatenate([cosine] * 4, axis=1),
        jnp.concatenate([-sine, nothing] * 2, axis=1),
        jnp.concatenate([nothing, sine] * 2, axis=1),
    )
    q_gain_f = jnp.concatenate([q_gain.astype(f32)] * 2)[None, :]
    k_gain_f = jnp.concatenate([k_gain.astype(f32)] * 2)[None, :]
    info = jnp.concatenate([offset[None], lengths])

    attn_gain = norm_attn.astype(f32)[:, None]
    ffn_gain = norm_ffn.astype(f32)[:, None]
    qkv_shard = (w_qkv.astype(f32) * attn_gain).astype(bf16)
    gateup_shard = (w_gateup.astype(f32) * ffn_gain).astype(bf16)

    order = Order()
    depth = grid.depth
    kv_steps = grid.ring(qkv_shard[:, query_width:])
    kv_own, kv_came = grid.spread(kv_steps)
    q_steps = grid.ring(
        qkv_shard[:, :query_width], [[], [kv_steps[2]]] + [[kv_steps[-1]]] * (depth - 3)
    )
    feed_steps = grid.ring(
        jnp.concatenate([w_out, w_down, gateup_shard], axis=1),
        [[kv_steps[1]], kv_came[0]] + [kv_came[-1]] * (depth - 3),
    )
    kv_pieces = grid.with_partner(kv_own, True)
    q_own, q_came = grid.spread(q_steps, [kv_came[-1]])
    q_pieces = grid.with_partner(q_own, True)
    feed_own, feed_came = grid.spread(feed_steps, [q_came[-1]])

    rows_in = tokens.reshape(row_count, model_width)
    kv, k_raw, scale1 = project(grid, rows_in, kv_pieces, k_gain_f, tables, kv_width, head_dim)
    order.leave(kv)
    kv = kv.reshape(seq_count, span_len, 2 * kv_width)
    q, q_raw = project(
        grid,
        order.enter(rows_in),
        q_pieces,
        q_gain_f * log2_scale,
        tables,
        query_width,
        head_dim,
        scale1,
    )
    order.leave(q)
    order.pin(*feed_came[0])
    feed_held = [grid.partner(order.late(feed_own[k])) for k in (0, 2)]
    q = q.reshape(seq_count, span_len, query_width)

    reach = [kv]
    for step in range(1, depth):
        held = reach[-1] if step == 1 else order.late(reach[-1])
        reach.append(grid.up(held))
    chunks, bases = [], []
    for step in range(depth):
        level = grid.level - step
        start = jnp.stack([level * 2 + grid.core, level * 2 + 1 - grid.core]) * span_len
        bases.append(jnp.where(level >= 0, start, -1).astype(jnp.int32))
    chunks = [(own, grid.partner(own)) for own in reach[:-1]]
    near = [c for pair in chunks for c in pair]
    acc = attend(info, jnp.concatenate(bases[:-1]), order.enter(q), near, None, False)
    order.leave(acc)
    feed_found = [grid.partner(order.late(feed_own[k])) for k in (1, 3)]
    order.pin(*feed_came[-1], *feed_held)
    feed_pieces = feed_own + [feed_held[0], feed_found[0], feed_held[1], feed_found[1]]
    farthest = order.late(reach[-1])
    chunks.append((farthest, grid.partner(farthest)))
    heads, logs = attend(info, bases[-1], order.enter(q), list(chunks[-1]), acc, True)
    order.leave(heads)
    attended = heads.reshape(row_count, query_width)

    flat_cot = cotangent.reshape(row_count, model_width)
    output, hidden, middle, grad_gu, grad_mid, grad_heads = feed(
        grid,
        info,
        rows_in,
        attended,
        flat_cot,
        feed_pieces,
        (query_width, w_gateup.shape[1]),
        span_len,
    )
    order.leave(hidden)
    grad_heads = grad_heads.reshape(seq_count, span_len, query_width)

    def advance(*sums):
        for each in sums:
            order.pin(*each.land())
            order.pin(*each.go())

    kv_flight = []

    def kv_hop(own, other):
        kv_flight[:] = [order.late(came) for came in kv_flight]
        order.pin(other, *kv_flight)
        here = own.astype(f32) + other.astype(f32)
        for came in kv_flight:
            here = here + came.astype(f32)
        sent = order.late(here.astype(bf16))
        order.pin(sent)
        kv_flight[:] = [grid.down(sent)]

    feed_sum = Sum(
        grid,
        order,
        weight_grad(grid, info, span_len, (flat_cot, hidden), (middle, grad_gu)),
    )
    order.leave(feed_sum.theirs)
    advance(feed_sum)

    split = max(1, depth // 2)
    far = [c for pair in chunks[split:] for c in pair]
    near = [c for pair in chunks[:split] for c in pair]
    *far_grads, acc_q = attend_back(
        info,
        jnp.concatenate(bases[split:]),
        order.enter(q),
        grad_heads,
        heads,
        logs,
        far,
        None,
        False,
    )
    order.leave(acc_q)
    far_grads = [far_grads[2 * k : 2 * k + 2] for k in range(depth - split)]
    crossed = [grid.partner(other) for _, other in far_grads]
    kv_hop(far_grads[-1][0], crossed[-1])
    advance(feed_sum)
    *near_grads, grad_q = attend_back(
        info,
        jnp.concatenate(bases[:split]),
        order.enter(q),
        grad_heads,
        heads,
        logs,
        near,
        acc_q,
        True,
    )
    order.leave(grad_q)
    near_grads = [near_grads[2 * k : 2 * k + 2] for k in range(split)]
    crossed = [grid.partner(order.late(other)) for _, other in near_grads] + crossed
    all_grads = near_grads + far_grads
    for step in reversed(range(split, depth - 1)):
        kv_hop(all_grads[step][0], crossed[step])
    advance(feed_sum)
    grad_pq, gq = unproject(
        info,
        order.enter(grad_q.reshape(row_count, query_width)),
        q_raw,
        scale1,
        q_gain_f,
        tables,
        head_dim,
    )
    order.leave(grad_pq)
    square_sum = Sum(
        grid,
        order,
        weight_grad(
            grid, info, span_len, (rows_in, order.enter(grad_pq)), (grad_mid, attended)
        ),
    )
    order.leave(square_sum.theirs)
    for step in reversed(range(1, split)):
        kv_hop(all_grads[step][0], crossed[step])
    advance(feed_sum, square_sum)
    back_q = query_back(grid, info, order.enter(grad_pq), q_pieces, model_width, span_len)
    order.leave(back_q)

    kv_flight = [order.late(came) for came in kv_flight]
    order.pin(*kv_flight)
    advance(feed_sum, square_sum)
    grad_kv = all_grads[0][0].astype(f32) + crossed[0].astype(f32)
    for came in kv_flight:
        grad_kv = grad_kv + came.astype(f32)
    grad_kv = grad_kv.astype(bf16).reshape(row_count, 2 * kv_width)
    grad_pkv, gk = unproject(
        info, order.enter(grad_kv), k_raw, scale1, k_gain_f, tables, head_dim
    )
    order.leave(grad_pkv)
    kv_sum = Sum(
        grid, order, weight_grad(grid, info, span_len, (rows_in, order.enter(grad_pkv)))
    )
    order.leave(kv_sum.theirs)
    advance(feed_sum, square_sum, kv_sum)
    grad_tokens = last(
        grid,
        info,
        rows_in,
        order.enter(grad_pkv),
        back_q,
        grad_mid,
        scale1,
        kv_pieces,
        span_len,
    )
    order.leave(grad_tokens)
    gains = grid.everywhere(jnp.concatenate([gq[:1], gk[:1]], axis=0))
    gains = gains[:, :head_dim] + gains[:, head_dim:]
    kv_total, square_total, feed_total = kv_sum.finish(), square_sum.finish(), feed_sum.finish()
    sum_qkv = jnp.concatenate([square_total[:, :query_width], kv_total], axis=1)
    sum_out = square_total[:, query_width:]
    sum_down, sum_gateup = feed_total[:, :query_width], feed_total[:, query_width:]
    return (
        output.reshape(tokens.shape),
        grad_tokens.reshape(tokens.shape),
        sum_qkv * attn_gain,
        sum_out,
        sum_gateup * ffn_gain,
        sum_down,
        jnp.sum(sum_qkv * w_qkv.astype(f32), axis=1),
        jnp.sum(sum_gateup * w_gateup.astype(f32), axis=1),
        gains[0],
        gains[1],
    )


def solution(mesh):
    rows = P("row", "seq", None)
    weight = P(both, None)
    vector = P(both)
    return jax.shard_map(
        functools.partial(shards, mesh.shape["row"], mesh.shape["seq"]),
        mesh=mesh,
        in_specs=(rows, P("row"), rows, weight, weight, weight, weight, vector, vector, P(), P()),
        out_specs=(rows, rows, weight, weight, weight, weight, vector, vector, P(), P()),
        check_vma=False,
    )
```

```python
import functools
import math

import jax
import jax.numpy as jnp
from jax import lax
from jax.experimental import pallas as pl
from jax.experimental.pallas import tpu as pltpu
from jax.sharding import PartitionSpec as P

norm_eps = 1e-06
theta_base = 10000.0
both = ("row", "seq")
f32 = jnp.float32
bf16 = jnp.bfloat16
vmem_cap = 56 * 1024 * 1024
any_spec = pl.BlockSpec(memory_space=pl.ANY)
NN = (((1,), (0,)), ((), ()))
NT = (((1,), (1,)), ((), ()))
TN = (((0,), (0,)), ((), ()))


def mm(left, right, dims=NN):
    return lax.dot_general(left, right, dims, preferred_element_type=f32)


def after(value, *earlier):
    return lax.optimization_barrier((value, *earlier))[0]


def params(n_grid):
    return pltpu.CompilerParams(
        dimension_semantics=("arbitrary",) * n_grid, vmem_limit_bytes=vmem_cap
    )


def lane_iota(shape):
    return lax.broadcasted_iota(jnp.int32, shape, len(shape) - 1)


def group_matrix(head_dim, value):
    i = lax.broadcasted_iota(jnp.int32, (128, 128), 0) // head_dim
    j = lax.broadcasted_iota(jnp.int32, (128, 128), 1) // head_dim
    return jnp.where(i == j, value, 0.0).astype(bf16)


def group_sum(values, matrix):
    high = values.astype(bf16)
    low = (values - high.astype(f32)).astype(bf16)
    return mm(high, matrix) + mm(low, matrix)


def turn(values, cos_ref, sa_ref, sb_ref):
    return (
        values * cos_ref[...]
        + pltpu.roll(values, 96, 1) * sa_ref[...]
        + pltpu.roll(values, 32, 1) * sb_ref[...]
    )


def turn_back(values, cos_ref, sa_ref, sb_ref):
    return (
        values * cos_ref[...]
        - pltpu.roll(values, 96, 1) * sa_ref[...]
        - pltpu.roll(values, 32, 1) * sb_ref[...]
    )


class Grid:
    def __init__(self, rows, seqs):
        self.rows, self.seqs, self.depth = rows, seqs, seqs // 2
        self.row = lax.axis_index("row")
        seq = lax.axis_index("seq")
        self.level, self.core = seq // 2, lax.rem(seq, 2)
        self.seq = seq
        bits = [1 << k for k in range(rows.bit_length() - 1)]
        self.orders = (bits, bits[::-1])
        self.place = jnp.stack([self.row, self.level, self.core]).astype(jnp.int32)

    def move(self, value, where):
        pairs = []
        for row in range(self.rows):
            for seq in range(self.seqs):
                target = where(row, seq)
                if target is not None:
                    pairs.append((row * self.seqs + seq, target[0] * self.seqs + target[1]))
        return lax.ppermute(value, both, pairs)

    def across(self, value, mask):
        return self.move(value, lambda r, s: (r ^ mask, s))

    def partner(self, value):
        return self.move(value, lambda r, s: (r, s ^ 1))

    def around(self, value, steps=1):
        return self.move(value, lambda r, s: (r, (s + 2 * steps) % self.seqs))

    def up(self, value):
        return self.move(value, lambda r, s: (r, s + 2) if s + 2 < self.seqs else None)

    def down(self, value):
        return self.move(value, lambda r, s: (r, s - 2) if s >= 2 else None)

    def masks(self, half):
        found = [0]
        for bit in self.orders[half]:
            found = found + [m ^ bit for m in found]
        return found

    def ring(self, shard, waits=()):
        steps = [shard]
        for hop in range(self.depth - 1):
            held = steps[-1]
            if hop < len(waits):
                held = after(held, *waits[hop])
            steps.append(self.around(held))
        return steps

    def spread(self, steps, waits=()):
        middle = self.depth // 2
        held = [jnp.stack(steps[:middle])[None], jnp.stack(steps[middle:])[None]]
        pieces = []
        arrived = []
        for stage in range(len(self.orders[0])):
            for half in range(2):
                if stage < len(waits):
                    held[half] = after(held[half], *waits[stage])
            found = [self.across(held[half], self.orders[half][stage]) for half in range(2)]
            arrived.append(found)
            if stage == len(self.orders[0]) - 1:
                pieces = [held[0], found[0], held[1], found[1]]
            else:
                held = [jnp.concatenate([held[k], found[k]], axis=0) for k in range(2)]
        return pieces, arrived

    def with_partner(self, pieces, *waits):
        pieces = jnp.stack(pieces)
        return [pieces, self.partner(after(pieces, *waits) if waits else pieces)]


class Order:
    def __init__(self):
        self.kernel = None
        self.waits = []

    def pin(self, *values):
        self.waits += values

    def enter(self, value):
        return after(value, *self.waits) if self.waits else value

    def leave(self, value):
        self.kernel = value
        self.waits = [value]

    def late(self, value):
        return after(value, self.kernel)


class Everywhere:
    def __init__(self, grid, order, value):
        self.grid, self.order, self.total = grid, order, value
        self.flight = []
        self.moves = [(bit, 0) for bit in grid.orders[0]]
        self.moves += [(0, 1 << k) for k in range(grid.seqs.bit_length() - 1)]

    def land(self):
        came, self.flight = [self.order.late(c) for c in self.flight], []
        for each in came:
            self.total = self.total + each
        return came

    def go(self):
        self.land()
        if not self.moves:
            return []
        row, seq = self.moves.pop(0)
        sent = self.order.late(self.total)
        self.flight = [self.grid.move(sent, lambda r, s: (r ^ row, s ^ seq))]
        return [sent]

    def finish(self):
        while self.go():
            pass
        return self.total


class Sum:
    def __init__(self, grid, order, parts, direct=False):
        mine, self.theirs = parts
        self.direct = direct
        self.grid = grid
        self.order = order
        self.halves = [[mine[half]] for half in range(2)]
        self.stage = 0
        self.flight = []
        self.row_stages = len(grid.orders[0])
        self.total = None

    def at(self, step):
        depth = self.grid.depth
        index = lax.rem(self.grid.level - step + 2 * depth, depth)
        return lax.dynamic_index_in_dim(self.levels, index, 0, keepdims=False)

    def land(self):
        came, self.flight = [self.order.late(c) for c in self.flight], []
        if came:
            if self.stage == 1:
                for half in range(2):
                    self.halves[half].append(came[0][half])
            elif self.stage <= 1 + self.row_stages:
                for half in range(2):
                    self.halves[half].append(came[half])
            elif self.direct:
                self.total = self.total + sum(c.astype(f32) for c in came)
            else:
                self.total = came[0].astype(f32) + self.at(self.stage - self.row_stages)
        return came

    def go(self):
        grid, late = self.grid, self.order.late
        self.land()
        if self.stage == 0:
            sent = [self.theirs]
            self.flight = [grid.partner(self.theirs)]
        elif self.stage <= self.row_stages:
            sent = []
            for half in range(2):
                parts = self.halves[half]
                bit = grid.orders[half][::-1][self.stage - 1]
                count = parts[0].shape[0] // 2
                if half == 0:
                    kept, given = slice(0, count), slice(count, None)
                else:
                    kept, given = slice(0, None, 2), slice(1, None, 2)
                value = sum(p[given].astype(f32) for p in parts).astype(bf16)
                self.halves[half] = [p[kept] for p in parts]
                sent.append(late(value))
                self.flight.append(grid.across(sent[half], bit))
        elif self.direct:
            if self.total is not None:
                return []
            self.levels = jnp.concatenate(
                [sum(p[0].astype(f32) for p in parts) for parts in self.halves], axis=0
            )
            self.total = self.at(0)
            sent = [
                late(self.at(grid.depth - step).astype(bf16)) for step in range(1, grid.depth)
            ]
            self.flight = [grid.around(each, k + 1) for k, each in enumerate(sent)]
        elif self.stage < self.row_stages + grid.depth:
            if self.total is None:
                self.levels = jnp.concatenate(
                    [sum(p[0].astype(f32) for p in parts) for parts in self.halves], axis=0
                )
                self.total = self.at(1)
            sent = [late(self.total.astype(bf16))]
            self.flight = [grid.around(sent[0])]
        else:
            return []
        self.stage += 1
        return sent

    def finish(self):
        while self.go():
            pass
        return self.total


def loads(grid, place_ref, pieces, target, sems, columns=None, at_column=0):
    row, level, core = place_ref[0], place_ref[1], place_ref[2]
    shard, columns_all = pieces[0].shape[-2:]
    if columns is None:
        columns = (0, columns_all)
    width = columns[1] - columns[0]
    merged = len(pieces) == 2
    copies = []
    for which in range(8):
        ref = pieces[which // 4].at[which % 4] if merged else pieces[which]
        half = which // 2 % 2
        whose = core if which < 4 else 1 - core
        first = 0 if half == 0 else grid.depth // 2
        masks = grid.masks(half)
        masks = masks[len(masks) // 2 :] if which % 2 else masks[: len(masks) // 2]
        for m, mask in enumerate(masks):
            for h in range(ref.shape[1]):
                at_level = lax.rem(level - (first + h) + grid.depth, grid.depth)
                start = ((row ^ mask) * grid.seqs + at_level * 2 + whose) * shard
                copies.append(
                    pltpu.make_async_copy(
                        ref.at[m, h, :, columns[0] : columns[1]],
                        target.at[
                            pl.ds(pl.multiple_of(start, shard), shard),
                            at_column : at_column + width,
                        ],
                        sems.at[len(copies)],
                    )
                )
    return copies


def n_loads(grid):
    return grid.rows * grid.seqs


def project_kernel(grid, normed_slabs, head_dim, with_scale, place_ref, tok_ref, *rest):
    pieces, rest = rest[:2], rest[2:]
    gain_ref, cos_ref, sa_ref, sb_ref, *rest = rest
    if with_scale:
        heads_ref, raw_ref, scale_ref, weight, sems = rest
    else:
        scale_in_ref, heads_ref, raw_ref, weight, sems = rest

    @pl.when(pl.program_id(0) == 0)
    def _():
        copies = loads(grid, place_ref, pieces, weight, sems)
        for copy in copies:
            copy.start()
        for copy in copies:
            copy.wait()

    if with_scale:
        x = tok_ref[...].astype(f32)
        scale = lax.rsqrt(jnp.mean(x * x, axis=-1, keepdims=True) + norm_eps)
        scale_ref[...] = jnp.broadcast_to(scale, scale_ref.shape)
    else:
        scale = scale_in_ref[:, :1]
    projected = mm(tok_ref[...], weight[...]) * scale
    mean_matrix = group_matrix(head_dim, 1.0 / head_dim)
    raw_ref[...] = projected[:, : raw_ref.shape[1]].astype(bf16)
    for slab in range(heads_ref.shape[1] // 128):
        lanes = slice(128 * slab, 128 * slab + 128)
        part = projected[:, lanes]
        if slab < normed_slabs:
            inverse = lax.rsqrt(group_sum(part * part, mean_matrix) + norm_eps)
            part = turn(part * inverse * gain_ref[...], cos_ref, sa_ref, sb_ref)
        heads_ref[:, lanes] = part.astype(bf16)


def project(grid, tokens, pieces, gain, tables, normed, head_dim, scale=None):
    rows, width = tokens.shape
    out_width = pieces[0].shape[-1]
    span = tables[0].shape[0]
    row_block = lambda n: pl.BlockSpec((span, n), lambda i, *_: (i, 0))
    fixed = lambda a: pl.BlockSpec(a.shape, lambda i, *_: (0,) * a.ndim)
    args = [tokens, *pieces, gain, *tables]
    in_specs = [row_block(width)] + [any_spec] * 2 + [fixed(a) for a in (gain, *tables)]
    out_shape = [
        jax.ShapeDtypeStruct((rows, out_width), bf16),
        jax.ShapeDtypeStruct((rows, normed), bf16),
    ]
    out_specs = [row_block(out_width), row_block(normed)]
    if scale is None:
        out_shape.append(jax.ShapeDtypeStruct((rows, 128), f32))
        out_specs.append(row_block(128))
    else:
        args.append(scale)
        in_specs.append(row_block(128))
    return pl.pallas_call(
        functools.partial(project_kernel, grid, normed // 128, head_dim, scale is None),
        grid_spec=pltpu.PrefetchScalarGridSpec(
            num_scalar_prefetch=1,
            grid=(rows // span,),
            in_specs=in_specs,
            out_specs=out_specs,
            scratch_shapes=[
                pltpu.VMEM((width, out_width), bf16),
                pltpu.SemaphoreType.DMA((n_loads(grid),)),
            ],
        ),
        out_shape=out_shape,
        compiler_params=params(1),
        cost_estimate=pl.CostEstimate(
            flops=4 * rows * width * out_width,
            bytes_accessed=2 * (rows * (width + 2 * out_width) + width * out_width),
            transcendentals=rows * normed,
        ),
    )(grid.place, *args)


def placed_pair(slab, parity, low):
    values = slab.astype(f32)
    rolled = pltpu.roll(values, 64, 1)
    here, there = (rolled, values) if parity else (values, rolled)
    return jnp.where(low, here, 0.0), jnp.where(low, 0.0, there)


def block_state(info_ref, seq, base, block, span):
    offset = info_ref[0]
    length = info_ref[1 + seq]
    some = (base >= 0) & (base < jnp.minimum(offset + span, length))
    whole = some & (base + block <= jnp.minimum(offset + 1, length))
    return whole, some & jnp.logical_not(whole)


def allowed(info_ref, seq, base, shape, key_axis, block, span):
    q_pos = info_ref[0] + lax.rem(
        lax.broadcasted_iota(jnp.int32, shape, 1 - key_axis), span
    )
    k_pos = base + lax.rem(lax.broadcasted_iota(jnp.int32, shape, key_axis), block)
    return (k_pos <= q_pos) & (k_pos < info_ref[1 + seq])


def chunk_copies(chunks, buffer, sems, info_ref, seq, n_seqs, slot, span, then, backward=False):
    for i, chunk in enumerate(chunks):
        base = info_ref[1 + n_seqs + i]
        needed = (base >= 0) & (base < jnp.minimum(info_ref[0] + span, info_ref[1 + seq]))
        if backward:
            needed = needed & (info_ref[0] < info_ref[1 + seq])

        @pl.when(needed)
        def _(i=i, chunk=chunk):
            then(pltpu.make_async_copy(chunk.at[seq], buffer.at[slot, i], sems.at[slot, i]))


def fetch_chunks(chunks, buffer, sems, info_ref, span, backward=False):
    seq, n_seqs = pl.program_id(0), pl.num_programs(0)
    slot = lax.rem(seq, 2)
    common = (chunks, buffer, sems, info_ref)

    @pl.when(seq == 0)
    def _():
        chunk_copies(*common, seq, n_seqs, slot, span, lambda c: c.start(), backward)

    @pl.when(seq + 1 < n_seqs)
    def _():
        chunk_copies(*common, seq + 1, n_seqs, 1 - slot, span, lambda c: c.start(), backward)

    chunk_copies(*common, seq, n_seqs, slot, span, lambda c: c.wait(), backward)
    return slot


def stacked_at(ref, head):
    first = head * 256
    return jnp.concatenate(
        [ref[0, :, first : first + 128], ref[0, :, first + 128 : first + 256]], axis=0
    )


def unstack_to(ref, head, value):
    first = head * 256
    span = ref.shape[1]
    ref[0, :, first : first + 128] = value[:span].astype(ref.dtype)
    ref[0, :, first + 128 : first + 256] = value[span:].astype(ref.dtype)


def split_lanes(values):
    lane = lax.rem(lane_iota(values.shape), 64)
    high = values.astype(bf16).astype(f32)
    rest = values - high
    return jnp.where(lane == 0, high, jnp.where(lane == 1, rest, 0.0)).astype(bf16)


def attend_kernel(n, with_acc, finish, info_ref, q_ref, *refs):
    chunks, refs = refs[:n], refs[n:]
    if with_acc:
        acc_in, refs = refs[0], refs[1:]
    if finish:
        out_ref, log_ref, buffer, sems, acc = refs
    else:
        acc_out, buffer, sems, acc = refs
    seq, n_seqs = pl.program_id(0), pl.num_programs(0)
    span = q_ref.shape[1]
    n_heads = q_ref.shape[2] // 256
    slot = fetch_chunks(chunks, buffer, sems, info_ref, span)

    def one_head(head):
        parity = head % 2
        k_lanes = slice(head // 2 * 128, head // 2 * 128 + 128)
        v_lanes = slice((n_heads + head) // 2 * 128, (n_heads + head) // 2 * 128 + 128)
        acc[...] = acc_in[0, head] if with_acc else jnp.zeros(acc.shape, f32)

        @pl.loop(0, n)
        def _(chunk):
            base = info_ref[1 + n_seqs + chunk]
            whole, partly = block_state(info_ref, seq, base, span, span)

            def step(masked):
                low = lane_iota((span, 128)) < 64
                ones_low = jnp.where(low, 1.0, 0.0).astype(bf16)
                ones_high = jnp.where(low, 0.0, 1.0).astype(bf16)
                k0, k1 = placed_pair(buffer[slot, chunk, :, k_lanes], parity, low)
                v0, v1 = placed_pair(buffer[slot, chunk, :, v_lanes], parity, low)
                k_pair = jnp.concatenate([k0, k1], axis=0).astype(bf16)
                v_pair = jnp.concatenate(
                    [
                        jnp.concatenate([v0.astype(bf16), ones_low], axis=1),
                        jnp.concatenate([v1.astype(bf16), ones_high], axis=1),
                    ],
                    axis=0,
                )
                weights = jnp.exp2(mm(stacked_at(q_ref, head), k_pair, NT))
                if masked:
                    ok = allowed(info_ref, seq, base, weights.shape, 1, span, span)
                    weights = jnp.where(ok, weights, 0.0)
                acc[...] += mm(weights.astype(bf16), v_pair)

            @pl.when(whole)
            def _():
                step(False)

            @pl.when(partly)
            def _():
                step(True)

        if finish:
            totals = acc[:, 128:]
            unstack_to(out_ref, head, acc[:, :128] / totals)
            unstack_to(log_ref, head, split_lanes(-jnp.log2(totals)))
        else:
            acc_out[0, head] = acc[...]

    for head in range(n_heads):
        one_head(head)


def attend(info, bases, queries, chunks, acc=None, finish=True):
    seqs, span, width = queries.shape
    n_heads = width // 256
    n = len(chunks)
    q_spec = pl.BlockSpec((1, span, width), lambda b, *_: (b, 0, 0))
    acc_spec = pl.BlockSpec((1, n_heads, 2 * span, 256), lambda b, *_: (b, 0, 0, 0))
    acc_shape = jax.ShapeDtypeStruct((seqs, n_heads, 2 * span, 256), f32)
    args = [queries, *chunks]
    in_specs = [q_spec] + [any_spec] * n
    if acc is not None:
        args.append(acc)
        in_specs.append(acc_spec)
    if finish:
        out_shape = [jax.ShapeDtypeStruct(queries.shape, bf16)] * 2
        out_specs = [q_spec, q_spec]
    else:
        out_shape, out_specs = acc_shape, acc_spec
    return pl.pallas_call(
        functools.partial(attend_kernel, n, acc is not None, finish),
        grid_spec=pltpu.PrefetchScalarGridSpec(
            num_scalar_prefetch=1,
            grid=(seqs,),
            in_specs=in_specs,
            out_specs=out_specs,
            scratch_shapes=[
                pltpu.VMEM((2, n, span, chunks[0].shape[2]), bf16),
                pltpu.SemaphoreType.DMA((2, n)),
                pltpu.VMEM((2 * span, 256), f32),
            ],
        ),
        out_shape=out_shape,
        compiler_params=params(1),
        cost_estimate=pl.CostEstimate(
            flops=4 * 4 * seqs * span * width * span * n,
            bytes_accessed=4 * seqs * (span * width * 3 + n * span * width // 2),
            transcendentals=seqs * span * width // 64 * span * n,
        ),
    )(jnp.concatenate([info, bases]), *args)


def attend_back_kernel(n, with_acc, finish, info_ref, q_ref, do_ref, o_ref, log_ref, *refs):
    chunks, refs = refs[:n], refs[n:]
    if with_acc:
        acc_in, refs = refs[0], refs[1:]
    own_ref, their_ref, dq_ref, buffer, sems, acc, q_wide, do_wide, grads_out = refs
    seq, n_seqs = pl.program_id(0), pl.num_programs(0)
    span = q_ref.shape[1]
    n_heads = q_ref.shape[2] // 256
    alive = info_ref[0] < info_ref[1 + seq]
    slot = fetch_chunks(chunks, buffer, sems, info_ref, span, True)
    grads_out[...] = jnp.zeros(grads_out.shape, grads_out.dtype)

    def one_head(head):
        parity = head % 2
        k_lanes = slice(head // 2 * 128, head // 2 * 128 + 128)
        v_lanes = slice((n_heads + head) // 2 * 128, (n_heads + head) // 2 * 128 + 128)
        acc[...] = acc_in[0, head] if with_acc else jnp.zeros(acc.shape, f32)

        @pl.when(alive)
        def _():
            heads = stacked_at(do_ref, head)
            dots = group_sum(
                heads.astype(f32) * stacked_at(o_ref, head).astype(f32), group_matrix(64, 1.0)
            )
            do_wide[:, :128] = heads
            do_wide[:, 128:] = split_lanes(-dots)
            q_wide[:, :128] = stacked_at(q_ref, head)
            q_wide[:, 128:] = stacked_at(log_ref, head)

            @pl.loop(0, n)
            def _(chunk):
                base = info_ref[1 + n_seqs + chunk]
                whole, partly = block_state(info_ref, seq, base, span, span)

                def step(masked):
                    low = lane_iota((span, 128)) < 64
                    half_lane = lax.rem(lane_iota((span, 128)), 64)
                    pick_low = jnp.where(low & (half_lane < 2), 1.0, 0.0)
                    pick_high = jnp.where(low | (half_lane >= 2), 0.0, 1.0)
                    picks = jnp.concatenate([pick_low, pick_high], axis=0).astype(bf16)
                    k0, k1 = placed_pair(buffer[slot, chunk, :, k_lanes], parity, low)
                    v0, v1 = placed_pair(buffer[slot, chunk, :, v_lanes], parity, low)
                    k_pair = jnp.concatenate([k0, k1], axis=0)
                    k_turned = jnp.transpose(k_pair).astype(bf16)
                    k_wide = jnp.concatenate([k_pair.astype(bf16), picks], axis=1)
                    v_wide = jnp.concatenate(
                        [jnp.concatenate([v0, v1], axis=0).astype(bf16), picks], axis=1
                    )
                    weights = jnp.exp2(mm(k_wide, q_wide[...], NT))
                    if masked:
                        ok = allowed(info_ref, seq, base, weights.shape, 0, span, span)
                        weights = jnp.where(ok, weights, 0.0)
                    grads = (weights * mm(v_wide, do_wide[...], NT)).astype(bf16)
                    both_v = mm(weights.astype(bf16), do_wide[:, :128])
                    both_k = mm(grads, q_wide[:, :128]) * math.log(2.0)
                    acc[...] += mm(k_turned, grads)

                    def joined(pair):
                        total = jnp.where(low, pair[:span] + pltpu.roll(pair[span:], 64, 1), 0.0)
                        return pltpu.roll(total, 64, 1) if parity else total

                    dtype = grads_out.dtype
                    grads_out[chunk, :, k_lanes] += joined(both_k).astype(dtype)
                    grads_out[chunk, :, v_lanes] += joined(both_v).astype(dtype)

                @pl.when(whole)
                def _():
                    step(False)

                @pl.when(partly)
                def _():
                    step(True)

        if finish:
            unstack_to(dq_ref, head, jnp.transpose(acc[...]) * 0.125)
        else:
            dq_ref[0, head] = acc[...]

    for head in range(n_heads):
        one_head(head)
    own_ref[:, 0] = grads_out[: n // 2]
    their_ref[:, 0] = grads_out[n // 2 :]


def attend_back(info, bases, queries, grad_out, out, logs, chunks, acc=None, finish=True):
    seqs, span, width = queries.shape
    n_heads = width // 256
    n = len(chunks)
    q_spec = pl.BlockSpec((1, span, width), lambda b, *_: (b, 0, 0))
    acc_spec = pl.BlockSpec((1, n_heads, 128, 2 * span), lambda b, *_: (b, 0, 0, 0))
    acc_shape = jax.ShapeDtypeStruct((seqs, n_heads, 128, 2 * span), f32)
    args = [queries, grad_out, out, logs, *chunks]
    in_specs = [q_spec] * 4 + [any_spec] * n
    if acc is not None:
        args.append(acc)
        in_specs.append(acc_spec)
    kv_width = chunks[0].shape[2]
    if finish:
        dq_shape, dq_spec = jax.ShapeDtypeStruct(queries.shape, bf16), q_spec
    else:
        dq_shape, dq_spec = acc_shape, acc_spec
    grad_shape = jax.ShapeDtypeStruct((n // 2, seqs, span, kv_width), bf16)
    grad_spec = pl.BlockSpec((n // 2, 1, span, kv_width), lambda b, *_: (0, b, 0, 0))
    return pl.pallas_call(
        functools.partial(attend_back_kernel, n, acc is not None, finish),
        grid_spec=pltpu.PrefetchScalarGridSpec(
            num_scalar_prefetch=1,
            grid=(seqs,),
            in_specs=in_specs,
            out_specs=[grad_spec, grad_spec, dq_spec],
            scratch_shapes=[
                pltpu.VMEM((2, n, span, kv_width), bf16),
                pltpu.SemaphoreType.DMA((2, n)),
                pltpu.VMEM((128, 2 * span), f32),
                pltpu.VMEM((2 * span, 256), bf16),
                pltpu.VMEM((2 * span, 256), bf16),
                pltpu.VMEM((n, span, kv_width), bf16),
            ],
        ),
        out_shape=[grad_shape, grad_shape, dq_shape],
        compiler_params=params(1),
        cost_estimate=pl.CostEstimate(
            flops=10 * 4 * seqs * span * width * span * n,
            bytes_accessed=4 * seqs * (span * width * 4 + span * n * width),
            transcendentals=seqs * span * width // 64 * span * n,
        ),
    )(jnp.concatenate([info, bases]), *args)


def unproject_kernel(
    head_dim,
    info_ref,
    grad_ref,
    raw_ref,
    scale_ref,
    gain_ref,
    cos_ref,
    sa_ref,
    sb_ref,
    out_ref,
    sum_ref,
):
    @pl.when(pl.program_id(0) == 0)
    def _():
        sum_ref[...] = jnp.zeros(sum_ref.shape, f32)

    alive = info_ref[0] < info_ref[1 + pl.program_id(0)]

    @pl.when(jnp.logical_not(alive))
    def _():
        out_ref[...] = jnp.zeros(out_ref.shape, out_ref.dtype)

    @pl.when(alive)
    def _():
        scale = scale_ref[:, :1]
        mean_matrix = group_matrix(head_dim, 1.0 / head_dim)
        normed = raw_ref.shape[1]
        for slab in range(normed // 128):
            lanes = slice(128 * slab, 128 * slab + 128)
            raw = raw_ref[:, lanes].astype(f32)
            inverse = lax.rsqrt(group_sum(raw * raw, mean_matrix) + norm_eps)
            unit = raw * inverse
            turned = turn_back(grad_ref[:, lanes].astype(f32), cos_ref, sa_ref, sb_ref)
            sum_ref[...] += jnp.broadcast_to(
                jnp.sum(turned * unit, axis=0, keepdims=True), sum_ref.shape
            )
            inner = turned * gain_ref[...]
            mean = group_sum(inner * unit, mean_matrix)
            out_ref[:, lanes] = (inverse * (inner - unit * mean) * scale).astype(bf16)
        if normed < grad_ref.shape[1]:
            out_ref[:, normed:] = (grad_ref[:, normed:].astype(f32) * scale).astype(bf16)


def unproject(info, grad, raw, scale, gain, tables, head_dim):
    rows, width = grad.shape
    span = tables[0].shape[0]
    row_block = lambda a: pl.BlockSpec((span, a.shape[1]), lambda i, *_: (i, 0))
    fixed = lambda a: pl.BlockSpec(a.shape, lambda i, *_: (0,) * a.ndim)
    return pl.pallas_call(
        functools.partial(unproject_kernel, head_dim),
        grid_spec=pltpu.PrefetchScalarGridSpec(
            num_scalar_prefetch=1,
            grid=(rows // span,),
            in_specs=[row_block(a) for a in (grad, raw, scale)]
            + [fixed(a) for a in (gain, *tables)],
            out_specs=[row_block(grad), pl.BlockSpec((8, 128), lambda i, *_: (0, 0))],
        ),
        out_shape=[
            jax.ShapeDtypeStruct((rows, width), bf16),
            jax.ShapeDtypeStruct((8, 128), f32),
        ],
        compiler_params=params(1),
        cost_estimate=pl.CostEstimate(
            flops=8 * 128 * rows * width,
            bytes_accessed=6 * rows * width,
            transcendentals=rows * width,
        ),
    )(info, grad, raw, scale, gain, *tables)


def feed_kernel(
    grid,
    span,
    split,
    info_ref,
    place_ref,
    tok_ref,
    heads_ref,
    cot_ref,
    *rest,
):
    pieces, rest = rest[:8], rest[8:]
    out_ref, hidden_ref, mid_ref, dgu_ref, dmid_ref, dheads_ref, *rest = rest
    w_out, w_gu, w_down, out_sems, gu_sems, down_sems = rest
    a, b = split
    out_loads = lambda: loads(grid, place_ref, pieces, w_out, out_sems, (0, a))
    gu_loads = lambda: loads(grid, place_ref, pieces, w_gu, gu_sems, (2 * a, 2 * a + b))
    down_loads = lambda: loads(grid, place_ref, pieces, w_down, down_sems, (a, 2 * a))

    @pl.when(pl.program_id(0) == 0)
    def _():
        load_all(out_loads() + gu_loads() + down_loads())

    rows = tok_ref.shape[0]
    middle = tok_ref[...].astype(f32) + mm(heads_ref[...], w_out[...], NT)
    middle_low = middle.astype(bf16)
    mid_ref[...] = middle_low
    scale = lax.rsqrt(jnp.mean(middle * middle, axis=-1, keepdims=True) + norm_eps)
    gate_up = mm(middle_low, w_gu[...]) * scale
    half = gate_up.shape[1] // 2
    gate, up = gate_up[:, :half], gate_up[:, half:]
    sig = 1.0 / (1.0 + jnp.exp(-gate))
    silu = gate * sig
    hidden = silu * up
    hidden_low = hidden.astype(bf16)
    out_ref[...] = (middle + mm(hidden_low, w_down[...], NT)).astype(bf16)

    first = pl.program_id(0) * (rows // span)
    count = rows // span
    longest = info_ref[1 + first]
    for k in range(1, count):
        longest = jnp.maximum(longest, info_ref[1 + first + k])
    alive = info_ref[0] < longest

    @pl.when(alive)
    def _():
        position = lax.broadcasted_iota(jnp.int32, (span, 1), 0) + info_ref[0]
        valid = jnp.concatenate(
            [(position < info_ref[1 + first + k]).astype(f32) for k in range(count)], axis=0
        )
        hidden_ref[...] = (hidden * valid).astype(bf16)
        cot = cot_ref[...].astype(f32) * valid
        grad_hidden = mm(cot.astype(bf16), w_down[...])
        grad_gate = grad_hidden * up * (sig * (1.0 + gate * (1.0 - sig))) * scale
        grad_up = grad_hidden * silu * scale
        grad_gu = jnp.concatenate([grad_gate.astype(bf16), grad_up.astype(bf16)], axis=1)
        dgu_ref[...] = grad_gu
        back = mm(grad_gu, w_gu[...], NT)
        unit = middle * scale
        grad_mid = cot + back - unit * jnp.mean(back * unit, axis=-1, keepdims=True)
        grad_mid = grad_mid.astype(bf16)
        dmid_ref[...] = grad_mid
        dheads_ref[...] = mm(grad_mid, w_out[...]).astype(bf16)

    @pl.when(jnp.logical_not(alive))
    def _():
        for ref in (hidden_ref, dgu_ref, dmid_ref, dheads_ref):
            ref[...] = jnp.zeros(ref.shape, ref.dtype)


def feed(grid, info, tokens, heads, cotangent, pieces, split, span):
    rows, width = tokens.shape
    a, b = split
    tile = max(span, min(256, rows))
    block = lambda n: pl.BlockSpec((tile, n), lambda i, *_: (i, 0))
    shape = lambda n: jax.ShapeDtypeStruct((rows, n), bf16)
    n = n_loads(grid)
    outs = (width, a, width, b, width, a)
    macs = width * (2 * a + b)
    return pl.pallas_call(
        functools.partial(feed_kernel, grid, span, split),
        grid_spec=pltpu.PrefetchScalarGridSpec(
            num_scalar_prefetch=2,
            grid=(rows // tile,),
            in_specs=[block(width), block(a), block(width)] + [any_spec] * 8,
            out_specs=[block(n) for n in outs],
            scratch_shapes=[
                pltpu.VMEM((width, a), bf16),
                pltpu.VMEM((width, b), bf16),
                pltpu.VMEM((width, a), bf16),
                pltpu.SemaphoreType.DMA((n,)),
                pltpu.SemaphoreType.DMA((n,)),
                pltpu.SemaphoreType.DMA((n,)),
            ],
        ),
        out_shape=[shape(n) for n in outs],
        compiler_params=params(1),
        cost_estimate=pl.CostEstimate(
            flops=6 * rows * macs,
            bytes_accessed=2 * (rows * (sum(outs) + 2 * width + a) + macs),
            transcendentals=rows * a,
        ),
    )(info, grid.place, tokens, heads, cotangent, *pieces)


def load_all(copies):
    for copy in copies:
        copy.start()
    for copy in copies:
        copy.wait()


def query_back_kernel(grid, info_ref, place_ref, grad_ref, *rest):
    pieces, (out_ref, weight, sems) = rest[:2], rest[2:]

    @pl.when(pl.program_id(0) == 0)
    def _():
        load_all(loads(grid, place_ref, pieces, weight, sems))

    @pl.when(info_ref[0] < info_ref[1 + pl.program_id(0)])
    def _():
        out_ref[...] = mm(grad_ref[...], weight[...], NT)


def query_back(grid, info, grad, pieces, width, span):
    rows, inner = grad.shape
    return pl.pallas_call(
        functools.partial(query_back_kernel, grid),
        grid_spec=pltpu.PrefetchScalarGridSpec(
            num_scalar_prefetch=2,
            grid=(rows // span,),
            in_specs=[pl.BlockSpec((span, inner), lambda i, *_: (i, 0))] + [any_spec] * 2,
            out_specs=pl.BlockSpec((span, width), lambda i, *_: (i, 0)),
            scratch_shapes=[
                pltpu.VMEM((width, inner), bf16),
                pltpu.SemaphoreType.DMA((n_loads(grid),)),
            ],
        ),
        out_shape=jax.ShapeDtypeStruct((rows, width), f32),
        compiler_params=params(1),
        cost_estimate=pl.CostEstimate(
            flops=2 * rows * width * inner,
            bytes_accessed=2 * (rows * (2 * width + inner) + width * inner),
            transcendentals=0,
        ),
    )(info, grid.place, grad, *pieces)


def last_kernel(grid, info_ref, place_ref, tok_ref, grad_ref, back_ref, dmid_ref, scale_ref, *rest):
    pieces, (out_ref, weight, sems) = rest[:2], rest[2:]

    @pl.when(pl.program_id(0) == 0)
    def _():
        load_all(loads(grid, place_ref, pieces, weight, sems))

    alive = info_ref[0] < info_ref[1 + pl.program_id(0)]

    @pl.when(alive)
    def _():
        back = back_ref[...] + mm(grad_ref[...], weight[...], NT)
        unit = tok_ref[...].astype(f32) * scale_ref[:, :1]
        grad = dmid_ref[...].astype(f32) + back
        grad = grad - unit * jnp.mean(back * unit, axis=-1, keepdims=True)
        out_ref[...] = grad.astype(bf16)

    @pl.when(jnp.logical_not(alive))
    def _():
        out_ref[...] = jnp.zeros(out_ref.shape, out_ref.dtype)


def last(grid, info, tokens, grad_kv, back, grad_mid, scale, pieces, span):
    rows, width = tokens.shape
    block = lambda a: pl.BlockSpec((span, a.shape[1]), lambda i, *_: (i, 0))
    inner = grad_kv.shape[1]
    args = (tokens, grad_kv, back, grad_mid, scale)
    return pl.pallas_call(
        functools.partial(last_kernel, grid),
        grid_spec=pltpu.PrefetchScalarGridSpec(
            num_scalar_prefetch=2,
            grid=(rows // span,),
            in_specs=[block(a) for a in args] + [any_spec] * 2,
            out_specs=block(tokens),
            scratch_shapes=[
                pltpu.VMEM((width, inner), bf16),
                pltpu.SemaphoreType.DMA((n_loads(grid),)),
            ],
        ),
        out_shape=jax.ShapeDtypeStruct(tokens.shape, bf16),
        compiler_params=params(1),
        cost_estimate=pl.CostEstimate(
            flops=2 * rows * width * inner,
            bytes_accessed=2 * (rows * (5 * width + inner) + width * inner),
            transcendentals=0,
        ),
    )(info, grid.place, *args, *pieces)


def weight_kernel(grid, shard, span, n_pairs, place_ref, info_ref, *refs):
    lefts, rights = refs[:n_pairs], refs[n_pairs : 2 * n_pairs]
    mine_ref, theirs_ref, acc = refs[2 * n_pairs :]
    core = place_ref[2]
    middle = grid.depth // 2
    n_seqs = lefts[0].shape[0] // span
    shortest = info_ref[1]
    for seq in range(1, n_seqs):
        shortest = jnp.minimum(shortest, info_ref[1 + seq])
    all_alive = info_ref[0] < shortest
    column = 0
    for left, right in zip(lefts, rights):
        width = right.shape[1]

        @pl.when(all_alive)
        def _(left=left, right=right, width=width):
            acc[:, :width] = mm(left[...], right[...], TN)

        @pl.when(jnp.logical_not(all_alive))
        def _(left=left, right=right, width=width):
            acc[:, :width] = jnp.zeros((acc.shape[0], width), f32)
            for seq in range(n_seqs):
                rows = slice(seq * span, (seq + 1) * span)

                @pl.when(info_ref[0] < info_ref[1 + seq])
                def _(rows=rows):
                    acc[:, :width] += mm(left[rows, :], right[rows, :], TN)

        for level in range(grid.depth):
            half, at = level // middle, level % middle
            for whose, ref in ((core, mine_ref), (1 - core, theirs_ref)):
                start = pl.multiple_of((level * 2 + whose) * shard, shard)
                ref[half, 0, at, :, column : column + width] = acc[
                    pl.ds(start, shard), :width
                ].astype(bf16)
        column += width


def weight_grad(grid, info, span, *pairs):
    lefts, rights = [p[0] for p in pairs], [p[1] for p in pairs]
    rows, features = lefts[0].shape
    widths = [r.shape[1] for r in rights]
    total = sum(widths)
    part = features // grid.rows
    shard = part // grid.seqs
    middle = grid.depth // 2
    shape = jax.ShapeDtypeStruct((2, grid.rows, middle, shard, total), bf16)
    piece = pl.BlockSpec((2, 1, middle, shard, total), lambda i, *_: (0, i, 0, 0, 0))
    return pl.pallas_call(
        functools.partial(weight_kernel, grid, shard, span, len(pairs)),
        grid_spec=pltpu.PrefetchScalarGridSpec(
            num_scalar_prefetch=2,
            grid=(grid.rows,),
            in_specs=[pl.BlockSpec((rows, part), lambda i, place, info: (0, place[0] ^ i))]
            * len(pairs)
            + [pl.BlockSpec(r.shape, lambda i, *_: (0, 0)) for r in rights],
            out_specs=[piece, piece],
            scratch_shapes=[pltpu.VMEM((part, max(widths)), f32)],
        ),
        out_shape=[shape, shape],
        compiler_params=params(1),
        cost_estimate=pl.CostEstimate(
            flops=2 * rows * features * total,
            bytes_accessed=2 * (rows * (features * len(pairs) + total) + features * total),
            transcendentals=0,
        ),
    )(grid.place, info, *lefts, *rights)


def shards(
    n_rows,
    n_seqs,
    tokens,
    lengths,
    cotangent,
    w_qkv,
    w_out,
    w_gateup,
    w_down,
    norm_attn,
    norm_ffn,
    q_gain,
    k_gain,
):
    grid = Grid(n_rows, n_seqs)
    seq_count, span_len, model_width = tokens.shape
    row_count = seq_count * span_len
    head_dim = q_gain.shape[0]
    half_dim = head_dim // 2
    query_width = w_out.shape[1]
    kv_width = (w_qkv.shape[1] - query_width) // 2
    log2_scale = math.log2(math.e) * head_dim ** (-0.5)

    offset = (grid.seq * span_len).astype(jnp.int32)
    positions = offset + jnp.arange(span_len, dtype=jnp.int32)
    inverse = theta_base ** (-jnp.arange(half_dim, dtype=f32) * 2.0 / head_dim)
    angles = positions.astype(f32)[:, None] * inverse[None, :]
    cosine, sine = jnp.cos(angles), jnp.sin(angles)
    nothing = jnp.zeros_like(sine)
    tables = (
        jnp.concatenate([cosine] * 4, axis=1),
        jnp.concatenate([-sine, nothing] * 2, axis=1),
        jnp.concatenate([nothing, sine] * 2, axis=1),
    )
    q_gain_f = jnp.concatenate([q_gain.astype(f32)] * 2)[None, :]
    k_gain_f = jnp.concatenate([k_gain.astype(f32)] * 2)[None, :]
    info = jnp.concatenate([offset[None], lengths])

    attn_gain = norm_attn.astype(f32)[:, None]
    ffn_gain = norm_ffn.astype(f32)[:, None]
    qkv_shard = (w_qkv.astype(f32) * attn_gain).astype(bf16)
    gateup_shard = (w_gateup.astype(f32) * ffn_gain).astype(bf16)

    order = Order()
    depth = grid.depth
    split = max(1, depth // 2)
    kv_steps = grid.ring(qkv_shard[:, query_width:])
    kv_own, kv_came = grid.spread(kv_steps)
    q_steps = grid.ring(qkv_shard[:, :query_width], [[kv_steps[1]], [kv_steps[-1]]])[:3]
    feed_steps = grid.ring(
        jnp.concatenate([w_out, w_down, gateup_shard], axis=1), [[kv_steps[2]], kv_came[-1]]
    )[:3]
    kv_pieces = grid.with_partner(kv_own, feed_steps[1], q_steps[1])

    rows_in = tokens.reshape(row_count, model_width)
    kv, k_raw, scale1 = project(grid, rows_in, kv_pieces, k_gain_f, tables, kv_width, head_dim)
    order.leave(kv)
    while len(feed_steps) < depth:
        feed_steps.append(grid.around(after(feed_steps[-1], kv)))
        q_steps.append(grid.around(after(q_steps[-1], kv)))
    q_own, q_came = grid.spread(q_steps, [[kv]] + [feed_steps[2:3]] * (len(grid.orders[0]) - 1))
    feed_own, feed_came = grid.spread(feed_steps, [q_came[-1]])
    kv = kv.reshape(seq_count, span_len, 2 * kv_width)
    reach = [kv]
    for _ in range(1, depth - 1):
        reach.append(grid.up(reach[-1]))
    q_pieces = grid.with_partner(q_own, reach[1], feed_steps[-1])
    q, q_raw = project(
        grid,
        order.enter(rows_in),
        q_pieces,
        q_gain_f * log2_scale,
        tables,
        query_width,
        head_dim,
        scale1,
    )
    order.leave(q)
    q = q.reshape(seq_count, span_len, query_width)
    bases = []
    for step in range(depth):
        level = grid.level - step
        start = jnp.stack([level * 2 + grid.core, level * 2 + 1 - grid.core]) * span_len
        bases.append(jnp.where(level >= 0, start, -1).astype(jnp.int32))
    reach[-1] = order.late(reach[-1])
    reach.append(grid.up(reach[-1]))
    crossed = [grid.partner(own) for own in reach[:-1]]
    order.pin(*feed_came[0])
    feed_held = [grid.partner(order.late(feed_own[k])) for k in (0, 2)]
    near = [c for pair in zip(reach[:-1], crossed) for c in pair]
    acc = attend(info, jnp.concatenate(bases[:-1]), order.enter(q), near, None, False)
    order.leave(acc)
    order.pin(*feed_came[-1], *feed_held)
    feed_found = [grid.partner(order.late(feed_own[k])) for k in (1, 3)]
    reach[-1] = order.late(reach[-1])
    crossed.append(grid.partner(reach[-1]))
    heads, logs = attend(
        info, bases[-1], order.enter(q), [reach[-1], crossed[-1]], acc, True
    )
    order.leave(heads)
    attended = heads.reshape(row_count, query_width)
    feed_pieces = feed_own + [feed_held[0], feed_found[0], feed_held[1], feed_found[1]]

    flat_cot = cotangent.reshape(row_count, model_width)
    output, hidden, middle, grad_gu, grad_mid, grad_heads = feed(
        grid,
        info,
        rows_in,
        attended,
        flat_cot,
        feed_pieces,
        (query_width, w_gateup.shape[1]),
        span_len,
    )
    order.leave(hidden)
    grad_heads = grad_heads.reshape(seq_count, span_len, query_width)

    def advance(*sums):
        for each in sums:
            order.pin(*each.land())
            order.pin(*each.go())

    kv_flight = []

    def kv_sum_here(own, other):
        kv_flight[:] = [order.late(came) for came in kv_flight]
        here = own.astype(f32) + other.astype(f32)
        for came in kv_flight:
            here = here + came.astype(f32)
        return here.astype(bf16)

    def kv_hop(own, other):
        sent = order.late(kv_sum_here(own, other))
        order.pin(sent)
        kv_flight[:] = [grid.down(sent)]

    def back(steps, acc, final):
        chosen = [reach[k] for k in steps] + [crossed[k] for k in steps]
        starts = jnp.stack([bases[k] for k in steps], axis=1).reshape(-1)
        return attend_back(
            info, starts, order.enter(q), grad_heads, heads, logs, chosen, acc, final
        )

    feed_sum = Sum(
        grid,
        order,
        weight_grad(
            grid, info, span_len, (flat_cot, order.enter(hidden)), (middle, grad_gu)
        ),
    )
    order.leave(feed_sum.theirs)
    advance(feed_sum)
    far_own, far_theirs, acc_q = back(range(split, depth), None, False)
    order.leave(acc_q)
    far_came = grid.partner(far_theirs)
    kv_hop(far_own[-1], far_came[-1])
    advance(feed_sum)
    near_own, near_theirs, grad_q = back(range(split), acc_q, True)
    order.leave(grad_q)
    near_came = grid.partner(order.late(near_theirs))
    for step in reversed(range(split, depth - 1)):
        kv_hop(far_own[step - split], far_came[step - split])
    advance(feed_sum)
    grad_pq, gq = unproject(
        info,
        order.enter(grad_q.reshape(row_count, query_width)),
        q_raw,
        scale1,
        q_gain_f,
        tables,
        head_dim,
    )
    order.leave(grad_pq)
    square_sum = Sum(
        grid,
        order,
        weight_grad(
            grid, info, span_len, (rows_in, order.enter(grad_pq)), (grad_mid, attended)
        ),
    )
    order.leave(square_sum.theirs)
    for step in reversed(range(1, split)):
        kv_hop(near_own[step], near_came[step])
    advance(feed_sum, square_sum)
    back_q = query_back(grid, info, order.enter(grad_pq), q_pieces, model_width, span_len)
    order.leave(back_q)
    advance(feed_sum, square_sum)
    grad_kv = kv_sum_here(near_own[0], near_came[0]).reshape(row_count, 2 * kv_width)
    grad_pkv, gk = unproject(
        info, order.enter(grad_kv), k_raw, scale1, k_gain_f, tables, head_dim
    )
    kv_sum = Sum(grid, order, weight_grad(grid, info, span_len, (rows_in, grad_pkv)), True)
    order.leave(kv_sum.theirs)
    gain_sum = Everywhere(grid, order, jnp.concatenate([gq[:1], gk[:1]], axis=0))
    advance(feed_sum, square_sum, kv_sum, gain_sum)
    grad_tokens = last(
        grid,
        info,
        rows_in,
        order.enter(grad_pkv),
        back_q,
        grad_mid,
        scale1,
        kv_pieces,
        span_len,
    )
    order.leave(grad_tokens)
    gains = gain_sum.finish()
    gains = gains[:, :head_dim] + gains[:, head_dim:]
    kv_total, square_total, feed_total = kv_sum.finish(), square_sum.finish(), feed_sum.finish()
    sum_qkv = jnp.concatenate([square_total[:, :query_width], kv_total], axis=1)
    sum_out = square_total[:, query_width:]
    sum_down, sum_gateup = feed_total[:, :query_width], feed_total[:, query_width:]
    return (
        output.reshape(tokens.shape),
        grad_tokens.reshape(tokens.shape),
        sum_qkv * attn_gain,
        sum_out,
        sum_gateup * ffn_gain,
        sum_down,
        jnp.sum(sum_qkv * w_qkv.astype(f32), axis=1),
        jnp.sum(sum_gateup * w_gateup.astype(f32), axis=1),
        gains[0],
        gains[1],
    )


def solution(mesh):
    rows = P("row", "seq", None)
    weight = P(both, None)
    vector = P(both)
    return jax.shard_map(
        functools.partial(shards, mesh.shape["row"], mesh.shape["seq"]),
        mesh=mesh,
        in_specs=(rows, P("row"), rows, weight, weight, weight, weight, vector, vector, P(), P()),
        out_specs=(rows, rows, weight, weight, weight, weight, vector, vector, P(), P()),
        check_vma=False,
    )
```

```python
import functools
import math

import jax
import jax.numpy as jnp
from jax import lax
from jax.experimental import pallas as pl
from jax.experimental.pallas import tpu as pltpu
from jax.sharding import PartitionSpec as P

norm_eps = 1e-06
theta_base = 10000.0
both = ("row", "seq")
f32 = jnp.float32
bf16 = jnp.bfloat16
vmem_cap = 56 * 1024 * 1024
any_spec = pl.BlockSpec(memory_space=pl.ANY)
NN = (((1,), (0,)), ((), ()))
NT = (((1,), (1,)), ((), ()))
TN = (((0,), (0,)), ((), ()))


def mm(left, right, dims=NN):
    return lax.dot_general(left, right, dims, preferred_element_type=f32)


def after(value, *earlier):
    return lax.optimization_barrier((value, *earlier))[0]


def params(n_grid):
    return pltpu.CompilerParams(
        dimension_semantics=("arbitrary",) * n_grid, vmem_limit_bytes=vmem_cap
    )


def lane_iota(shape):
    return lax.broadcasted_iota(jnp.int32, shape, len(shape) - 1)


def group_matrix(head_dim, value):
    i = lax.broadcasted_iota(jnp.int32, (128, 128), 0) // head_dim
    j = lax.broadcasted_iota(jnp.int32, (128, 128), 1) // head_dim
    return jnp.where(i == j, value, 0.0).astype(bf16)


def group_sum(values, matrix):
    high = values.astype(bf16)
    low = (values - high.astype(f32)).astype(bf16)
    return mm(high, matrix) + mm(low, matrix)


def turn(values, cos_ref, sa_ref, sb_ref):
    return (
        values * cos_ref[...]
        + pltpu.roll(values, 96, 1) * sa_ref[...]
        + pltpu.roll(values, 32, 1) * sb_ref[...]
    )


def turn_back(values, cos_ref, sa_ref, sb_ref):
    return (
        values * cos_ref[...]
        - pltpu.roll(values, 96, 1) * sa_ref[...]
        - pltpu.roll(values, 32, 1) * sb_ref[...]
    )


class Grid:
    def __init__(self, rows, seqs):
        self.rows, self.seqs, self.depth = rows, seqs, seqs // 2
        self.row = lax.axis_index("row")
        seq = lax.axis_index("seq")
        self.level, self.core = seq // 2, lax.rem(seq, 2)
        self.seq = seq
        bits = [1 << k for k in range(rows.bit_length() - 1)]
        self.orders = (bits, bits[::-1])
        self.place = jnp.stack([self.row, self.level, self.core]).astype(jnp.int32)

    def move(self, value, where):
        pairs = []
        for row in range(self.rows):
            for seq in range(self.seqs):
                target = where(row, seq)
                if target is not None:
                    pairs.append((row * self.seqs + seq, target[0] * self.seqs + target[1]))
        return lax.ppermute(value, both, pairs)

    def across(self, value, mask):
        return self.move(value, lambda r, s: (r ^ mask, s))

    def partner(self, value):
        return self.move(value, lambda r, s: (r, s ^ 1))

    def around(self, value, steps=1):
        return self.move(value, lambda r, s: (r, (s + 2 * steps) % self.seqs))

    def up(self, value):
        return self.move(value, lambda r, s: (r, s + 2) if s + 2 < self.seqs else None)

    def down(self, value):
        return self.move(value, lambda r, s: (r, s - 2) if s >= 2 else None)

    def masks(self, half):
        found = [0]
        for bit in self.orders[half]:
            found = found + [m ^ bit for m in found]
        return found

    def ring(self, shard, waits=()):
        steps = [shard]
        for hop in range(self.depth - 1):
            held = steps[-1]
            if hop < len(waits):
                held = after(held, *waits[hop])
            steps.append(self.around(held))
        return steps

    def spread(self, steps, waits=()):
        middle = self.depth // 2
        held = [jnp.stack(steps[:middle])[None], jnp.stack(steps[middle:])[None]]
        pieces = []
        arrived = []
        for stage in range(len(self.orders[0])):
            for half in range(2):
                if stage < len(waits):
                    held[half] = after(held[half], *waits[stage])
            found = [self.across(held[half], self.orders[half][stage]) for half in range(2)]
            arrived.append(found)
            if stage == len(self.orders[0]) - 1:
                pieces = [held[0], found[0], held[1], found[1]]
            else:
                held = [jnp.concatenate([held[k], found[k]], axis=0) for k in range(2)]
        return pieces, arrived

    def with_partner(self, pieces, *waits):
        pieces = jnp.stack(pieces)
        return [pieces, self.partner(after(pieces, *waits) if waits else pieces)]


class Order:
    def __init__(self):
        self.kernel = None
        self.waits = []

    def pin(self, *values):
        self.waits += values

    def enter(self, value):
        return after(value, *self.waits) if self.waits else value

    def leave(self, value):
        self.kernel = value
        self.waits = [value]

    def late(self, value):
        return after(value, self.kernel)


class Everywhere:
    def __init__(self, grid, order, value):
        self.grid, self.order, self.total = grid, order, value
        self.flight = []
        self.moves = [(bit, 0) for bit in grid.orders[0]]
        self.moves += [(0, 1 << k) for k in range(grid.seqs.bit_length() - 1)]

    def land(self):
        came, self.flight = [self.order.late(c) for c in self.flight], []
        for each in came:
            self.total = self.total + each
        return came

    def go(self):
        self.land()
        if not self.moves:
            return []
        row, seq = self.moves.pop(0)
        sent = self.order.late(self.total)
        self.flight = [self.grid.move(sent, lambda r, s: (r ^ row, s ^ seq))]
        return [sent]

    def finish(self):
        while self.go():
            pass
        return self.total


class Sum:
    def __init__(self, grid, order, parts, direct=False):
        mine, self.theirs = parts
        self.direct = direct
        self.grid = grid
        self.order = order
        self.halves = [[mine[half]] for half in range(2)]
        self.stage = 0
        self.flight = []
        self.row_stages = len(grid.orders[0])
        self.total = None

    def at(self, step):
        depth = self.grid.depth
        index = lax.rem(self.grid.level - step + 2 * depth, depth)
        return lax.dynamic_index_in_dim(self.levels, index, 0, keepdims=False)

    def land(self):
        came, self.flight = [self.order.late(c) for c in self.flight], []
        if came:
            if self.stage == 1:
                for half in range(2):
                    self.halves[half].append(came[0][half])
            elif self.stage <= 1 + self.row_stages:
                for half in range(2):
                    self.halves[half].append(came[half])
            elif self.direct:
                self.total = self.total + sum(c.astype(f32) for c in came)
            else:
                self.total = came[0].astype(f32) + self.at(self.stage - self.row_stages)
        return came

    def go(self):
        grid, late = self.grid, self.order.late
        self.land()
        if self.stage == 0:
            sent = [self.theirs]
            self.flight = [grid.partner(self.theirs)]
        elif self.stage <= self.row_stages:
            sent = []
            for half in range(2):
                parts = self.halves[half]
                bit = grid.orders[half][::-1][self.stage - 1]
                count = parts[0].shape[0] // 2
                if half == 0:
                    kept, given = slice(0, count), slice(count, None)
                else:
                    kept, given = slice(0, None, 2), slice(1, None, 2)
                value = sum(p[given].astype(f32) for p in parts).astype(bf16)
                self.halves[half] = [p[kept] for p in parts]
                sent.append(late(value))
                self.flight.append(grid.across(sent[half], bit))
        elif self.direct:
            if self.total is not None:
                return []
            self.levels = jnp.concatenate(
                [sum(p[0].astype(f32) for p in parts) for parts in self.halves], axis=0
            )
            self.total = self.at(0)
            sent = [
                late(self.at(grid.depth - step).astype(bf16)) for step in range(1, grid.depth)
            ]
            self.flight = [grid.around(each, k + 1) for k, each in enumerate(sent)]
        elif self.stage < self.row_stages + grid.depth:
            if self.total is None:
                self.levels = jnp.concatenate(
                    [sum(p[0].astype(f32) for p in parts) for parts in self.halves], axis=0
                )
                self.total = self.at(1)
            sent = [late(self.total.astype(bf16))]
            self.flight = [grid.around(sent[0])]
        else:
            return []
        self.stage += 1
        return sent

    def finish(self):
        while self.go():
            pass
        return self.total


def loads(grid, place_ref, pieces, target, sems, columns=None, at_column=0):
    row, level, core = place_ref[0], place_ref[1], place_ref[2]
    shard, columns_all = pieces[0].shape[-2:]
    if columns is None:
        columns = (0, columns_all)
    width = columns[1] - columns[0]
    merged = len(pieces) == 2
    copies = []
    for which in range(8):
        ref = pieces[which // 4].at[which % 4] if merged else pieces[which]
        half = which // 2 % 2
        whose = core if which < 4 else 1 - core
        first = 0 if half == 0 else grid.depth // 2
        masks = grid.masks(half)
        masks = masks[len(masks) // 2 :] if which % 2 else masks[: len(masks) // 2]
        for m, mask in enumerate(masks):
            for h in range(ref.shape[1]):
                at_level = lax.rem(level - (first + h) + grid.depth, grid.depth)
                start = ((row ^ mask) * grid.seqs + at_level * 2 + whose) * shard
                copies.append(
                    pltpu.make_async_copy(
                        ref.at[m, h, :, columns[0] : columns[1]],
                        target.at[
                            pl.ds(pl.multiple_of(start, shard), shard),
                            at_column : at_column + width,
                        ],
                        sems.at[len(copies)],
                    )
                )
    return copies


def n_loads(grid):
    return grid.rows * grid.seqs


def project_kernel(grid, normed_slabs, head_dim, with_scale, place_ref, tok_ref, *rest):
    pieces, rest = rest[:2], rest[2:]
    gain_ref, cos_ref, sa_ref, sb_ref, *rest = rest
    if with_scale:
        heads_ref, raw_ref, scale_ref, weight, sems = rest
    else:
        scale_in_ref, heads_ref, raw_ref, weight, sems = rest

    @pl.when(pl.program_id(0) == 0)
    def _():
        copies = loads(grid, place_ref, pieces, weight, sems)
        for copy in copies:
            copy.start()
        for copy in copies:
            copy.wait()

    if with_scale:
        x = tok_ref[...].astype(f32)
        scale = lax.rsqrt(jnp.mean(x * x, axis=-1, keepdims=True) + norm_eps)
        scale_ref[...] = jnp.broadcast_to(scale, scale_ref.shape)
    else:
        scale = scale_in_ref[:, :1]
    projected = mm(tok_ref[...], weight[...]) * scale
    mean_matrix = group_matrix(head_dim, 1.0 / head_dim)
    raw_ref[...] = projected[:, : raw_ref.shape[1]].astype(bf16)
    for slab in range(heads_ref.shape[1] // 128):
        lanes = slice(128 * slab, 128 * slab + 128)
        part = projected[:, lanes]
        if slab < normed_slabs:
            inverse = lax.rsqrt(group_sum(part * part, mean_matrix) + norm_eps)
            part = turn(part * inverse * gain_ref[...], cos_ref, sa_ref, sb_ref)
        heads_ref[:, lanes] = part.astype(bf16)


def project(grid, tokens, pieces, gain, tables, normed, head_dim, scale=None):
    rows, width = tokens.shape
    out_width = pieces[0].shape[-1]
    span = tables[0].shape[0]
    row_block = lambda n: pl.BlockSpec((span, n), lambda i, *_: (i, 0))
    fixed = lambda a: pl.BlockSpec(a.shape, lambda i, *_: (0,) * a.ndim)
    args = [tokens, *pieces, gain, *tables]
    in_specs = [row_block(width)] + [any_spec] * 2 + [fixed(a) for a in (gain, *tables)]
    out_shape = [
        jax.ShapeDtypeStruct((rows, out_width), bf16),
        jax.ShapeDtypeStruct((rows, normed), bf16),
    ]
    out_specs = [row_block(out_width), row_block(normed)]
    if scale is None:
        out_shape.append(jax.ShapeDtypeStruct((rows, 128), f32))
        out_specs.append(row_block(128))
    else:
        args.append(scale)
        in_specs.append(row_block(128))
    return pl.pallas_call(
        functools.partial(project_kernel, grid, normed // 128, head_dim, scale is None),
        grid_spec=pltpu.PrefetchScalarGridSpec(
            num_scalar_prefetch=1,
            grid=(rows // span,),
            in_specs=in_specs,
            out_specs=out_specs,
            scratch_shapes=[
                pltpu.VMEM((width, out_width), bf16),
                pltpu.SemaphoreType.DMA((n_loads(grid),)),
            ],
        ),
        out_shape=out_shape,
        compiler_params=params(1),
        cost_estimate=pl.CostEstimate(
            flops=4 * rows * width * out_width,
            bytes_accessed=2 * (rows * (width + 2 * out_width) + width * out_width),
            transcendentals=rows * normed,
        ),
    )(grid.place, *args)


def placed_pair(slab, parity, low):
    values = slab.astype(f32)
    rolled = pltpu.roll(values, 64, 1)
    here, there = (rolled, values) if parity else (values, rolled)
    return jnp.where(low, here, 0.0), jnp.where(low, 0.0, there)


def block_state(info_ref, seq, base, block, span):
    offset = info_ref[0]
    length = info_ref[1 + seq]
    some = (base >= 0) & (base < jnp.minimum(offset + span, length))
    whole = some & (base + block <= jnp.minimum(offset + 1, length))
    return whole, some & jnp.logical_not(whole)


def mask_bias(info_ref, seq, base, span, key_axis):
    shape = (span, span)
    behind = lax.broadcasted_iota(jnp.int32, shape, key_axis) - lax.broadcasted_iota(
        jnp.int32, shape, 1 - key_axis
    )
    key = lax.broadcasted_iota(jnp.int32, shape, key_axis)
    ok = (behind <= info_ref[0] - base) & (key < info_ref[1 + seq] - base)
    bias = jnp.where(ok, 0.0, -1e30)
    pair = jnp.concatenate([bias, bias], axis=1)
    return jnp.concatenate([pair, pair], axis=0)


def chunk_copies(chunks, buffer, sems, info_ref, seq, n_seqs, slot, span, then, backward=False):
    for i, chunk in enumerate(chunks):
        base = info_ref[1 + n_seqs + i]
        needed = (base >= 0) & (base < jnp.minimum(info_ref[0] + span, info_ref[1 + seq]))
        if backward:
            needed = needed & (info_ref[0] < info_ref[1 + seq])

        @pl.when(needed)
        def _(i=i, chunk=chunk):
            then(pltpu.make_async_copy(chunk.at[seq], buffer.at[slot, i], sems.at[slot, i]))


def fetch_chunks(chunks, buffer, sems, info_ref, span, backward=False):
    seq, n_seqs = pl.program_id(0), pl.num_programs(0)
    slot = lax.rem(seq, 2)
    common = (chunks, buffer, sems, info_ref)

    @pl.when(seq == 0)
    def _():
        chunk_copies(*common, seq, n_seqs, slot, span, lambda c: c.start(), backward)

    @pl.when(seq + 1 < n_seqs)
    def _():
        chunk_copies(*common, seq + 1, n_seqs, 1 - slot, span, lambda c: c.start(), backward)

    chunk_copies(*common, seq, n_seqs, slot, span, lambda c: c.wait(), backward)
    return slot


def stacked_at(ref, head):
    first = head * 256
    return jnp.concatenate(
        [ref[0, :, first : first + 128], ref[0, :, first + 128 : first + 256]], axis=0
    )


def unstack_to(ref, head, value):
    first = head * 256
    span = ref.shape[1]
    ref[0, :, first : first + 128] = value[:span].astype(ref.dtype)
    ref[0, :, first + 128 : first + 256] = value[span:].astype(ref.dtype)


def split_lanes(values):
    lane = lax.rem(lane_iota(values.shape), 64)
    high = values.astype(bf16).astype(f32)
    rest = values - high
    return jnp.where(lane == 0, high, jnp.where(lane == 1, rest, 0.0)).astype(bf16)


def attend_kernel(n, with_acc, finish, info_ref, q_ref, *refs):
    chunks, refs = refs[:n], refs[n:]
    if with_acc:
        acc_in, refs = refs[0], refs[1:]
    if finish:
        out_ref, log_ref, buffer, sems, acc = refs
    else:
        acc_out, buffer, sems, acc = refs
    seq, n_seqs = pl.program_id(0), pl.num_programs(0)
    span = q_ref.shape[1]
    n_heads = q_ref.shape[2] // 256
    slot = fetch_chunks(chunks, buffer, sems, info_ref, span)

    def one_head(head):
        parity = head % 2
        k_lanes = slice(head // 2 * 128, head // 2 * 128 + 128)
        v_lanes = slice((n_heads + head) // 2 * 128, (n_heads + head) // 2 * 128 + 128)
        acc[...] = acc_in[0, head] if with_acc else jnp.zeros(acc.shape, f32)

        @pl.loop(0, n)
        def _(chunk):
            base = info_ref[1 + n_seqs + chunk]
            whole, partly = block_state(info_ref, seq, base, span, span)

            def step(masked):
                low = lane_iota((span, 128)) < 64
                ones_low = jnp.where(low, 1.0, 0.0).astype(bf16)
                ones_high = jnp.where(low, 0.0, 1.0).astype(bf16)
                k0, k1 = placed_pair(buffer[slot, chunk, :, k_lanes], parity, low)
                v0, v1 = placed_pair(buffer[slot, chunk, :, v_lanes], parity, low)
                k_pair = jnp.concatenate([k0, k1], axis=0).astype(bf16)
                v_pair = jnp.concatenate(
                    [
                        jnp.concatenate([v0.astype(bf16), ones_low], axis=1),
                        jnp.concatenate([v1.astype(bf16), ones_high], axis=1),
                    ],
                    axis=0,
                )
                scores = mm(stacked_at(q_ref, head), k_pair, NT)
                if masked:
                    scores = scores + mask_bias(info_ref, seq, base, span, 1)
                weights = jnp.exp2(scores)
                acc[...] += mm(weights.astype(bf16), v_pair)

            @pl.when(whole)
            def _():
                step(False)

            @pl.when(partly)
            def _():
                step(True)

        if finish:
            totals = acc[:, 128:]
            unstack_to(out_ref, head, acc[:, :128] / totals)
            unstack_to(log_ref, head, split_lanes(-jnp.log2(totals)))
        else:
            acc_out[0, head] = acc[...]

    for head in range(n_heads):
        one_head(head)


def attend(info, bases, queries, chunks, acc=None, finish=True):
    seqs, span, width = queries.shape
    n_heads = width // 256
    n = len(chunks)
    q_spec = pl.BlockSpec((1, span, width), lambda b, *_: (b, 0, 0))
    acc_spec = pl.BlockSpec((1, n_heads, 2 * span, 256), lambda b, *_: (b, 0, 0, 0))
    acc_shape = jax.ShapeDtypeStruct((seqs, n_heads, 2 * span, 256), f32)
    args = [queries, *chunks]
    in_specs = [q_spec] + [any_spec] * n
    if acc is not None:
        args.append(acc)
        in_specs.append(acc_spec)
    if finish:
        out_shape = [jax.ShapeDtypeStruct(queries.shape, bf16)] * 2
        out_specs = [q_spec, q_spec]
    else:
        out_shape, out_specs = acc_shape, acc_spec
    return pl.pallas_call(
        functools.partial(attend_kernel, n, acc is not None, finish),
        grid_spec=pltpu.PrefetchScalarGridSpec(
            num_scalar_prefetch=1,
            grid=(seqs,),
            in_specs=in_specs,
            out_specs=out_specs,
            scratch_shapes=[
                pltpu.VMEM((2, n, span, chunks[0].shape[2]), bf16),
                pltpu.SemaphoreType.DMA((2, n)),
                pltpu.VMEM((2 * span, 256), f32),
            ],
        ),
        out_shape=out_shape,
        compiler_params=params(1),
        cost_estimate=pl.CostEstimate(
            flops=4 * 4 * seqs * span * width * span * n,
            bytes_accessed=4 * seqs * (span * width * 3 + n * span * width // 2),
            transcendentals=seqs * span * width // 64 * span * n,
        ),
    )(jnp.concatenate([info, bases]), *args)


def attend_back_kernel(n, with_acc, finish, info_ref, q_ref, do_ref, dot_ref, log_ref, *refs):
    chunks, refs = refs[:n], refs[n:]
    if with_acc:
        acc_in, refs = refs[0], refs[1:]
    own_ref, their_ref, dq_ref, buffer, sems, acc, q_wide, do_wide, grads_out = refs
    seq, n_seqs = pl.program_id(0), pl.num_programs(0)
    span = q_ref.shape[1]
    n_heads = q_ref.shape[2] // 256
    alive = info_ref[0] < info_ref[1 + seq]
    slot = fetch_chunks(chunks, buffer, sems, info_ref, span, True)
    grads_out[...] = jnp.zeros(grads_out.shape, grads_out.dtype)

    def one_head(head):
        parity = head % 2
        k_lanes = slice(head // 2 * 128, head // 2 * 128 + 128)
        v_lanes = slice((n_heads + head) // 2 * 128, (n_heads + head) // 2 * 128 + 128)
        acc[...] = acc_in[0, head] if with_acc else jnp.zeros(acc.shape, f32)

        @pl.when(alive)
        def _():
            do_wide[:, :128] = stacked_at(do_ref, head)
            do_wide[:, 128:] = stacked_at(dot_ref, head)
            q_wide[:, :128] = stacked_at(q_ref, head)
            q_wide[:, 128:] = stacked_at(log_ref, head)

            @pl.loop(0, n)
            def _(chunk):
                base = info_ref[1 + n_seqs + chunk]
                whole, partly = block_state(info_ref, seq, base, span, span)

                def step(masked):
                    low = lane_iota((span, 128)) < 64
                    half_lane = lax.rem(lane_iota((span, 128)), 64)
                    pick_low = jnp.where(low & (half_lane < 2), 1.0, 0.0)
                    pick_high = jnp.where(low | (half_lane >= 2), 0.0, 1.0)
                    picks = jnp.concatenate([pick_low, pick_high], axis=0).astype(bf16)
                    k0, k1 = placed_pair(buffer[slot, chunk, :, k_lanes], parity, low)
                    v0, v1 = placed_pair(buffer[slot, chunk, :, v_lanes], parity, low)
                    k_pair = jnp.concatenate([k0, k1], axis=0)
                    k_turned = jnp.transpose(k_pair).astype(bf16)
                    k_wide = jnp.concatenate([k_pair.astype(bf16), picks], axis=1)
                    v_wide = jnp.concatenate(
                        [jnp.concatenate([v0, v1], axis=0).astype(bf16), picks], axis=1
                    )
                    scores = mm(k_wide, q_wide[...], NT)
                    if masked:
                        scores = scores + mask_bias(info_ref, seq, base, span, 0)
                    weights = jnp.exp2(scores)
                    grads = (weights * mm(v_wide, do_wide[...], NT)).astype(bf16)
                    both_v = mm(weights.astype(bf16), do_wide[:, :128])
                    both_k = mm(grads, q_wide[:, :128]) * math.log(2.0)
                    acc[...] += mm(k_turned, grads)

                    def joined(pair):
                        total = jnp.where(low, pair[:span] + pltpu.roll(pair[span:], 64, 1), 0.0)
                        return pltpu.roll(total, 64, 1) if parity else total

                    dtype = grads_out.dtype
                    grads_out[chunk, :, k_lanes] += joined(both_k).astype(dtype)
                    grads_out[chunk, :, v_lanes] += joined(both_v).astype(dtype)

                @pl.when(whole)
                def _():
                    step(False)

                @pl.when(partly)
                def _():
                    step(True)

        if finish:
            unstack_to(dq_ref, head, jnp.transpose(acc[...]) * 0.125)
        else:
            dq_ref[0, head] = acc[...]

    for head in range(n_heads):
        one_head(head)
    own_ref[:, 0] = grads_out[: n // 2]
    their_ref[:, 0] = grads_out[n // 2 :]


def attend_back(info, bases, queries, grad_out, dots, logs, chunks, acc=None, finish=True):
    seqs, span, width = queries.shape
    n_heads = width // 256
    n = len(chunks)
    q_spec = pl.BlockSpec((1, span, width), lambda b, *_: (b, 0, 0))
    acc_spec = pl.BlockSpec((1, n_heads, 128, 2 * span), lambda b, *_: (b, 0, 0, 0))
    acc_shape = jax.ShapeDtypeStruct((seqs, n_heads, 128, 2 * span), f32)
    args = [queries, grad_out, dots, logs, *chunks]
    in_specs = [q_spec] * 4 + [any_spec] * n
    if acc is not None:
        args.append(acc)
        in_specs.append(acc_spec)
    kv_width = chunks[0].shape[2]
    if finish:
        dq_shape, dq_spec = jax.ShapeDtypeStruct(queries.shape, bf16), q_spec
    else:
        dq_shape, dq_spec = acc_shape, acc_spec
    grad_shape = jax.ShapeDtypeStruct((n // 2, seqs, span, kv_width), bf16)
    grad_spec = pl.BlockSpec((n // 2, 1, span, kv_width), lambda b, *_: (0, b, 0, 0))
    return pl.pallas_call(
        functools.partial(attend_back_kernel, n, acc is not None, finish),
        grid_spec=pltpu.PrefetchScalarGridSpec(
            num_scalar_prefetch=1,
            grid=(seqs,),
            in_specs=in_specs,
            out_specs=[grad_spec, grad_spec, dq_spec],
            scratch_shapes=[
                pltpu.VMEM((2, n, span, kv_width), bf16),
                pltpu.SemaphoreType.DMA((2, n)),
                pltpu.VMEM((128, 2 * span), f32),
                pltpu.VMEM((2 * span, 256), bf16),
                pltpu.VMEM((2 * span, 256), bf16),
                pltpu.VMEM((n, span, kv_width), bf16),
            ],
        ),
        out_shape=[grad_shape, grad_shape, dq_shape],
        compiler_params=params(1),
        cost_estimate=pl.CostEstimate(
            flops=10 * 4 * seqs * span * width * span * n,
            bytes_accessed=4 * seqs * (span * width * 4 + span * n * width),
            transcendentals=seqs * span * width // 64 * span * n,
        ),
    )(jnp.concatenate([info, bases]), *args)


def unproject_kernel(
    head_dim,
    info_ref,
    grad_ref,
    raw_ref,
    scale_ref,
    gain_ref,
    cos_ref,
    sa_ref,
    sb_ref,
    out_ref,
    sum_ref,
):
    @pl.when(pl.program_id(0) == 0)
    def _():
        sum_ref[...] = jnp.zeros(sum_ref.shape, f32)

    alive = info_ref[0] < info_ref[1 + pl.program_id(0)]

    @pl.when(jnp.logical_not(alive))
    def _():
        out_ref[...] = jnp.zeros(out_ref.shape, out_ref.dtype)

    @pl.when(alive)
    def _():
        scale = scale_ref[:, :1]
        mean_matrix = group_matrix(head_dim, 1.0 / head_dim)
        normed = raw_ref.shape[1]
        for slab in range(normed // 128):
            lanes = slice(128 * slab, 128 * slab + 128)
            raw = raw_ref[:, lanes].astype(f32)
            inverse = lax.rsqrt(group_sum(raw * raw, mean_matrix) + norm_eps)
            unit = raw * inverse
            turned = turn_back(grad_ref[:, lanes].astype(f32), cos_ref, sa_ref, sb_ref)
            sum_ref[...] += jnp.broadcast_to(
                jnp.sum(turned * unit, axis=0, keepdims=True), sum_ref.shape
            )
            inner = turned * gain_ref[...]
            mean = group_sum(inner * unit, mean_matrix)
            out_ref[:, lanes] = (inverse * (inner - unit * mean) * scale).astype(bf16)
        if normed < grad_ref.shape[1]:
            out_ref[:, normed:] = (grad_ref[:, normed:].astype(f32) * scale).astype(bf16)


def unproject(info, grad, raw, scale, gain, tables, head_dim):
    rows, width = grad.shape
    span = tables[0].shape[0]
    row_block = lambda a: pl.BlockSpec((span, a.shape[1]), lambda i, *_: (i, 0))
    fixed = lambda a: pl.BlockSpec(a.shape, lambda i, *_: (0,) * a.ndim)
    return pl.pallas_call(
        functools.partial(unproject_kernel, head_dim),
        grid_spec=pltpu.PrefetchScalarGridSpec(
            num_scalar_prefetch=1,
            grid=(rows // span,),
            in_specs=[row_block(a) for a in (grad, raw, scale)]
            + [fixed(a) for a in (gain, *tables)],
            out_specs=[row_block(grad), pl.BlockSpec((8, 128), lambda i, *_: (0, 0))],
        ),
        out_shape=[
            jax.ShapeDtypeStruct((rows, width), bf16),
            jax.ShapeDtypeStruct((8, 128), f32),
        ],
        compiler_params=params(1),
        cost_estimate=pl.CostEstimate(
            flops=8 * 128 * rows * width,
            bytes_accessed=6 * rows * width,
            transcendentals=rows * width,
        ),
    )(info, grad, raw, scale, gain, *tables)


def feed_kernel(
    grid,
    span,
    split,
    info_ref,
    place_ref,
    tok_ref,
    heads_ref,
    cot_ref,
    *rest,
):
    pieces, rest = rest[:8], rest[8:]
    out_ref, hidden_ref, mid_ref, dgu_ref, dmid_ref, dheads_ref, dots_ref, *rest = rest
    w_out, w_gu, w_down, out_sems, gu_sems, down_sems = rest
    a, b = split
    out_loads = lambda: loads(grid, place_ref, pieces, w_out, out_sems, (0, a))
    gu_loads = lambda: loads(grid, place_ref, pieces, w_gu, gu_sems, (2 * a, 2 * a + b))
    down_loads = lambda: loads(grid, place_ref, pieces, w_down, down_sems, (a, 2 * a))

    @pl.when(pl.program_id(0) == 0)
    def _():
        load_all(out_loads() + gu_loads() + down_loads())

    rows = tok_ref.shape[0]
    middle = tok_ref[...].astype(f32) + mm(heads_ref[...], w_out[...], NT)
    middle_low = middle.astype(bf16)
    mid_ref[...] = middle_low
    scale = lax.rsqrt(jnp.mean(middle * middle, axis=-1, keepdims=True) + norm_eps)
    gate_up = mm(middle_low, w_gu[...]) * scale
    half = gate_up.shape[1] // 2
    gate, up = gate_up[:, :half], gate_up[:, half:]
    sig = 1.0 / (1.0 + jnp.exp(-gate))
    silu = gate * sig
    hidden = silu * up
    hidden_low = hidden.astype(bf16)
    out_ref[...] = (middle + mm(hidden_low, w_down[...], NT)).astype(bf16)

    first = pl.program_id(0) * (rows // span)
    count = rows // span
    longest = info_ref[1 + first]
    for k in range(1, count):
        longest = jnp.maximum(longest, info_ref[1 + first + k])
    alive = info_ref[0] < longest

    @pl.when(alive)
    def _():
        position = lax.broadcasted_iota(jnp.int32, (span, 1), 0) + info_ref[0]
        valid = jnp.concatenate(
            [(position < info_ref[1 + first + k]).astype(f32) for k in range(count)], axis=0
        )
        hidden_ref[...] = (hidden * valid).astype(bf16)
        cot = cot_ref[...].astype(f32) * valid
        grad_hidden = mm(cot.astype(bf16), w_down[...])
        grad_gate = grad_hidden * up * (sig * (1.0 + gate * (1.0 - sig))) * scale
        grad_up = grad_hidden * silu * scale
        grad_gu = jnp.concatenate([grad_gate.astype(bf16), grad_up.astype(bf16)], axis=1)
        dgu_ref[...] = grad_gu
        back = mm(grad_gu, w_gu[...], NT)
        unit = middle * scale
        grad_mid = cot + back - unit * jnp.mean(back * unit, axis=-1, keepdims=True)
        grad_mid = grad_mid.astype(bf16)
        dmid_ref[...] = grad_mid
        grad_heads = mm(grad_mid, w_out[...]).astype(bf16)
        dheads_ref[...] = grad_heads
        ones = group_matrix(64, 1.0)
        for slab in range(a // 128):
            lanes = slice(128 * slab, 128 * slab + 128)
            product = grad_heads[:, lanes].astype(f32) * heads_ref[:, lanes].astype(f32)
            dots_ref[:, lanes] = split_lanes(-group_sum(product, ones))

    @pl.when(jnp.logical_not(alive))
    def _():
        for ref in (hidden_ref, dgu_ref, dmid_ref, dheads_ref, dots_ref):
            ref[...] = jnp.zeros(ref.shape, ref.dtype)


def feed(grid, info, tokens, heads, cotangent, pieces, split, span):
    rows, width = tokens.shape
    a, b = split
    tile = max(span, min(256, rows))
    block = lambda n: pl.BlockSpec((tile, n), lambda i, *_: (i, 0))
    shape = lambda n: jax.ShapeDtypeStruct((rows, n), bf16)
    n = n_loads(grid)
    outs = (width, a, width, b, width, a, a)
    macs = width * (2 * a + b)
    return pl.pallas_call(
        functools.partial(feed_kernel, grid, span, split),
        grid_spec=pltpu.PrefetchScalarGridSpec(
            num_scalar_prefetch=2,
            grid=(rows // tile,),
            in_specs=[block(width), block(a), block(width)] + [any_spec] * 8,
            out_specs=[block(n) for n in outs],
            scratch_shapes=[
                pltpu.VMEM((width, a), bf16),
                pltpu.VMEM((width, b), bf16),
                pltpu.VMEM((width, a), bf16),
                pltpu.SemaphoreType.DMA((n,)),
                pltpu.SemaphoreType.DMA((n,)),
                pltpu.SemaphoreType.DMA((n,)),
            ],
        ),
        out_shape=[shape(n) for n in outs],
        compiler_params=params(1),
        cost_estimate=pl.CostEstimate(
            flops=6 * rows * macs,
            bytes_accessed=2 * (rows * (sum(outs) + 2 * width + a) + macs),
            transcendentals=rows * a,
        ),
    )(info, grid.place, tokens, heads, cotangent, *pieces)


def load_all(copies):
    for copy in copies:
        copy.start()
    for copy in copies:
        copy.wait()


def query_back_kernel(grid, info_ref, place_ref, grad_ref, *rest):
    pieces, (out_ref, weight, sems) = rest[:2], rest[2:]

    @pl.when(pl.program_id(0) == 0)
    def _():
        load_all(loads(grid, place_ref, pieces, weight, sems))

    @pl.when(info_ref[0] < info_ref[1 + pl.program_id(0)])
    def _():
        out_ref[...] = mm(grad_ref[...], weight[...], NT)


def query_back(grid, info, grad, pieces, width, span):
    rows, inner = grad.shape
    return pl.pallas_call(
        functools.partial(query_back_kernel, grid),
        grid_spec=pltpu.PrefetchScalarGridSpec(
            num_scalar_prefetch=2,
            grid=(rows // span,),
            in_specs=[pl.BlockSpec((span, inner), lambda i, *_: (i, 0))] + [any_spec] * 2,
            out_specs=pl.BlockSpec((span, width), lambda i, *_: (i, 0)),
            scratch_shapes=[
                pltpu.VMEM((width, inner), bf16),
                pltpu.SemaphoreType.DMA((n_loads(grid),)),
            ],
        ),
        out_shape=jax.ShapeDtypeStruct((rows, width), f32),
        compiler_params=params(1),
        cost_estimate=pl.CostEstimate(
            flops=2 * rows * width * inner,
            bytes_accessed=2 * (rows * (2 * width + inner) + width * inner),
            transcendentals=0,
        ),
    )(info, grid.place, grad, *pieces)


def last_kernel(grid, info_ref, place_ref, tok_ref, grad_ref, back_ref, dmid_ref, scale_ref, *rest):
    pieces, (out_ref, weight, sems) = rest[:2], rest[2:]

    @pl.when(pl.program_id(0) == 0)
    def _():
        load_all(loads(grid, place_ref, pieces, weight, sems))

    alive = info_ref[0] < info_ref[1 + pl.program_id(0)]

    @pl.when(alive)
    def _():
        back = back_ref[...] + mm(grad_ref[...], weight[...], NT)
        unit = tok_ref[...].astype(f32) * scale_ref[:, :1]
        grad = dmid_ref[...].astype(f32) + back
        grad = grad - unit * jnp.mean(back * unit, axis=-1, keepdims=True)
        out_ref[...] = grad.astype(bf16)

    @pl.when(jnp.logical_not(alive))
    def _():
        out_ref[...] = jnp.zeros(out_ref.shape, out_ref.dtype)


def last(grid, info, tokens, grad_kv, back, grad_mid, scale, pieces, span):
    rows, width = tokens.shape
    block = lambda a: pl.BlockSpec((span, a.shape[1]), lambda i, *_: (i, 0))
    inner = grad_kv.shape[1]
    args = (tokens, grad_kv, back, grad_mid, scale)
    return pl.pallas_call(
        functools.partial(last_kernel, grid),
        grid_spec=pltpu.PrefetchScalarGridSpec(
            num_scalar_prefetch=2,
            grid=(rows // span,),
            in_specs=[block(a) for a in args] + [any_spec] * 2,
            out_specs=block(tokens),
            scratch_shapes=[
                pltpu.VMEM((width, inner), bf16),
                pltpu.SemaphoreType.DMA((n_loads(grid),)),
            ],
        ),
        out_shape=jax.ShapeDtypeStruct(tokens.shape, bf16),
        compiler_params=params(1),
        cost_estimate=pl.CostEstimate(
            flops=2 * rows * width * inner,
            bytes_accessed=2 * (rows * (5 * width + inner) + width * inner),
            transcendentals=0,
        ),
    )(info, grid.place, *args, *pieces)


def weight_kernel(grid, shard, span, n_pairs, place_ref, info_ref, *refs):
    lefts, rights = refs[:n_pairs], refs[n_pairs : 2 * n_pairs]
    mine_ref, theirs_ref, acc = refs[2 * n_pairs :]
    core = place_ref[2]
    middle = grid.depth // 2
    n_seqs = lefts[0].shape[0] // span
    shortest = info_ref[1]
    for seq in range(1, n_seqs):
        shortest = jnp.minimum(shortest, info_ref[1 + seq])
    all_alive = info_ref[0] < shortest
    column = 0
    for left, right in zip(lefts, rights):
        width = right.shape[1]

        @pl.when(all_alive)
        def _(left=left, right=right, width=width):
            acc[:, :width] = mm(left[...], right[...], TN)

        @pl.when(jnp.logical_not(all_alive))
        def _(left=left, right=right, width=width):
            acc[:, :width] = jnp.zeros((acc.shape[0], width), f32)
            for seq in range(n_seqs):
                rows = slice(seq * span, (seq + 1) * span)

                @pl.when(info_ref[0] < info_ref[1 + seq])
                def _(rows=rows):
                    acc[:, :width] += mm(left[rows, :], right[rows, :], TN)

        for level in range(grid.depth):
            half, at = level // middle, level % middle
            for whose, ref in ((core, mine_ref), (1 - core, theirs_ref)):
                start = pl.multiple_of((level * 2 + whose) * shard, shard)
                ref[half, 0, at, :, column : column + width] = acc[
                    pl.ds(start, shard), :width
                ].astype(bf16)
        column += width


def weight_grad(grid, info, span, *pairs):
    lefts, rights = [p[0] for p in pairs], [p[1] for p in pairs]
    rows, features = lefts[0].shape
    widths = [r.shape[1] for r in rights]
    total = sum(widths)
    part = features // grid.rows
    shard = part // grid.seqs
    middle = grid.depth // 2
    shape = jax.ShapeDtypeStruct((2, grid.rows, middle, shard, total), bf16)
    piece = pl.BlockSpec((2, 1, middle, shard, total), lambda i, *_: (0, i, 0, 0, 0))
    return pl.pallas_call(
        functools.partial(weight_kernel, grid, shard, span, len(pairs)),
        grid_spec=pltpu.PrefetchScalarGridSpec(
            num_scalar_prefetch=2,
            grid=(grid.rows,),
            in_specs=[pl.BlockSpec((rows, part), lambda i, place, info: (0, place[0] ^ i))]
            * len(pairs)
            + [pl.BlockSpec(r.shape, lambda i, *_: (0, 0)) for r in rights],
            out_specs=[piece, piece],
            scratch_shapes=[pltpu.VMEM((part, max(widths)), f32)],
        ),
        out_shape=[shape, shape],
        compiler_params=params(1),
        cost_estimate=pl.CostEstimate(
            flops=2 * rows * features * total,
            bytes_accessed=2 * (rows * (features * len(pairs) + total) + features * total),
            transcendentals=0,
        ),
    )(grid.place, info, *lefts, *rights)


def shards(
    n_rows,
    n_seqs,
    tokens,
    lengths,
    cotangent,
    w_qkv,
    w_out,
    w_gateup,
    w_down,
    norm_attn,
    norm_ffn,
    q_gain,
    k_gain,
):
    grid = Grid(n_rows, n_seqs)
    seq_count, span_len, model_width = tokens.shape
    row_count = seq_count * span_len
    head_dim = q_gain.shape[0]
    half_dim = head_dim // 2
    query_width = w_out.shape[1]
    kv_width = (w_qkv.shape[1] - query_width) // 2
    log2_scale = math.log2(math.e) * head_dim ** (-0.5)

    offset = (grid.seq * span_len).astype(jnp.int32)
    positions = offset + jnp.arange(span_len, dtype=jnp.int32)
    inverse = theta_base ** (-jnp.arange(half_dim, dtype=f32) * 2.0 / head_dim)
    angles = positions.astype(f32)[:, None] * inverse[None, :]
    cosine, sine = jnp.cos(angles), jnp.sin(angles)
    nothing = jnp.zeros_like(sine)
    tables = (
        jnp.concatenate([cosine] * 4, axis=1),
        jnp.concatenate([-sine, nothing] * 2, axis=1),
        jnp.concatenate([nothing, sine] * 2, axis=1),
    )
    q_gain_f = jnp.concatenate([q_gain.astype(f32)] * 2)[None, :]
    k_gain_f = jnp.concatenate([k_gain.astype(f32)] * 2)[None, :]
    info = jnp.concatenate([offset[None], lengths])

    attn_gain = norm_attn.astype(f32)[:, None]
    ffn_gain = norm_ffn.astype(f32)[:, None]
    qkv_shard = (w_qkv.astype(f32) * attn_gain).astype(bf16)
    gateup_shard = (w_gateup.astype(f32) * ffn_gain).astype(bf16)

    order = Order()
    depth = grid.depth
    split = max(1, depth // 2)
    kv_steps = grid.ring(qkv_shard[:, query_width:])
    kv_own, kv_came = grid.spread(kv_steps)
    q_steps = grid.ring(qkv_shard[:, :query_width], [[kv_steps[1]], [kv_steps[-1]]])[:3]
    feed_steps = grid.ring(
        jnp.concatenate([w_out, w_down, gateup_shard], axis=1), [[kv_steps[2]], kv_came[-1]]
    )[:3]
    kv_pieces = grid.with_partner(kv_own, feed_steps[1], q_steps[1])

    rows_in = tokens.reshape(row_count, model_width)
    kv, k_raw, scale1 = project(grid, rows_in, kv_pieces, k_gain_f, tables, kv_width, head_dim)
    order.leave(kv)
    while len(feed_steps) < depth:
        feed_steps.append(grid.around(after(feed_steps[-1], kv)))
        q_steps.append(grid.around(after(q_steps[-1], kv)))
    q_own, q_came = grid.spread(q_steps, [[kv]] + [feed_steps[2:3]] * (len(grid.orders[0]) - 1))
    feed_own, feed_came = grid.spread(feed_steps, [q_came[-1]])
    kv = kv.reshape(seq_count, span_len, 2 * kv_width)
    reach = [kv]
    for _ in range(1, depth - 1):
        reach.append(grid.up(reach[-1]))
    q_pieces = grid.with_partner(q_own, reach[1], feed_steps[-1])
    q, q_raw = project(
        grid,
        order.enter(rows_in),
        q_pieces,
        q_gain_f * log2_scale,
        tables,
        query_width,
        head_dim,
        scale1,
    )
    order.leave(q)
    q = q.reshape(seq_count, span_len, query_width)
    bases = []
    for step in range(depth):
        level = grid.level - step
        start = jnp.stack([level * 2 + grid.core, level * 2 + 1 - grid.core]) * span_len
        bases.append(jnp.where(level >= 0, start, -1).astype(jnp.int32))
    reach[-1] = order.late(reach[-1])
    reach.append(grid.up(reach[-1]))
    crossed = [grid.partner(own) for own in reach[:-1]]
    order.pin(*feed_came[0])
    feed_held = [grid.partner(order.late(feed_own[k])) for k in (0, 2)]
    near = [c for pair in zip(reach[:-1], crossed) for c in pair]
    acc = attend(info, jnp.concatenate(bases[:-1]), order.enter(q), near, None, False)
    order.leave(acc)
    order.pin(*feed_came[-1], *feed_held)
    feed_found = [grid.partner(order.late(feed_own[k])) for k in (1, 3)]
    reach[-1] = order.late(reach[-1])
    crossed.append(grid.partner(reach[-1]))
    heads, logs = attend(
        info, bases[-1], order.enter(q), [reach[-1], crossed[-1]], acc, True
    )
    order.leave(heads)
    attended = heads.reshape(row_count, query_width)
    feed_pieces = feed_own + [feed_held[0], feed_found[0], feed_held[1], feed_found[1]]

    flat_cot = cotangent.reshape(row_count, model_width)
    output, hidden, middle, grad_gu, grad_mid, grad_heads, dots = feed(
        grid,
        info,
        rows_in,
        attended,
        flat_cot,
        feed_pieces,
        (query_width, w_gateup.shape[1]),
        span_len,
    )
    order.leave(hidden)
    grad_heads = grad_heads.reshape(seq_count, span_len, query_width)
    dots = dots.reshape(seq_count, span_len, query_width)

    def advance(*sums):
        for each in sums:
            order.pin(*each.land())
            order.pin(*each.go())

    kv_flight = []

    def kv_sum_here(own, other):
        kv_flight[:] = [order.late(came) for came in kv_flight]
        here = own.astype(f32) + other.astype(f32)
        for came in kv_flight:
            here = here + came.astype(f32)
        return here.astype(bf16)

    def kv_hop(own, other):
        sent = order.late(kv_sum_here(own, other))
        order.pin(sent)
        kv_flight[:] = [grid.down(sent)]

    def back(steps, acc, final):
        chosen = [reach[k] for k in steps] + [crossed[k] for k in steps]
        starts = jnp.stack([bases[k] for k in steps], axis=1).reshape(-1)
        return attend_back(
            info, starts, order.enter(q), grad_heads, dots, logs, chosen, acc, final
        )

    feed_sum = Sum(
        grid,
        order,
        weight_grad(
            grid,
            info,
            span_len,
            (flat_cot, order.enter(hidden)),
            (middle, grad_gu),
            (grad_mid, attended),
        ),
    )
    order.leave(feed_sum.theirs)
    advance(feed_sum)
    far_own, far_theirs, acc_q = back(range(split, depth), None, False)
    order.leave(acc_q)
    far_came = grid.partner(far_theirs)
    kv_hop(far_own[-1], far_came[-1])
    advance(feed_sum)
    near_own, near_theirs, grad_q = back(range(split), acc_q, True)
    order.leave(grad_q)
    near_came = grid.partner(order.late(near_theirs))
    for step in reversed(range(split, depth - 1)):
        kv_hop(far_own[step - split], far_came[step - split])
    advance(feed_sum)
    grad_pq, gq = unproject(
        info,
        order.enter(grad_q.reshape(row_count, query_width)),
        q_raw,
        scale1,
        q_gain_f,
        tables,
        head_dim,
    )
    order.leave(grad_pq)
    q_sum = Sum(
        grid, order, weight_grad(grid, info, span_len, (rows_in, order.enter(grad_pq))), True
    )
    order.leave(q_sum.theirs)
    for step in reversed(range(1, split)):
        kv_hop(near_own[step], near_came[step])
    advance(feed_sum, q_sum)
    back_q = query_back(grid, info, order.enter(grad_pq), q_pieces, model_width, span_len)
    order.leave(back_q)
    advance(feed_sum, q_sum)
    grad_kv = kv_sum_here(near_own[0], near_came[0]).reshape(row_count, 2 * kv_width)
    grad_pkv, gk = unproject(
        info, order.enter(grad_kv), k_raw, scale1, k_gain_f, tables, head_dim
    )
    kv_sum = Sum(grid, order, weight_grad(grid, info, span_len, (rows_in, grad_pkv)), True)
    order.leave(kv_sum.theirs)
    gain_sum = Everywhere(grid, order, jnp.concatenate([gq[:1], gk[:1]], axis=0))
    advance(feed_sum, q_sum, kv_sum, gain_sum)
    grad_tokens = last(
        grid,
        info,
        rows_in,
        order.enter(grad_pkv),
        back_q,
        grad_mid,
        scale1,
        kv_pieces,
        span_len,
    )
    order.leave(grad_tokens)
    gains = gain_sum.finish()
    gains = gains[:, :head_dim] + gains[:, head_dim:]
    kv_total, q_total, feed_total = kv_sum.finish(), q_sum.finish(), feed_sum.finish()
    sum_qkv = jnp.concatenate([q_total, kv_total], axis=1)
    sum_down, sum_gateup = feed_total[:, :query_width], feed_total[:, query_width:-query_width]
    sum_out = feed_total[:, -query_width:]
    return (
        output.reshape(tokens.shape),
        grad_tokens.reshape(tokens.shape),
        sum_qkv * attn_gain,
        sum_out,
        sum_gateup * ffn_gain,
        sum_down,
        jnp.sum(sum_qkv * w_qkv.astype(f32), axis=1),
        jnp.sum(sum_gateup * w_gateup.astype(f32), axis=1),
        gains[0],
        gains[1],
    )


def solution(mesh):
    rows = P("row", "seq", None)
    weight = P(both, None)
    vector = P(both)
    return jax.shard_map(
        functools.partial(shards, mesh.shape["row"], mesh.shape["seq"]),
        mesh=mesh,
        in_specs=(rows, P("row"), rows, weight, weight, weight, weight, vector, vector, P(), P()),
        out_specs=(rows, rows, weight, weight, weight, weight, vector, vector, P(), P()),
        check_vma=False,
    )
```

```python
import functools
import math

import jax
import jax.numpy as jnp
from jax import lax
from jax.experimental import pallas as pl
from jax.experimental.pallas import tpu as pltpu
from jax.sharding import PartitionSpec as P

norm_eps = 1e-06
theta_base = 10000.0
both = ("row", "seq")
f32 = jnp.float32
bf16 = jnp.bfloat16
vmem_cap = 56 * 1024 * 1024
any_spec = pl.BlockSpec(memory_space=pl.ANY)
NN = (((1,), (0,)), ((), ()))
NT = (((1,), (1,)), ((), ()))
TN = (((0,), (0,)), ((), ()))


def mm(left, right, dims=NN):
    return lax.dot_general(left, right, dims, preferred_element_type=f32)


def after(value, *earlier):
    return lax.optimization_barrier((value, *earlier))[0]


def params(n_grid):
    return pltpu.CompilerParams(
        dimension_semantics=("arbitrary",) * n_grid, vmem_limit_bytes=vmem_cap
    )


def lane_iota(shape):
    return lax.broadcasted_iota(jnp.int32, shape, len(shape) - 1)


def group_matrix(head_dim, value):
    i = lax.broadcasted_iota(jnp.int32, (128, 128), 0) // head_dim
    j = lax.broadcasted_iota(jnp.int32, (128, 128), 1) // head_dim
    return jnp.where(i == j, value, 0.0).astype(bf16)


def group_sum(values, matrix):
    high = values.astype(bf16)
    low = (values - high.astype(f32)).astype(bf16)
    return mm(high, matrix) + mm(low, matrix)


def turn(values, cos_ref, sa_ref, sb_ref):
    return (
        values * cos_ref[...]
        + pltpu.roll(values, 96, 1) * sa_ref[...]
        + pltpu.roll(values, 32, 1) * sb_ref[...]
    )


def turn_back(values, cos_ref, sa_ref, sb_ref):
    return (
        values * cos_ref[...]
        - pltpu.roll(values, 96, 1) * sa_ref[...]
        - pltpu.roll(values, 32, 1) * sb_ref[...]
    )


class Grid:
    def __init__(self, rows, seqs):
        self.rows, self.seqs, self.depth = rows, seqs, seqs // 2
        self.row = lax.axis_index("row")
        seq = lax.axis_index("seq")
        self.level, self.core = seq // 2, lax.rem(seq, 2)
        self.seq = seq
        bits = [1 << k for k in range(rows.bit_length() - 1)]
        self.orders = (bits, bits[::-1])
        self.place = jnp.stack([self.row, self.level, self.core]).astype(jnp.int32)

    def move(self, value, where):
        pairs = []
        for row in range(self.rows):
            for seq in range(self.seqs):
                target = where(row, seq)
                if target is not None:
                    pairs.append((row * self.seqs + seq, target[0] * self.seqs + target[1]))
        return lax.ppermute(value, both, pairs)

    def across(self, value, mask):
        return self.move(value, lambda r, s: (r ^ mask, s))

    def partner(self, value):
        return self.move(value, lambda r, s: (r, s ^ 1))

    def around(self, value, steps=1):
        return self.move(value, lambda r, s: (r, (s + 2 * steps) % self.seqs))

    def up(self, value):
        return self.move(value, lambda r, s: (r, s + 2) if s + 2 < self.seqs else None)

    def down(self, value):
        return self.move(value, lambda r, s: (r, s - 2) if s >= 2 else None)

    def masks(self, half):
        found = [0]
        for bit in self.orders[half]:
            found = found + [m ^ bit for m in found]
        return found

    def ring(self, shard, waits=()):
        steps = [shard]
        for hop in range(self.depth - 1):
            held = steps[-1]
            if hop < len(waits):
                held = after(held, *waits[hop])
            steps.append(self.around(held))
        return steps

    def spread(self, steps, waits=()):
        middle = self.depth // 2
        held = [jnp.stack(steps[:middle])[None], jnp.stack(steps[middle:])[None]]
        pieces = []
        arrived = []
        for stage in range(len(self.orders[0])):
            for half in range(2):
                if stage < len(waits):
                    held[half] = after(held[half], *waits[stage])
            found = [self.across(held[half], self.orders[half][stage]) for half in range(2)]
            arrived.append(found)
            if stage == len(self.orders[0]) - 1:
                pieces = [held[0], found[0], held[1], found[1]]
            else:
                held = [jnp.concatenate([held[k], found[k]], axis=0) for k in range(2)]
        return pieces, arrived

    def with_partner(self, pieces, *waits):
        pieces = jnp.stack(pieces)
        return [pieces, self.partner(after(pieces, *waits) if waits else pieces)]


class Order:
    def __init__(self):
        self.kernel = None
        self.waits = []

    def pin(self, *values):
        self.waits += values

    def enter(self, value):
        return after(value, *self.waits) if self.waits else value

    def leave(self, value):
        self.kernel = value
        self.waits = [value]

    def late(self, value):
        return after(value, self.kernel)


class Everywhere:
    def __init__(self, grid, order, value):
        self.grid, self.order, self.total = grid, order, value
        self.flight = []
        self.moves = [(bit, 0) for bit in grid.orders[0]]
        self.moves += [(0, 1 << k) for k in range(grid.seqs.bit_length() - 1)]

    def land(self):
        came, self.flight = [self.order.late(c) for c in self.flight], []
        for each in came:
            self.total = self.total + each
        return came

    def go(self):
        self.land()
        if not self.moves:
            return []
        row, seq = self.moves.pop(0)
        sent = self.order.late(self.total)
        self.flight = [self.grid.move(sent, lambda r, s: (r ^ row, s ^ seq))]
        return [sent]

    def finish(self):
        while self.go():
            pass
        return self.total


class Sum:
    def __init__(self, grid, order, parts, direct=False):
        mine, self.theirs = parts
        self.direct = direct
        self.grid = grid
        self.order = order
        self.halves = [[mine[half]] for half in range(2)]
        self.stage = 0
        self.flight = []
        self.row_stages = len(grid.orders[0])
        self.total = None

    def at(self, step):
        depth = self.grid.depth
        index = lax.rem(self.grid.level - step + 2 * depth, depth)
        return lax.dynamic_index_in_dim(self.levels, index, 0, keepdims=False)

    def land(self):
        came, self.flight = [self.order.late(c) for c in self.flight], []
        if came:
            if self.stage == 1:
                for half in range(2):
                    self.halves[half].append(came[0][half])
            elif self.stage <= 1 + self.row_stages:
                for half in range(2):
                    self.halves[half].append(came[half])
            elif self.direct:
                self.total = self.total + sum(c.astype(f32) for c in came)
            else:
                self.total = came[0].astype(f32) + self.at(self.stage - self.row_stages)
        return came

    def go(self):
        grid, late = self.grid, self.order.late
        self.land()
        if self.stage == 0:
            sent = [self.theirs]
            self.flight = [grid.partner(self.theirs)]
        elif self.stage <= self.row_stages:
            sent = []
            for half in range(2):
                parts = self.halves[half]
                bit = grid.orders[half][::-1][self.stage - 1]
                count = parts[0].shape[0] // 2
                if half == 0:
                    kept, given = slice(0, count), slice(count, None)
                else:
                    kept, given = slice(0, None, 2), slice(1, None, 2)
                value = sum(p[given].astype(f32) for p in parts).astype(bf16)
                self.halves[half] = [p[kept] for p in parts]
                sent.append(late(value))
                self.flight.append(grid.across(sent[half], bit))
        elif self.direct:
            if self.total is not None:
                return []
            self.levels = jnp.concatenate(
                [sum(p[0].astype(f32) for p in parts) for parts in self.halves], axis=0
            )
            self.total = self.at(0)
            sent = [
                late(self.at(grid.depth - step).astype(bf16)) for step in range(1, grid.depth)
            ]
            self.flight = [grid.around(each, k + 1) for k, each in enumerate(sent)]
        elif self.stage < self.row_stages + grid.depth:
            if self.total is None:
                self.levels = jnp.concatenate(
                    [sum(p[0].astype(f32) for p in parts) for parts in self.halves], axis=0
                )
                self.total = self.at(1)
            sent = [late(self.total.astype(bf16))]
            self.flight = [grid.around(sent[0])]
        else:
            return []
        self.stage += 1
        return sent

    def finish(self):
        while self.go():
            pass
        return self.total


def loads(grid, place_ref, pieces, target, sems, columns=None, at_column=0):
    row, level, core = place_ref[0], place_ref[1], place_ref[2]
    shard, columns_all = pieces[0].shape[-2:]
    if columns is None:
        columns = (0, columns_all)
    width = columns[1] - columns[0]
    merged = len(pieces) == 2
    copies = []
    for which in range(8):
        ref = pieces[which // 4].at[which % 4] if merged else pieces[which]
        half = which // 2 % 2
        whose = core if which < 4 else 1 - core
        first = 0 if half == 0 else grid.depth // 2
        masks = grid.masks(half)
        masks = masks[len(masks) // 2 :] if which % 2 else masks[: len(masks) // 2]
        for m, mask in enumerate(masks):
            for h in range(ref.shape[1]):
                at_level = lax.rem(level - (first + h) + grid.depth, grid.depth)
                start = ((row ^ mask) * grid.seqs + at_level * 2 + whose) * shard
                copies.append(
                    pltpu.make_async_copy(
                        ref.at[m, h, :, columns[0] : columns[1]],
                        target.at[
                            pl.ds(pl.multiple_of(start, shard), shard),
                            at_column : at_column + width,
                        ],
                        sems.at[len(copies)],
                    )
                )
    return copies


def n_loads(grid):
    return grid.rows * grid.seqs


def project_kernel(grid, normed_slabs, head_dim, with_scale, place_ref, tok_ref, *rest):
    pieces, rest = rest[:2], rest[2:]
    gain_ref, cos_ref, sa_ref, sb_ref, *rest = rest
    if with_scale:
        heads_ref, raw_ref, scale_ref, weight, sems = rest
    else:
        scale_in_ref, heads_ref, raw_ref, weight, sems = rest

    @pl.when(pl.program_id(0) == 0)
    def _():
        copies = loads(grid, place_ref, pieces, weight, sems)
        for copy in copies:
            copy.start()
        for copy in copies:
            copy.wait()

    if with_scale:
        x = tok_ref[...].astype(f32)
        scale = lax.rsqrt(jnp.mean(x * x, axis=-1, keepdims=True) + norm_eps)
        scale_ref[...] = jnp.broadcast_to(scale, scale_ref.shape)
    else:
        scale = scale_in_ref[:, :1]
    projected = mm(tok_ref[...], weight[...]) * scale
    mean_matrix = group_matrix(head_dim, 1.0 / head_dim)
    raw_ref[...] = projected[:, : raw_ref.shape[1]].astype(bf16)
    for slab in range(heads_ref.shape[1] // 128):
        lanes = slice(128 * slab, 128 * slab + 128)
        part = projected[:, lanes]
        if slab < normed_slabs:
            inverse = lax.rsqrt(group_sum(part * part, mean_matrix) + norm_eps)
            part = turn(part * inverse * gain_ref[...], cos_ref, sa_ref, sb_ref)
        heads_ref[:, lanes] = part.astype(bf16)


def project(grid, tokens, pieces, gain, tables, normed, head_dim, scale=None):
    rows, width = tokens.shape
    out_width = pieces[0].shape[-1]
    span = tables[0].shape[0]
    row_block = lambda n: pl.BlockSpec((span, n), lambda i, *_: (i, 0))
    fixed = lambda a: pl.BlockSpec(a.shape, lambda i, *_: (0,) * a.ndim)
    args = [tokens, *pieces, gain, *tables]
    in_specs = [row_block(width)] + [any_spec] * 2 + [fixed(a) for a in (gain, *tables)]
    out_shape = [
        jax.ShapeDtypeStruct((rows, out_width), bf16),
        jax.ShapeDtypeStruct((rows, normed), bf16),
    ]
    out_specs = [row_block(out_width), row_block(normed)]
    if scale is None:
        out_shape.append(jax.ShapeDtypeStruct((rows, 128), f32))
        out_specs.append(row_block(128))
    else:
        args.append(scale)
        in_specs.append(row_block(128))
    return pl.pallas_call(
        functools.partial(project_kernel, grid, normed // 128, head_dim, scale is None),
        grid_spec=pltpu.PrefetchScalarGridSpec(
            num_scalar_prefetch=1,
            grid=(rows // span,),
            in_specs=in_specs,
            out_specs=out_specs,
            scratch_shapes=[
                pltpu.VMEM((width, out_width), bf16),
                pltpu.SemaphoreType.DMA((n_loads(grid),)),
            ],
        ),
        out_shape=out_shape,
        compiler_params=params(1),
        cost_estimate=pl.CostEstimate(
            flops=4 * rows * width * out_width,
            bytes_accessed=2 * (rows * (width + 2 * out_width) + width * out_width),
            transcendentals=rows * normed,
        ),
    )(grid.place, *args)


def placed_pair(slab, parity, low):
    values = slab.astype(f32)
    rolled = pltpu.roll(values, 64, 1)
    here, there = (rolled, values) if parity else (values, rolled)
    return jnp.where(low, here, 0.0), jnp.where(low, 0.0, there)


def block_state(info_ref, seq, base, block, span):
    offset = info_ref[0]
    length = info_ref[1 + seq]
    some = (base >= 0) & (base < jnp.minimum(offset + span, length))
    whole = some & (base + block <= jnp.minimum(offset + 1, length))
    return whole, some & jnp.logical_not(whole)


def mask_bias(info_ref, seq, base, span, key_axis):
    shape = (span, span)
    behind = lax.broadcasted_iota(jnp.int32, shape, key_axis) - lax.broadcasted_iota(
        jnp.int32, shape, 1 - key_axis
    )
    key = lax.broadcasted_iota(jnp.int32, shape, key_axis)
    ok = (behind <= info_ref[0] - base) & (key < info_ref[1 + seq] - base)
    bias = jnp.where(ok, 0.0, -1e30)
    pair = jnp.concatenate([bias, bias], axis=1)
    return jnp.concatenate([pair, pair], axis=0)


def chunk_copies(chunks, buffer, sems, info_ref, seq, n_seqs, slot, span, then, backward=False):
    for i, chunk in enumerate(chunks):
        base = info_ref[1 + n_seqs + i]
        needed = (base >= 0) & (base < jnp.minimum(info_ref[0] + span, info_ref[1 + seq]))
        if backward:
            needed = needed & (info_ref[0] < info_ref[1 + seq])

        @pl.when(needed)
        def _(i=i, chunk=chunk):
            then(pltpu.make_async_copy(chunk.at[seq], buffer.at[slot, i], sems.at[slot, i]))


def fetch_chunks(chunks, buffer, sems, info_ref, span, backward=False):
    seq, n_seqs = pl.program_id(0), pl.num_programs(0)
    slot = lax.rem(seq, 2)
    common = (chunks, buffer, sems, info_ref)

    @pl.when(seq == 0)
    def _():
        chunk_copies(*common, seq, n_seqs, slot, span, lambda c: c.start(), backward)

    @pl.when(seq + 1 < n_seqs)
    def _():
        chunk_copies(*common, seq + 1, n_seqs, 1 - slot, span, lambda c: c.start(), backward)

    chunk_copies(*common, seq, n_seqs, slot, span, lambda c: c.wait(), backward)
    return slot


def stacked_at(ref, head):
    first = head * 256
    return jnp.concatenate(
        [ref[0, :, first : first + 128], ref[0, :, first + 128 : first + 256]], axis=0
    )


def unstack_to(ref, head, value):
    first = head * 256
    span = ref.shape[1]
    ref[0, :, first : first + 128] = value[:span].astype(ref.dtype)
    ref[0, :, first + 128 : first + 256] = value[span:].astype(ref.dtype)


def split_lanes(values):
    lane = lax.rem(lane_iota(values.shape), 64)
    high = values.astype(bf16).astype(f32)
    rest = values - high
    return jnp.where(lane == 0, high, jnp.where(lane == 1, rest, 0.0)).astype(bf16)


def attend_kernel(n, with_acc, finish, info_ref, q_ref, *refs):
    chunks, refs = refs[:n], refs[n:]
    if with_acc:
        acc_in, refs = refs[0], refs[1:]
    if finish:
        out_ref, log_ref, buffer, sems, acc = refs
    else:
        acc_out, buffer, sems, acc = refs
    seq, n_seqs = pl.program_id(0), pl.num_programs(0)
    span = q_ref.shape[1]
    n_heads = q_ref.shape[2] // 256
    slot = fetch_chunks(chunks, buffer, sems, info_ref, span)

    def one_head(head):
        parity = head % 2
        k_lanes = slice(head // 2 * 128, head // 2 * 128 + 128)
        v_lanes = slice((n_heads + head) // 2 * 128, (n_heads + head) // 2 * 128 + 128)
        acc[...] = acc_in[0, head] if with_acc else jnp.zeros(acc.shape, f32)

        @pl.loop(0, n)
        def _(chunk):
            base = info_ref[1 + n_seqs + chunk]
            whole, partly = block_state(info_ref, seq, base, span, span)

            def step(masked):
                low = lane_iota((span, 128)) < 64
                ones_low = jnp.where(low, 1.0, 0.0).astype(bf16)
                ones_high = jnp.where(low, 0.0, 1.0).astype(bf16)
                k0, k1 = placed_pair(buffer[slot, chunk, :, k_lanes], parity, low)
                v0, v1 = placed_pair(buffer[slot, chunk, :, v_lanes], parity, low)
                k_pair = jnp.concatenate([k0, k1], axis=0).astype(bf16)
                v_pair = jnp.concatenate(
                    [
                        jnp.concatenate([v0.astype(bf16), ones_low], axis=1),
                        jnp.concatenate([v1.astype(bf16), ones_high], axis=1),
                    ],
                    axis=0,
                )
                scores = mm(stacked_at(q_ref, head), k_pair, NT)
                if masked:
                    scores = scores + mask_bias(info_ref, seq, base, span, 1)
                weights = jnp.exp2(scores)
                acc[...] += mm(weights.astype(bf16), v_pair)

            @pl.when(whole)
            def _():
                step(False)

            @pl.when(partly)
            def _():
                step(True)

        if finish:
            totals = acc[:, 128:]
            unstack_to(out_ref, head, acc[:, :128] / totals)
            unstack_to(log_ref, head, split_lanes(-jnp.log2(totals)))
        else:
            acc_out[0, head] = acc[...]

    for head in range(n_heads):
        one_head(head)


def attend(info, bases, queries, chunks, acc=None, finish=True):
    seqs, span, width = queries.shape
    n_heads = width // 256
    n = len(chunks)
    q_spec = pl.BlockSpec((1, span, width), lambda b, *_: (b, 0, 0))
    acc_spec = pl.BlockSpec((1, n_heads, 2 * span, 256), lambda b, *_: (b, 0, 0, 0))
    acc_shape = jax.ShapeDtypeStruct((seqs, n_heads, 2 * span, 256), f32)
    args = [queries, *chunks]
    in_specs = [q_spec] + [any_spec] * n
    if acc is not None:
        args.append(acc)
        in_specs.append(acc_spec)
    if finish:
        out_shape = [jax.ShapeDtypeStruct(queries.shape, bf16)] * 2
        out_specs = [q_spec, q_spec]
    else:
        out_shape, out_specs = acc_shape, acc_spec
    return pl.pallas_call(
        functools.partial(attend_kernel, n, acc is not None, finish),
        grid_spec=pltpu.PrefetchScalarGridSpec(
            num_scalar_prefetch=1,
            grid=(seqs,),
            in_specs=in_specs,
            out_specs=out_specs,
            scratch_shapes=[
                pltpu.VMEM((2, n, span, chunks[0].shape[2]), bf16),
                pltpu.SemaphoreType.DMA((2, n)),
                pltpu.VMEM((2 * span, 256), f32),
            ],
        ),
        out_shape=out_shape,
        compiler_params=params(1),
        cost_estimate=pl.CostEstimate(
            flops=4 * 4 * seqs * span * width * span * n,
            bytes_accessed=4 * seqs * (span * width * 3 + n * span * width // 2),
            transcendentals=seqs * span * width // 64 * span * n,
        ),
    )(jnp.concatenate([info, bases]), *args)


def attend_back_kernel(n, with_acc, finish, info_ref, q_ref, do_ref, dot_ref, log_ref, *refs):
    chunks, refs = refs[:n], refs[n:]
    if with_acc:
        acc_in, refs = refs[0], refs[1:]
    own_ref, their_ref, dq_ref, buffer, sems, acc, q_wide, do_wide, grads_out = refs
    seq, n_seqs = pl.program_id(0), pl.num_programs(0)
    span = q_ref.shape[1]
    n_heads = q_ref.shape[2] // 256
    alive = info_ref[0] < info_ref[1 + seq]
    slot = fetch_chunks(chunks, buffer, sems, info_ref, span, True)
    grads_out[...] = jnp.zeros(grads_out.shape, grads_out.dtype)

    def one_head(head):
        parity = head % 2
        k_lanes = slice(head // 2 * 128, head // 2 * 128 + 128)
        v_lanes = slice((n_heads + head) // 2 * 128, (n_heads + head) // 2 * 128 + 128)
        acc[...] = acc_in[0, head] if with_acc else jnp.zeros(acc.shape, f32)

        @pl.when(alive)
        def _():
            do_wide[:, :128] = stacked_at(do_ref, head)
            do_wide[:, 128:] = stacked_at(dot_ref, head)
            q_wide[:, :128] = stacked_at(q_ref, head)
            q_wide[:, 128:] = stacked_at(log_ref, head)

            @pl.loop(0, n)
            def _(chunk):
                base = info_ref[1 + n_seqs + chunk]
                whole, partly = block_state(info_ref, seq, base, span, span)

                def step(masked):
                    low = lane_iota((span, 128)) < 64
                    half_lane = lax.rem(lane_iota((span, 128)), 64)
                    pick_low = jnp.where(low & (half_lane < 2), 1.0, 0.0)
                    pick_high = jnp.where(low | (half_lane >= 2), 0.0, 1.0)
                    picks = jnp.concatenate([pick_low, pick_high], axis=0).astype(bf16)
                    k0, k1 = placed_pair(buffer[slot, chunk, :, k_lanes], parity, low)
                    v0, v1 = placed_pair(buffer[slot, chunk, :, v_lanes], parity, low)
                    k_pair = jnp.concatenate([k0, k1], axis=0)
                    k_turned = jnp.transpose(k_pair).astype(bf16)
                    k_wide = jnp.concatenate([k_pair.astype(bf16), picks], axis=1)
                    v_wide = jnp.concatenate(
                        [jnp.concatenate([v0, v1], axis=0).astype(bf16), picks], axis=1
                    )
                    scores = mm(k_wide, q_wide[...], NT)
                    if masked:
                        scores = scores + mask_bias(info_ref, seq, base, span, 0)
                    weights = jnp.exp2(scores)
                    grads = (weights * mm(v_wide, do_wide[...], NT)).astype(bf16)
                    both_v = mm(weights.astype(bf16), do_wide[:, :128])
                    both_k = mm(grads, q_wide[:, :128]) * math.log(2.0)
                    acc[...] += mm(k_turned, grads)

                    def joined(pair):
                        total = jnp.where(low, pair[:span] + pltpu.roll(pair[span:], 64, 1), 0.0)
                        return pltpu.roll(total, 64, 1) if parity else total

                    dtype = grads_out.dtype
                    grads_out[chunk, :, k_lanes] += joined(both_k).astype(dtype)
                    grads_out[chunk, :, v_lanes] += joined(both_v).astype(dtype)

                @pl.when(whole)
                def _():
                    step(False)

                @pl.when(partly)
                def _():
                    step(True)

        if finish:
            unstack_to(dq_ref, head, jnp.transpose(acc[...]) * 0.125)
        else:
            dq_ref[0, head] = acc[...]

    for head in range(n_heads):
        one_head(head)
    own_ref[:, 0] = grads_out[: n // 2]
    their_ref[:, 0] = grads_out[n // 2 :]


def attend_back(info, bases, queries, grad_out, dots, logs, chunks, acc=None, finish=True):
    seqs, span, width = queries.shape
    n_heads = width // 256
    n = len(chunks)
    q_spec = pl.BlockSpec((1, span, width), lambda b, *_: (b, 0, 0))
    acc_spec = pl.BlockSpec((1, n_heads, 128, 2 * span), lambda b, *_: (b, 0, 0, 0))
    acc_shape = jax.ShapeDtypeStruct((seqs, n_heads, 128, 2 * span), f32)
    args = [queries, grad_out, dots, logs, *chunks]
    in_specs = [q_spec] * 4 + [any_spec] * n
    if acc is not None:
        args.append(acc)
        in_specs.append(acc_spec)
    kv_width = chunks[0].shape[2]
    if finish:
        dq_shape, dq_spec = jax.ShapeDtypeStruct(queries.shape, bf16), q_spec
    else:
        dq_shape, dq_spec = acc_shape, acc_spec
    grad_shape = jax.ShapeDtypeStruct((n // 2, seqs, span, kv_width), bf16)
    grad_spec = pl.BlockSpec((n // 2, 1, span, kv_width), lambda b, *_: (0, b, 0, 0))
    return pl.pallas_call(
        functools.partial(attend_back_kernel, n, acc is not None, finish),
        grid_spec=pltpu.PrefetchScalarGridSpec(
            num_scalar_prefetch=1,
            grid=(seqs,),
            in_specs=in_specs,
            out_specs=[grad_spec, grad_spec, dq_spec],
            scratch_shapes=[
                pltpu.VMEM((2, n, span, kv_width), bf16),
                pltpu.SemaphoreType.DMA((2, n)),
                pltpu.VMEM((128, 2 * span), f32),
                pltpu.VMEM((2 * span, 256), bf16),
                pltpu.VMEM((2 * span, 256), bf16),
                pltpu.VMEM((n, span, kv_width), bf16),
            ],
        ),
        out_shape=[grad_shape, grad_shape, dq_shape],
        compiler_params=params(1),
        cost_estimate=pl.CostEstimate(
            flops=10 * 4 * seqs * span * width * span * n,
            bytes_accessed=4 * seqs * (span * width * 4 + span * n * width),
            transcendentals=seqs * span * width // 64 * span * n,
        ),
    )(jnp.concatenate([info, bases]), *args)


def unproject_kernel(
    head_dim,
    info_ref,
    grad_ref,
    raw_ref,
    scale_ref,
    gain_ref,
    cos_ref,
    sa_ref,
    sb_ref,
    out_ref,
    sum_ref,
):
    @pl.when(pl.program_id(0) == 0)
    def _():
        sum_ref[...] = jnp.zeros(sum_ref.shape, f32)

    alive = info_ref[0] < info_ref[1 + pl.program_id(0)]

    @pl.when(jnp.logical_not(alive))
    def _():
        out_ref[...] = jnp.zeros(out_ref.shape, out_ref.dtype)

    @pl.when(alive)
    def _():
        scale = scale_ref[:, :1]
        mean_matrix = group_matrix(head_dim, 1.0 / head_dim)
        normed = raw_ref.shape[1]
        for slab in range(normed // 128):
            lanes = slice(128 * slab, 128 * slab + 128)
            raw = raw_ref[:, lanes].astype(f32)
            inverse = lax.rsqrt(group_sum(raw * raw, mean_matrix) + norm_eps)
            unit = raw * inverse
            turned = turn_back(grad_ref[:, lanes].astype(f32), cos_ref, sa_ref, sb_ref)
            sum_ref[...] += jnp.broadcast_to(
                jnp.sum(turned * unit, axis=0, keepdims=True), sum_ref.shape
            )
            inner = turned * gain_ref[...]
            mean = group_sum(inner * unit, mean_matrix)
            out_ref[:, lanes] = (inverse * (inner - unit * mean) * scale).astype(bf16)
        if normed < grad_ref.shape[1]:
            out_ref[:, normed:] = (grad_ref[:, normed:].astype(f32) * scale).astype(bf16)


def unproject(info, grad, raw, scale, gain, tables, head_dim):
    rows, width = grad.shape
    span = tables[0].shape[0]
    row_block = lambda a: pl.BlockSpec((span, a.shape[1]), lambda i, *_: (i, 0))
    fixed = lambda a: pl.BlockSpec(a.shape, lambda i, *_: (0,) * a.ndim)
    return pl.pallas_call(
        functools.partial(unproject_kernel, head_dim),
        grid_spec=pltpu.PrefetchScalarGridSpec(
            num_scalar_prefetch=1,
            grid=(rows // span,),
            in_specs=[row_block(a) for a in (grad, raw, scale)]
            + [fixed(a) for a in (gain, *tables)],
            out_specs=[row_block(grad), pl.BlockSpec((8, 128), lambda i, *_: (0, 0))],
        ),
        out_shape=[
            jax.ShapeDtypeStruct((rows, width), bf16),
            jax.ShapeDtypeStruct((8, 128), f32),
        ],
        compiler_params=params(1),
        cost_estimate=pl.CostEstimate(
            flops=8 * 128 * rows * width,
            bytes_accessed=6 * rows * width,
            transcendentals=rows * width,
        ),
    )(info, grad, raw, scale, gain, *tables)


def feed_kernel(
    grid,
    span,
    split,
    info_ref,
    place_ref,
    tok_ref,
    heads_ref,
    cot_ref,
    *rest,
):
    pieces, rest = rest[:8], rest[8:]
    out_ref, hidden_ref, mid_ref, dgu_ref, dmid_ref, dheads_ref, dots_ref, *rest = rest
    w_out, w_gu, w_down, out_sems, gu_sems, down_sems = rest
    a, b = split
    out_loads = lambda: loads(grid, place_ref, pieces, w_out, out_sems, (0, a))
    gu_loads = lambda: loads(grid, place_ref, pieces, w_gu, gu_sems, (2 * a, 2 * a + b))
    down_loads = lambda: loads(grid, place_ref, pieces, w_down, down_sems, (a, 2 * a))

    @pl.when(pl.program_id(0) == 0)
    def _():
        load_all(out_loads() + gu_loads() + down_loads())

    rows = tok_ref.shape[0]
    middle = tok_ref[...].astype(f32) + mm(heads_ref[...], w_out[...], NT)
    middle_low = middle.astype(bf16)
    mid_ref[...] = middle_low
    scale = lax.rsqrt(jnp.mean(middle * middle, axis=-1, keepdims=True) + norm_eps)
    gate_up = mm(middle_low, w_gu[...]) * scale
    half = gate_up.shape[1] // 2
    gate, up = gate_up[:, :half], gate_up[:, half:]
    sig = 1.0 / (1.0 + jnp.exp(-gate))
    silu = gate * sig
    hidden = silu * up
    hidden_low = hidden.astype(bf16)
    out_ref[...] = (middle + mm(hidden_low, w_down[...], NT)).astype(bf16)

    first = pl.program_id(0) * (rows // span)
    count = rows // span
    longest = info_ref[1 + first]
    for k in range(1, count):
        longest = jnp.maximum(longest, info_ref[1 + first + k])
    alive = info_ref[0] < longest

    @pl.when(alive)
    def _():
        position = lax.broadcasted_iota(jnp.int32, (span, 1), 0) + info_ref[0]
        valid = jnp.concatenate(
            [(position < info_ref[1 + first + k]).astype(f32) for k in range(count)], axis=0
        )
        hidden_ref[...] = (hidden * valid).astype(bf16)
        cot = cot_ref[...].astype(f32) * valid
        grad_hidden = mm(cot.astype(bf16), w_down[...])
        grad_gate = grad_hidden * up * (sig * (1.0 + gate * (1.0 - sig))) * scale
        grad_up = grad_hidden * silu * scale
        grad_gu = jnp.concatenate([grad_gate.astype(bf16), grad_up.astype(bf16)], axis=1)
        dgu_ref[...] = grad_gu
        back = mm(grad_gu, w_gu[...], NT)
        unit = middle * scale
        grad_mid = cot + back - unit * jnp.mean(back * unit, axis=-1, keepdims=True)
        grad_mid = grad_mid.astype(bf16)
        dmid_ref[...] = grad_mid
        grad_heads = mm(grad_mid, w_out[...]).astype(bf16)
        dheads_ref[...] = grad_heads
        ones = group_matrix(64, 1.0)
        for slab in range(a // 128):
            lanes = slice(128 * slab, 128 * slab + 128)
            product = grad_heads[:, lanes].astype(f32) * heads_ref[:, lanes].astype(f32)
            dots_ref[:, lanes] = split_lanes(-group_sum(product, ones))

    @pl.when(jnp.logical_not(alive))
    def _():
        for ref in (hidden_ref, dgu_ref, dmid_ref, dheads_ref, dots_ref):
            ref[...] = jnp.zeros(ref.shape, ref.dtype)


def feed(grid, info, tokens, heads, cotangent, pieces, split, span):
    rows, width = tokens.shape
    a, b = split
    tile = max(span, min(256, rows))
    block = lambda n: pl.BlockSpec((tile, n), lambda i, *_: (i, 0))
    shape = lambda n: jax.ShapeDtypeStruct((rows, n), bf16)
    n = n_loads(grid)
    outs = (width, a, width, b, width, a, a)
    macs = width * (2 * a + b)
    return pl.pallas_call(
        functools.partial(feed_kernel, grid, span, split),
        grid_spec=pltpu.PrefetchScalarGridSpec(
            num_scalar_prefetch=2,
            grid=(rows // tile,),
            in_specs=[block(width), block(a), block(width)] + [any_spec] * 8,
            out_specs=[block(n) for n in outs],
            scratch_shapes=[
                pltpu.VMEM((width, a), bf16),
                pltpu.VMEM((width, b), bf16),
                pltpu.VMEM((width, a), bf16),
                pltpu.SemaphoreType.DMA((n,)),
                pltpu.SemaphoreType.DMA((n,)),
                pltpu.SemaphoreType.DMA((n,)),
            ],
        ),
        out_shape=[shape(n) for n in outs],
        compiler_params=params(1),
        cost_estimate=pl.CostEstimate(
            flops=6 * rows * macs,
            bytes_accessed=2 * (rows * (sum(outs) + 2 * width + a) + macs),
            transcendentals=rows * a,
        ),
    )(info, grid.place, tokens, heads, cotangent, *pieces)


def load_all(copies):
    for copy in copies:
        copy.start()
    for copy in copies:
        copy.wait()


def query_back_kernel(grid, info_ref, place_ref, grad_ref, *rest):
    pieces, (out_ref, weight, sems) = rest[:2], rest[2:]

    @pl.when(pl.program_id(0) == 0)
    def _():
        load_all(loads(grid, place_ref, pieces, weight, sems))

    @pl.when(info_ref[0] < info_ref[1 + pl.program_id(0)])
    def _():
        out_ref[...] = mm(grad_ref[...], weight[...], NT)


def query_back(grid, info, grad, pieces, width, span):
    rows, inner = grad.shape
    return pl.pallas_call(
        functools.partial(query_back_kernel, grid),
        grid_spec=pltpu.PrefetchScalarGridSpec(
            num_scalar_prefetch=2,
            grid=(rows // span,),
            in_specs=[pl.BlockSpec((span, inner), lambda i, *_: (i, 0))] + [any_spec] * 2,
            out_specs=pl.BlockSpec((span, width), lambda i, *_: (i, 0)),
            scratch_shapes=[
                pltpu.VMEM((width, inner), bf16),
                pltpu.SemaphoreType.DMA((n_loads(grid),)),
            ],
        ),
        out_shape=jax.ShapeDtypeStruct((rows, width), f32),
        compiler_params=params(1),
        cost_estimate=pl.CostEstimate(
            flops=2 * rows * width * inner,
            bytes_accessed=2 * (rows * (2 * width + inner) + width * inner),
            transcendentals=0,
        ),
    )(info, grid.place, grad, *pieces)


def last_kernel(grid, info_ref, place_ref, tok_ref, grad_ref, back_ref, dmid_ref, scale_ref, *rest):
    pieces, (out_ref, weight, sems) = rest[:2], rest[2:]

    @pl.when(pl.program_id(0) == 0)
    def _():
        load_all(loads(grid, place_ref, pieces, weight, sems))

    alive = info_ref[0] < info_ref[1 + pl.program_id(0)]

    @pl.when(alive)
    def _():
        back = back_ref[...] + mm(grad_ref[...], weight[...], NT)
        unit = tok_ref[...].astype(f32) * scale_ref[:, :1]
        grad = dmid_ref[...].astype(f32) + back
        grad = grad - unit * jnp.mean(back * unit, axis=-1, keepdims=True)
        out_ref[...] = grad.astype(bf16)

    @pl.when(jnp.logical_not(alive))
    def _():
        out_ref[...] = jnp.zeros(out_ref.shape, out_ref.dtype)


def last(grid, info, tokens, grad_kv, back, grad_mid, scale, pieces, span):
    rows, width = tokens.shape
    block = lambda a: pl.BlockSpec((span, a.shape[1]), lambda i, *_: (i, 0))
    inner = grad_kv.shape[1]
    args = (tokens, grad_kv, back, grad_mid, scale)
    return pl.pallas_call(
        functools.partial(last_kernel, grid),
        grid_spec=pltpu.PrefetchScalarGridSpec(
            num_scalar_prefetch=2,
            grid=(rows // span,),
            in_specs=[block(a) for a in args] + [any_spec] * 2,
            out_specs=block(tokens),
            scratch_shapes=[
                pltpu.VMEM((width, inner), bf16),
                pltpu.SemaphoreType.DMA((n_loads(grid),)),
            ],
        ),
        out_shape=jax.ShapeDtypeStruct(tokens.shape, bf16),
        compiler_params=params(1),
        cost_estimate=pl.CostEstimate(
            flops=2 * rows * width * inner,
            bytes_accessed=2 * (rows * (5 * width + inner) + width * inner),
            transcendentals=0,
        ),
    )(info, grid.place, *args, *pieces)


def weight_kernel(grid, shard, span, n_pairs, place_ref, info_ref, *refs):
    lefts, rights = refs[:n_pairs], refs[n_pairs : 2 * n_pairs]
    mine_ref, theirs_ref, acc = refs[2 * n_pairs :]
    core = place_ref[2]
    middle = grid.depth // 2
    n_seqs = lefts[0].shape[0] // span
    shortest = info_ref[1]
    for seq in range(1, n_seqs):
        shortest = jnp.minimum(shortest, info_ref[1 + seq])
    all_alive = info_ref[0] < shortest
    column = 0
    for left, right in zip(lefts, rights):
        width = right.shape[1]

        @pl.when(all_alive)
        def _(left=left, right=right, width=width):
            acc[:, :width] = mm(left[...], right[...], TN)

        @pl.when(jnp.logical_not(all_alive))
        def _(left=left, right=right, width=width):
            acc[:, :width] = jnp.zeros((acc.shape[0], width), f32)
            for seq in range(n_seqs):
                rows = slice(seq * span, (seq + 1) * span)

                @pl.when(info_ref[0] < info_ref[1 + seq])
                def _(rows=rows):
                    acc[:, :width] += mm(left[rows, :], right[rows, :], TN)

        for level in range(grid.depth):
            half, at = level // middle, level % middle
            for whose, ref in ((core, mine_ref), (1 - core, theirs_ref)):
                start = pl.multiple_of((level * 2 + whose) * shard, shard)
                ref[half, 0, at, :, column : column + width] = acc[
                    pl.ds(start, shard), :width
                ].astype(bf16)
        column += width


def weight_grad(grid, info, span, *pairs):
    lefts, rights = [p[0] for p in pairs], [p[1] for p in pairs]
    rows, features = lefts[0].shape
    widths = [r.shape[1] for r in rights]
    total = sum(widths)
    part = features // grid.rows
    shard = part // grid.seqs
    middle = grid.depth // 2
    shape = jax.ShapeDtypeStruct((2, grid.rows, middle, shard, total), bf16)
    piece = pl.BlockSpec((2, 1, middle, shard, total), lambda i, *_: (0, i, 0, 0, 0))
    return pl.pallas_call(
        functools.partial(weight_kernel, grid, shard, span, len(pairs)),
        grid_spec=pltpu.PrefetchScalarGridSpec(
            num_scalar_prefetch=2,
            grid=(grid.rows,),
            in_specs=[pl.BlockSpec((rows, part), lambda i, place, info: (0, place[0] ^ i))]
            * len(pairs)
            + [pl.BlockSpec(r.shape, lambda i, *_: (0, 0)) for r in rights],
            out_specs=[piece, piece],
            scratch_shapes=[pltpu.VMEM((part, max(widths)), f32)],
        ),
        out_shape=[shape, shape],
        compiler_params=params(1),
        cost_estimate=pl.CostEstimate(
            flops=2 * rows * features * total,
            bytes_accessed=2 * (rows * (features * len(pairs) + total) + features * total),
            transcendentals=0,
        ),
    )(grid.place, info, *lefts, *rights)


def shards(
    n_rows,
    n_seqs,
    tokens,
    lengths,
    cotangent,
    w_qkv,
    w_out,
    w_gateup,
    w_down,
    norm_attn,
    norm_ffn,
    q_gain,
    k_gain,
):
    grid = Grid(n_rows, n_seqs)
    seq_count, span_len, model_width = tokens.shape
    row_count = seq_count * span_len
    head_dim = q_gain.shape[0]
    half_dim = head_dim // 2
    query_width = w_out.shape[1]
    kv_width = (w_qkv.shape[1] - query_width) // 2
    log2_scale = math.log2(math.e) * head_dim ** (-0.5)

    offset = (grid.seq * span_len).astype(jnp.int32)
    positions = offset + jnp.arange(span_len, dtype=jnp.int32)
    inverse = theta_base ** (-jnp.arange(half_dim, dtype=f32) * 2.0 / head_dim)
    angles = positions.astype(f32)[:, None] * inverse[None, :]
    cosine, sine = jnp.cos(angles), jnp.sin(angles)
    nothing = jnp.zeros_like(sine)
    tables = (
        jnp.concatenate([cosine] * 4, axis=1),
        jnp.concatenate([-sine, nothing] * 2, axis=1),
        jnp.concatenate([nothing, sine] * 2, axis=1),
    )
    q_gain_f = jnp.concatenate([q_gain.astype(f32)] * 2)[None, :]
    k_gain_f = jnp.concatenate([k_gain.astype(f32)] * 2)[None, :]
    info = jnp.concatenate([offset[None], lengths])

    attn_gain = norm_attn.astype(f32)[:, None]
    ffn_gain = norm_ffn.astype(f32)[:, None]
    qkv_shard = (w_qkv.astype(f32) * attn_gain).astype(bf16)
    gateup_shard = (w_gateup.astype(f32) * ffn_gain).astype(bf16)

    order = Order()
    depth = grid.depth
    split = max(1, depth // 2)
    kv_steps = grid.ring(qkv_shard[:, query_width:])
    kv_own, kv_came = grid.spread(kv_steps)
    q_steps = grid.ring(qkv_shard[:, :query_width], [[kv_steps[1]], [kv_steps[-1]]])[:3]
    feed_steps = grid.ring(
        jnp.concatenate([w_out, w_down, gateup_shard], axis=1), [[kv_steps[2]], kv_came[-1]]
    )[:3]
    kv_pieces = grid.with_partner(kv_own, feed_steps[1], q_steps[1])

    rows_in = tokens.reshape(row_count, model_width)
    kv, k_raw, scale1 = project(grid, rows_in, kv_pieces, k_gain_f, tables, kv_width, head_dim)
    order.leave(kv)
    while len(feed_steps) < depth:
        feed_steps.append(grid.around(after(feed_steps[-1], kv)))
        q_steps.append(grid.around(after(q_steps[-1], kv)))
    q_own, q_came = grid.spread(q_steps, [[kv]] + [feed_steps[2:3]] * (len(grid.orders[0]) - 1))
    feed_own, feed_came = grid.spread(feed_steps, [q_came[-1]])
    kv = kv.reshape(seq_count, span_len, 2 * kv_width)
    reach = [kv]
    for _ in range(split):
        reach.append(grid.up(reach[-1]))
    q_pieces = grid.with_partner(q_own, reach[1], feed_steps[-1])
    q, q_raw = project(
        grid,
        order.enter(rows_in),
        q_pieces,
        q_gain_f * log2_scale,
        tables,
        query_width,
        head_dim,
        scale1,
    )
    order.leave(q)
    q = q.reshape(seq_count, span_len, query_width)
    bases = []
    for step in range(depth):
        level = grid.level - step
        start = jnp.stack([level * 2 + grid.core, level * 2 + 1 - grid.core]) * span_len
        bases.append(jnp.where(level >= 0, start, -1).astype(jnp.int32))
    reach[split - 1] = order.late(reach[split - 1])
    crossed = [grid.partner(own) for own in reach[:split]]
    order.pin(*feed_came[0])
    feed_held = [grid.partner(order.late(feed_own[k])) for k in (0, 2)]
    near = [c for pair in zip(reach, crossed) for c in pair]
    acc = attend(info, jnp.concatenate(bases[:split]), order.enter(q), near, None, False)
    order.leave(acc)
    for step in range(split, depth):
        final = step == depth - 1
        reach[step] = order.late(reach[step])
        if final:
            order.pin(*feed_came[-1], *feed_held)
            feed_found = [grid.partner(order.late(feed_own[k])) for k in (1, 3)]
        else:
            reach.append(grid.up(reach[step]))
            order.pin(reach[step])
        crossed.append(grid.partner(reach[step]))
        result = attend(
            info, bases[step], order.enter(q), [reach[step], crossed[step]], acc, final
        )
        acc = result
        order.leave(result[0] if final else acc)
    heads, logs = result
    attended = heads.reshape(row_count, query_width)
    feed_pieces = feed_own + [feed_held[0], feed_found[0], feed_held[1], feed_found[1]]

    flat_cot = cotangent.reshape(row_count, model_width)
    output, hidden, middle, grad_gu, grad_mid, grad_heads, dots = feed(
        grid,
        info,
        rows_in,
        attended,
        flat_cot,
        feed_pieces,
        (query_width, w_gateup.shape[1]),
        span_len,
    )
    order.leave(hidden)
    grad_heads = grad_heads.reshape(seq_count, span_len, query_width)
    dots = dots.reshape(seq_count, span_len, query_width)

    def advance(*sums):
        for each in sums:
            order.pin(*each.land())
            order.pin(*each.go())

    kv_flight = []

    def kv_sum_here(own, other):
        kv_flight[:] = [order.late(came) for came in kv_flight]
        here = own.astype(f32) + other.astype(f32)
        for came in kv_flight:
            here = here + came.astype(f32)
        return here.astype(bf16)

    def kv_hop(own, other):
        sent = order.late(kv_sum_here(own, other))
        order.pin(sent)
        order.kernel = sent
        kv_flight[:] = [grid.down(sent)]

    def back(steps, acc, final):
        chosen = [reach[k] for k in steps] + [crossed[k] for k in steps]
        starts = jnp.stack([bases[k] for k in steps], axis=1).reshape(-1)
        return attend_back(
            info, starts, order.enter(q), grad_heads, dots, logs, chosen, acc, final
        )

    feed_sum = Sum(
        grid,
        order,
        weight_grad(
            grid,
            info,
            span_len,
            (flat_cot, order.enter(hidden)),
            (middle, grad_gu),
            (grad_mid, attended),
        ),
    )
    order.leave(feed_sum.theirs)
    advance(feed_sum)
    far_own, far_theirs, acc_q = back(range(split, depth), None, False)
    order.leave(acc_q)
    far_came = grid.partner(far_theirs)
    kv_hop(far_own[-1], far_came[-1])
    advance(feed_sum)
    near_own, near_theirs, grad_q = back(range(split), acc_q, True)
    order.leave(grad_q)
    near_came = grid.partner(order.late(near_theirs))
    for step in reversed(range(split, depth - 1)):
        kv_hop(far_own[step - split], far_came[step - split])
    advance(feed_sum)
    grad_pq, gq = unproject(
        info,
        order.enter(grad_q.reshape(row_count, query_width)),
        q_raw,
        scale1,
        q_gain_f,
        tables,
        head_dim,
    )
    order.leave(grad_pq)
    q_sum = Sum(
        grid, order, weight_grad(grid, info, span_len, (rows_in, order.enter(grad_pq))), True
    )
    order.leave(q_sum.theirs)
    for step in reversed(range(1, split)):
        kv_hop(near_own[step], near_came[step])
    advance(feed_sum, q_sum)
    back_q = query_back(grid, info, order.enter(grad_pq), q_pieces, model_width, span_len)
    order.leave(back_q)
    advance(feed_sum, q_sum)
    grad_kv = kv_sum_here(near_own[0], near_came[0]).reshape(row_count, 2 * kv_width)
    grad_pkv, gk = unproject(
        info, order.enter(grad_kv), k_raw, scale1, k_gain_f, tables, head_dim
    )
    kv_sum = Sum(grid, order, weight_grad(grid, info, span_len, (rows_in, grad_pkv)), True)
    order.leave(kv_sum.theirs)
    gain_sum = Everywhere(grid, order, jnp.concatenate([gq[:1], gk[:1]], axis=0))
    advance(feed_sum, q_sum, kv_sum, gain_sum)
    grad_tokens = last(
        grid,
        info,
        rows_in,
        order.enter(grad_pkv),
        back_q,
        grad_mid,
        scale1,
        kv_pieces,
        span_len,
    )
    order.leave(grad_tokens)
    gains = gain_sum.finish()
    gains = gains[:, :head_dim] + gains[:, head_dim:]
    kv_total, q_total, feed_total = kv_sum.finish(), q_sum.finish(), feed_sum.finish()
    sum_qkv = jnp.concatenate([q_total, kv_total], axis=1)
    sum_down, sum_gateup = feed_total[:, :query_width], feed_total[:, query_width:-query_width]
    sum_out = feed_total[:, -query_width:]
    return (
        output.reshape(tokens.shape),
        grad_tokens.reshape(tokens.shape),
        sum_qkv * attn_gain,
        sum_out,
        sum_gateup * ffn_gain,
        sum_down,
        jnp.sum(sum_qkv * w_qkv.astype(f32), axis=1),
        jnp.sum(sum_gateup * w_gateup.astype(f32), axis=1),
        gains[0],
        gains[1],
    )


def solution(mesh):
    rows = P("row", "seq", None)
    weight = P(both, None)
    vector = P(both)
    return jax.shard_map(
        functools.partial(shards, mesh.shape["row"], mesh.shape["seq"]),
        mesh=mesh,
        in_specs=(rows, P("row"), rows, weight, weight, weight, weight, vector, vector, P(), P()),
        out_specs=(rows, rows, weight, weight, weight, weight, vector, vector, P(), P()),
        check_vma=False,
    )
```

```python
import functools
import math

import jax
import jax.numpy as jnp
from jax import lax
from jax.experimental import pallas as pl
from jax.experimental.pallas import tpu as pltpu
from jax.sharding import PartitionSpec as P

norm_eps = 1e-06
theta_base = 10000.0
both = ("row", "seq")
f32 = jnp.float32
bf16 = jnp.bfloat16
vmem_cap = 56 * 1024 * 1024
any_spec = pl.BlockSpec(memory_space=pl.ANY)
NN = (((1,), (0,)), ((), ()))
NT = (((1,), (1,)), ((), ()))
TN = (((0,), (0,)), ((), ()))


def mm(left, right, dims=NN):
    return lax.dot_general(left, right, dims, preferred_element_type=f32)


def after(value, *earlier):
    return lax.optimization_barrier((value, *earlier))[0]


def params(n_grid):
    return pltpu.CompilerParams(
        dimension_semantics=("arbitrary",) * n_grid, vmem_limit_bytes=vmem_cap
    )


def lane_iota(shape):
    return lax.broadcasted_iota(jnp.int32, shape, len(shape) - 1)


def group_matrix(head_dim, value):
    i = lax.broadcasted_iota(jnp.int32, (128, 128), 0) // head_dim
    j = lax.broadcasted_iota(jnp.int32, (128, 128), 1) // head_dim
    return jnp.where(i == j, value, 0.0).astype(bf16)


def group_sum(values, matrix):
    high = values.astype(bf16)
    low = (values - high.astype(f32)).astype(bf16)
    return mm(high, matrix) + mm(low, matrix)


def turn(values, cos_ref, sa_ref, sb_ref):
    return (
        values * cos_ref[...]
        + pltpu.roll(values, 96, 1) * sa_ref[...]
        + pltpu.roll(values, 32, 1) * sb_ref[...]
    )


def turn_back(values, cos_ref, sa_ref, sb_ref):
    return (
        values * cos_ref[...]
        - pltpu.roll(values, 96, 1) * sa_ref[...]
        - pltpu.roll(values, 32, 1) * sb_ref[...]
    )


class Grid:
    def __init__(self, rows, seqs):
        self.rows, self.seqs, self.depth = rows, seqs, seqs // 2
        self.row = lax.axis_index("row")
        seq = lax.axis_index("seq")
        self.level, self.core = seq // 2, lax.rem(seq, 2)
        self.seq = seq
        bits = [1 << k for k in range(rows.bit_length() - 1)]
        self.orders = (bits, bits[::-1])
        self.place = jnp.stack([self.row, self.level, self.core]).astype(jnp.int32)

    def move(self, value, where):
        pairs = []
        for row in range(self.rows):
            for seq in range(self.seqs):
                target = where(row, seq)
                if target is not None:
                    pairs.append((row * self.seqs + seq, target[0] * self.seqs + target[1]))
        return lax.ppermute(value, both, pairs)

    def across(self, value, mask):
        return self.move(value, lambda r, s: (r ^ mask, s))

    def partner(self, value):
        return self.move(value, lambda r, s: (r, s ^ 1))

    def around(self, value, steps=1):
        return self.move(value, lambda r, s: (r, (s + 2 * steps) % self.seqs))

    def up(self, value):
        return self.move(value, lambda r, s: (r, s + 2) if s + 2 < self.seqs else None)

    def down(self, value):
        return self.move(value, lambda r, s: (r, s - 2) if s >= 2 else None)

    def masks(self, half):
        found = [0]
        for bit in self.orders[half]:
            found = found + [m ^ bit for m in found]
        return found

    def ring(self, shard, waits=()):
        steps = [shard]
        for hop in range(self.depth - 1):
            held = steps[-1]
            if hop < len(waits):
                held = after(held, *waits[hop])
            steps.append(self.around(held))
        return steps

    def spread(self, steps, waits=()):
        middle = self.depth // 2
        held = [jnp.stack(steps[:middle])[None], jnp.stack(steps[middle:])[None]]
        pieces = []
        arrived = []
        for stage in range(len(self.orders[0])):
            for half in range(2):
                if stage < len(waits):
                    held[half] = after(held[half], *waits[stage])
            found = [self.across(held[half], self.orders[half][stage]) for half in range(2)]
            arrived.append(found)
            if stage == len(self.orders[0]) - 1:
                pieces = [held[0], found[0], held[1], found[1]]
            else:
                held = [jnp.concatenate([held[k], found[k]], axis=0) for k in range(2)]
        return pieces, arrived

    def with_partner(self, pieces, *waits):
        pieces = jnp.stack(pieces)
        return [pieces, self.partner(after(pieces, *waits) if waits else pieces)]


class Order:
    def __init__(self):
        self.kernel = None
        self.waits = []

    def pin(self, *values):
        self.waits += values

    def enter(self, value):
        return after(value, *self.waits) if self.waits else value

    def leave(self, value):
        self.kernel = value
        self.waits = [value]

    def late(self, value):
        return after(value, self.kernel)


class Everywhere:
    def __init__(self, grid, order, value):
        self.grid, self.order, self.total = grid, order, value
        self.flight = []
        self.moves = [(bit, 0) for bit in grid.orders[0]]
        self.moves += [(0, 1 << k) for k in range(grid.seqs.bit_length() - 1)]

    def land(self):
        came, self.flight = [self.order.late(c) for c in self.flight], []
        for each in came:
            self.total = self.total + each
        return came

    def go(self):
        self.land()
        if not self.moves:
            return []
        row, seq = self.moves.pop(0)
        sent = self.order.late(self.total)
        self.flight = [self.grid.move(sent, lambda r, s: (r ^ row, s ^ seq))]
        return [sent]

    def finish(self):
        while self.go():
            pass
        return self.total


class Sum:
    def __init__(self, grid, order, parts, direct=False):
        mine, self.theirs = parts
        self.direct = direct
        self.grid = grid
        self.order = order
        self.halves = [[mine[half]] for half in range(2)]
        self.stage = 0
        self.flight = []
        self.row_stages = len(grid.orders[0])
        self.total = None

    def at(self, step):
        depth = self.grid.depth
        index = lax.rem(self.grid.level - step + 2 * depth, depth)
        return lax.dynamic_index_in_dim(self.levels, index, 0, keepdims=False)

    def land(self):
        came, self.flight = [self.order.late(c) for c in self.flight], []
        if came:
            if self.stage == 1:
                for half in range(2):
                    self.halves[half].append(came[0][half])
            elif self.stage <= 1 + self.row_stages:
                for half in range(2):
                    self.halves[half].append(came[half])
            elif self.direct:
                self.total = self.total + sum(c.astype(f32) for c in came)
            else:
                self.total = came[0].astype(f32) + self.at(self.stage - self.row_stages)
        return came

    def go(self):
        grid, late = self.grid, self.order.late
        self.land()
        if self.stage == 0:
            sent = [self.theirs]
            self.flight = [grid.partner(self.theirs)]
        elif self.stage <= self.row_stages:
            sent = []
            for half in range(2):
                parts = self.halves[half]
                bit = grid.orders[half][::-1][self.stage - 1]
                count = parts[0].shape[0] // 2
                if half == 0:
                    kept, given = slice(0, count), slice(count, None)
                else:
                    kept, given = slice(0, None, 2), slice(1, None, 2)
                value = sum(p[given].astype(f32) for p in parts).astype(bf16)
                self.halves[half] = [p[kept] for p in parts]
                sent.append(late(value))
                self.flight.append(grid.across(sent[half], bit))
        elif self.direct:
            if self.total is not None:
                return []
            self.levels = jnp.concatenate(
                [sum(p[0].astype(f32) for p in parts) for parts in self.halves], axis=0
            )
            self.total = self.at(0)
            sent = [
                late(self.at(grid.depth - step).astype(bf16)) for step in range(1, grid.depth)
            ]
            self.flight = [grid.around(each, k + 1) for k, each in enumerate(sent)]
        elif self.stage < self.row_stages + grid.depth:
            if self.total is None:
                self.levels = jnp.concatenate(
                    [sum(p[0].astype(f32) for p in parts) for parts in self.halves], axis=0
                )
                self.total = self.at(1)
            sent = [late(self.total.astype(bf16))]
            self.flight = [grid.around(sent[0])]
        else:
            return []
        self.stage += 1
        return sent

    def finish(self):
        while self.go():
            pass
        return self.total


def loads(grid, place_ref, pieces, target, sems, columns=None, at_column=0):
    row, level, core = place_ref[0], place_ref[1], place_ref[2]
    shard, columns_all = pieces[0].shape[-2:]
    if columns is None:
        columns = (0, columns_all)
    width = columns[1] - columns[0]
    merged = len(pieces) == 2
    copies = []
    for which in range(8):
        ref = pieces[which // 4].at[which % 4] if merged else pieces[which]
        half = which // 2 % 2
        whose = core if which < 4 else 1 - core
        first = 0 if half == 0 else grid.depth // 2
        masks = grid.masks(half)
        masks = masks[len(masks) // 2 :] if which % 2 else masks[: len(masks) // 2]
        for m, mask in enumerate(masks):
            for h in range(ref.shape[1]):
                at_level = lax.rem(level - (first + h) + grid.depth, grid.depth)
                start = ((row ^ mask) * grid.seqs + at_level * 2 + whose) * shard
                copies.append(
                    pltpu.make_async_copy(
                        ref.at[m, h, :, columns[0] : columns[1]],
                        target.at[
                            pl.ds(pl.multiple_of(start, shard), shard),
                            at_column : at_column + width,
                        ],
                        sems.at[len(copies)],
                    )
                )
    return copies


def n_loads(grid):
    return grid.rows * grid.seqs


def project_kernel(grid, normed_slabs, head_dim, with_scale, place_ref, tok_ref, *rest):
    pieces, rest = rest[:2], rest[2:]
    gain_ref, cos_ref, sa_ref, sb_ref, *rest = rest
    if with_scale:
        heads_ref, raw_ref, scale_ref, weight, sems = rest
    else:
        scale_in_ref, heads_ref, raw_ref, weight, sems = rest

    @pl.when(pl.program_id(0) == 0)
    def _():
        copies = loads(grid, place_ref, pieces, weight, sems)
        for copy in copies:
            copy.start()
        for copy in copies:
            copy.wait()

    if with_scale:
        x = tok_ref[...].astype(f32)
        scale = lax.rsqrt(jnp.mean(x * x, axis=-1, keepdims=True) + norm_eps)
        scale_ref[...] = jnp.broadcast_to(scale, scale_ref.shape)
    else:
        scale = scale_in_ref[:, :1]
    projected = mm(tok_ref[...], weight[...]) * scale
    mean_matrix = group_matrix(head_dim, 1.0 / head_dim)
    raw_ref[...] = projected[:, : raw_ref.shape[1]].astype(bf16)
    for slab in range(heads_ref.shape[1] // 128):
        lanes = slice(128 * slab, 128 * slab + 128)
        part = projected[:, lanes]
        if slab < normed_slabs:
            inverse = lax.rsqrt(group_sum(part * part, mean_matrix) + norm_eps)
            part = turn(part * inverse * gain_ref[...], cos_ref, sa_ref, sb_ref)
        heads_ref[:, lanes] = part.astype(bf16)


def project(grid, tokens, pieces, gain, tables, normed, head_dim, scale=None):
    rows, width = tokens.shape
    out_width = pieces[0].shape[-1]
    span = tables[0].shape[0]
    row_block = lambda n: pl.BlockSpec((span, n), lambda i, *_: (i, 0))
    fixed = lambda a: pl.BlockSpec(a.shape, lambda i, *_: (0,) * a.ndim)
    args = [tokens, *pieces, gain, *tables]
    in_specs = [row_block(width)] + [any_spec] * 2 + [fixed(a) for a in (gain, *tables)]
    out_shape = [
        jax.ShapeDtypeStruct((rows, out_width), bf16),
        jax.ShapeDtypeStruct((rows, normed), bf16),
    ]
    out_specs = [row_block(out_width), row_block(normed)]
    if scale is None:
        out_shape.append(jax.ShapeDtypeStruct((rows, 128), f32))
        out_specs.append(row_block(128))
    else:
        args.append(scale)
        in_specs.append(row_block(128))
    return pl.pallas_call(
        functools.partial(project_kernel, grid, normed // 128, head_dim, scale is None),
        grid_spec=pltpu.PrefetchScalarGridSpec(
            num_scalar_prefetch=1,
            grid=(rows // span,),
            in_specs=in_specs,
            out_specs=out_specs,
            scratch_shapes=[
                pltpu.VMEM((width, out_width), bf16),
                pltpu.SemaphoreType.DMA((n_loads(grid),)),
            ],
        ),
        out_shape=out_shape,
        compiler_params=params(1),
        cost_estimate=pl.CostEstimate(
            flops=4 * rows * width * out_width,
            bytes_accessed=2 * (rows * (width + 2 * out_width) + width * out_width),
            transcendentals=rows * normed,
        ),
    )(grid.place, *args)


def placed_pair(slab, parity, low):
    values = slab.astype(f32)
    rolled = pltpu.roll(values, 64, 1)
    here, there = (rolled, values) if parity else (values, rolled)
    return jnp.where(low, here, 0.0), jnp.where(low, 0.0, there)


def block_state(info_ref, seq, base, block, span):
    offset = info_ref[0]
    length = info_ref[1 + seq]
    some = (base >= 0) & (base < jnp.minimum(offset + span, length))
    whole = some & (base + block <= jnp.minimum(offset + 1, length))
    return whole, some & jnp.logical_not(whole)


def mask_bias(info_ref, seq, base, span, key_axis):
    shape = (span, span)
    behind = lax.broadcasted_iota(jnp.int32, shape, key_axis) - lax.broadcasted_iota(
        jnp.int32, shape, 1 - key_axis
    )
    key = lax.broadcasted_iota(jnp.int32, shape, key_axis)
    ok = (behind <= info_ref[0] - base) & (key < info_ref[1 + seq] - base)
    bias = jnp.where(ok, 0.0, -1e30)
    pair = jnp.concatenate([bias, bias], axis=1)
    return jnp.concatenate([pair, pair], axis=0)


def chunk_copies(chunks, buffer, sems, info_ref, seq, n_seqs, slot, span, then, backward=False):
    for i, chunk in enumerate(chunks):
        base = info_ref[1 + n_seqs + i]
        needed = (base >= 0) & (base < jnp.minimum(info_ref[0] + span, info_ref[1 + seq]))
        if backward:
            needed = needed & (info_ref[0] < info_ref[1 + seq])

        @pl.when(needed)
        def _(i=i, chunk=chunk):
            then(pltpu.make_async_copy(chunk.at[seq], buffer.at[slot, i], sems.at[slot, i]))


def fetch_chunks(chunks, buffer, sems, info_ref, span, backward=False):
    seq, n_seqs = pl.program_id(0), pl.num_programs(0)
    slot = lax.rem(seq, 2)
    common = (chunks, buffer, sems, info_ref)

    @pl.when(seq == 0)
    def _():
        chunk_copies(*common, seq, n_seqs, slot, span, lambda c: c.start(), backward)

    @pl.when(seq + 1 < n_seqs)
    def _():
        chunk_copies(*common, seq + 1, n_seqs, 1 - slot, span, lambda c: c.start(), backward)

    chunk_copies(*common, seq, n_seqs, slot, span, lambda c: c.wait(), backward)
    return slot


def stacked_at(ref, head):
    first = head * 256
    return jnp.concatenate(
        [ref[0, :, first : first + 128], ref[0, :, first + 128 : first + 256]], axis=0
    )


def unstack_to(ref, head, value):
    first = head * 256
    span = ref.shape[1]
    ref[0, :, first : first + 128] = value[:span].astype(ref.dtype)
    ref[0, :, first + 128 : first + 256] = value[span:].astype(ref.dtype)


def split_lanes(values):
    lane = lax.rem(lane_iota(values.shape), 64)
    high = values.astype(bf16).astype(f32)
    rest = values - high
    return jnp.where(lane == 0, high, jnp.where(lane == 1, rest, 0.0)).astype(bf16)


def attend_kernel(n, with_acc, finish, info_ref, q_ref, *refs):
    chunks, refs = refs[:n], refs[n:]
    if with_acc:
        acc_in, refs = refs[0], refs[1:]
    if finish:
        out_ref, log_ref, buffer, sems, acc = refs
    else:
        acc_out, buffer, sems, acc = refs
    seq, n_seqs = pl.program_id(0), pl.num_programs(0)
    span = q_ref.shape[1]
    n_heads = q_ref.shape[2] // 256
    slot = fetch_chunks(chunks, buffer, sems, info_ref, span)

    def one_head(head):
        parity = head % 2
        k_lanes = slice(head // 2 * 128, head // 2 * 128 + 128)
        v_lanes = slice((n_heads + head) // 2 * 128, (n_heads + head) // 2 * 128 + 128)
        acc[...] = acc_in[0, head] if with_acc else jnp.zeros(acc.shape, f32)

        @pl.loop(0, n)
        def _(chunk):
            base = info_ref[1 + n_seqs + chunk]
            whole, partly = block_state(info_ref, seq, base, span, span)

            def step(masked):
                low = lane_iota((span, 128)) < 64
                ones_low = jnp.where(low, 1.0, 0.0).astype(bf16)
                ones_high = jnp.where(low, 0.0, 1.0).astype(bf16)
                k0, k1 = placed_pair(buffer[slot, chunk, :, k_lanes], parity, low)
                v0, v1 = placed_pair(buffer[slot, chunk, :, v_lanes], parity, low)
                k_pair = jnp.concatenate([k0, k1], axis=0).astype(bf16)
                v_pair = jnp.concatenate(
                    [
                        jnp.concatenate([v0.astype(bf16), ones_low], axis=1),
                        jnp.concatenate([v1.astype(bf16), ones_high], axis=1),
                    ],
                    axis=0,
                )
                scores = mm(stacked_at(q_ref, head), k_pair, NT)
                if masked:
                    scores = scores + mask_bias(info_ref, seq, base, span, 1)
                weights = jnp.exp2(scores)
                acc[...] += mm(weights.astype(bf16), v_pair)

            @pl.when(whole)
            def _():
                step(False)

            @pl.when(partly)
            def _():
                step(True)

        if finish:
            totals = acc[:, 128:]
            unstack_to(out_ref, head, acc[:, :128] / totals)
            unstack_to(log_ref, head, split_lanes(-jnp.log2(totals)))
        else:
            acc_out[0, head] = acc[...]

    for head in range(n_heads):
        one_head(head)


def attend(info, bases, queries, chunks, acc=None, finish=True):
    seqs, span, width = queries.shape
    n_heads = width // 256
    n = len(chunks)
    q_spec = pl.BlockSpec((1, span, width), lambda b, *_: (b, 0, 0))
    acc_spec = pl.BlockSpec((1, n_heads, 2 * span, 256), lambda b, *_: (b, 0, 0, 0))
    acc_shape = jax.ShapeDtypeStruct((seqs, n_heads, 2 * span, 256), f32)
    args = [queries, *chunks]
    in_specs = [q_spec] + [any_spec] * n
    if acc is not None:
        args.append(acc)
        in_specs.append(acc_spec)
    if finish:
        out_shape = [jax.ShapeDtypeStruct(queries.shape, bf16)] * 2
        out_specs = [q_spec, q_spec]
    else:
        out_shape, out_specs = acc_shape, acc_spec
    return pl.pallas_call(
        functools.partial(attend_kernel, n, acc is not None, finish),
        grid_spec=pltpu.PrefetchScalarGridSpec(
            num_scalar_prefetch=1,
            grid=(seqs,),
            in_specs=in_specs,
            out_specs=out_specs,
            scratch_shapes=[
                pltpu.VMEM((2, n, span, chunks[0].shape[2]), bf16),
                pltpu.SemaphoreType.DMA((2, n)),
                pltpu.VMEM((2 * span, 256), f32),
            ],
        ),
        out_shape=out_shape,
        compiler_params=params(1),
        cost_estimate=pl.CostEstimate(
            flops=4 * 4 * seqs * span * width * span * n,
            bytes_accessed=4 * seqs * (span * width * 3 + n * span * width // 2),
            transcendentals=seqs * span * width // 64 * span * n,
        ),
    )(jnp.concatenate([info, bases]), *args)


def attend_back_kernel(n, with_acc, finish, info_ref, q_ref, do_ref, dot_ref, log_ref, *refs):
    chunks, refs = refs[:n], refs[n:]
    if with_acc:
        acc_in, refs = refs[0], refs[1:]
    own_ref, their_ref, dq_ref, buffer, sems, acc, q_wide, do_wide, grads_out = refs
    seq, n_seqs = pl.program_id(0), pl.num_programs(0)
    span = q_ref.shape[1]
    n_heads = q_ref.shape[2] // 256
    alive = info_ref[0] < info_ref[1 + seq]
    slot = fetch_chunks(chunks, buffer, sems, info_ref, span, True)
    grads_out[...] = jnp.zeros(grads_out.shape, grads_out.dtype)

    def one_head(head):
        parity = head % 2
        k_lanes = slice(head // 2 * 128, head // 2 * 128 + 128)
        v_lanes = slice((n_heads + head) // 2 * 128, (n_heads + head) // 2 * 128 + 128)
        acc[...] = acc_in[0, head] if with_acc else jnp.zeros(acc.shape, f32)

        @pl.when(alive)
        def _():
            do_wide[:, :128] = stacked_at(do_ref, head)
            do_wide[:, 128:] = stacked_at(dot_ref, head)
            q_wide[:, :128] = stacked_at(q_ref, head)
            q_wide[:, 128:] = stacked_at(log_ref, head)

            @pl.loop(0, n)
            def _(chunk):
                base = info_ref[1 + n_seqs + chunk]
                whole, partly = block_state(info_ref, seq, base, span, span)

                def step(masked):
                    low = lane_iota((span, 128)) < 64
                    half_lane = lax.rem(lane_iota((span, 128)), 64)
                    pick_low = jnp.where(low & (half_lane < 2), 1.0, 0.0)
                    pick_high = jnp.where(low | (half_lane >= 2), 0.0, 1.0)
                    picks = jnp.concatenate([pick_low, pick_high], axis=0).astype(bf16)
                    k0, k1 = placed_pair(buffer[slot, chunk, :, k_lanes], parity, low)
                    v0, v1 = placed_pair(buffer[slot, chunk, :, v_lanes], parity, low)
                    k_pair = jnp.concatenate([k0, k1], axis=0)
                    k_turned = jnp.transpose(k_pair).astype(bf16)
                    k_wide = jnp.concatenate([k_pair.astype(bf16), picks], axis=1)
                    v_wide = jnp.concatenate(
                        [jnp.concatenate([v0, v1], axis=0).astype(bf16), picks], axis=1
                    )
                    scores = mm(k_wide, q_wide[...], NT)
                    if masked:
                        scores = scores + mask_bias(info_ref, seq, base, span, 0)
                    weights = jnp.exp2(scores)
                    grads = (weights * mm(v_wide, do_wide[...], NT)).astype(bf16)
                    both_v = mm(weights.astype(bf16), do_wide[:, :128])
                    both_k = mm(grads, q_wide[:, :128]) * math.log(2.0)
                    acc[...] += mm(k_turned, grads)

                    def joined(pair):
                        total = jnp.where(low, pair[:span] + pltpu.roll(pair[span:], 64, 1), 0.0)
                        return pltpu.roll(total, 64, 1) if parity else total

                    dtype = grads_out.dtype
                    grads_out[chunk, :, k_lanes] += joined(both_k).astype(dtype)
                    grads_out[chunk, :, v_lanes] += joined(both_v).astype(dtype)

                @pl.when(whole)
                def _():
                    step(False)

                @pl.when(partly)
                def _():
                    step(True)

        if finish:
            unstack_to(dq_ref, head, jnp.transpose(acc[...]) * 0.125)
        else:
            dq_ref[0, head] = acc[...]

    for head in range(n_heads):
        one_head(head)
    own_ref[:, 0] = grads_out[: n // 2]
    their_ref[:, 0] = grads_out[n // 2 :]


def attend_back(info, bases, queries, grad_out, dots, logs, chunks, acc=None, finish=True):
    seqs, span, width = queries.shape
    n_heads = width // 256
    n = len(chunks)
    q_spec = pl.BlockSpec((1, span, width), lambda b, *_: (b, 0, 0))
    acc_spec = pl.BlockSpec((1, n_heads, 128, 2 * span), lambda b, *_: (b, 0, 0, 0))
    acc_shape = jax.ShapeDtypeStruct((seqs, n_heads, 128, 2 * span), f32)
    args = [queries, grad_out, dots, logs, *chunks]
    in_specs = [q_spec] * 4 + [any_spec] * n
    if acc is not None:
        args.append(acc)
        in_specs.append(acc_spec)
    kv_width = chunks[0].shape[2]
    if finish:
        dq_shape, dq_spec = jax.ShapeDtypeStruct(queries.shape, bf16), q_spec
    else:
        dq_shape, dq_spec = acc_shape, acc_spec
    grad_shape = jax.ShapeDtypeStruct((n // 2, seqs, span, kv_width), bf16)
    grad_spec = pl.BlockSpec((n // 2, 1, span, kv_width), lambda b, *_: (0, b, 0, 0))
    return pl.pallas_call(
        functools.partial(attend_back_kernel, n, acc is not None, finish),
        grid_spec=pltpu.PrefetchScalarGridSpec(
            num_scalar_prefetch=1,
            grid=(seqs,),
            in_specs=in_specs,
            out_specs=[grad_spec, grad_spec, dq_spec],
            scratch_shapes=[
                pltpu.VMEM((2, n, span, kv_width), bf16),
                pltpu.SemaphoreType.DMA((2, n)),
                pltpu.VMEM((128, 2 * span), f32),
                pltpu.VMEM((2 * span, 256), bf16),
                pltpu.VMEM((2 * span, 256), bf16),
                pltpu.VMEM((n, span, kv_width), bf16),
            ],
        ),
        out_shape=[grad_shape, grad_shape, dq_shape],
        compiler_params=params(1),
        cost_estimate=pl.CostEstimate(
            flops=10 * 4 * seqs * span * width * span * n,
            bytes_accessed=4 * seqs * (span * width * 4 + span * n * width),
            transcendentals=seqs * span * width // 64 * span * n,
        ),
    )(jnp.concatenate([info, bases]), *args)


def unproject_kernel(
    head_dim,
    info_ref,
    grad_ref,
    raw_ref,
    scale_ref,
    gain_ref,
    cos_ref,
    sa_ref,
    sb_ref,
    out_ref,
    sum_ref,
):
    @pl.when(pl.program_id(0) == 0)
    def _():
        sum_ref[...] = jnp.zeros(sum_ref.shape, f32)

    alive = info_ref[0] < info_ref[1 + pl.program_id(0)]

    @pl.when(jnp.logical_not(alive))
    def _():
        out_ref[...] = jnp.zeros(out_ref.shape, out_ref.dtype)

    @pl.when(alive)
    def _():
        scale = scale_ref[:, :1]
        mean_matrix = group_matrix(head_dim, 1.0 / head_dim)
        normed = raw_ref.shape[1]
        for slab in range(normed // 128):
            lanes = slice(128 * slab, 128 * slab + 128)
            raw = raw_ref[:, lanes].astype(f32)
            inverse = lax.rsqrt(group_sum(raw * raw, mean_matrix) + norm_eps)
            unit = raw * inverse
            turned = turn_back(grad_ref[:, lanes].astype(f32), cos_ref, sa_ref, sb_ref)
            sum_ref[...] += jnp.broadcast_to(
                jnp.sum(turned * unit, axis=0, keepdims=True), sum_ref.shape
            )
            inner = turned * gain_ref[...]
            mean = group_sum(inner * unit, mean_matrix)
            out_ref[:, lanes] = (inverse * (inner - unit * mean) * scale).astype(bf16)
        if normed < grad_ref.shape[1]:
            out_ref[:, normed:] = (grad_ref[:, normed:].astype(f32) * scale).astype(bf16)


def unproject(info, grad, raw, scale, gain, tables, head_dim):
    rows, width = grad.shape
    span = tables[0].shape[0]
    row_block = lambda a: pl.BlockSpec((span, a.shape[1]), lambda i, *_: (i, 0))
    fixed = lambda a: pl.BlockSpec(a.shape, lambda i, *_: (0,) * a.ndim)
    return pl.pallas_call(
        functools.partial(unproject_kernel, head_dim),
        grid_spec=pltpu.PrefetchScalarGridSpec(
            num_scalar_prefetch=1,
            grid=(rows // span,),
            in_specs=[row_block(a) for a in (grad, raw, scale)]
            + [fixed(a) for a in (gain, *tables)],
            out_specs=[row_block(grad), pl.BlockSpec((8, 128), lambda i, *_: (0, 0))],
        ),
        out_shape=[
            jax.ShapeDtypeStruct((rows, width), bf16),
            jax.ShapeDtypeStruct((8, 128), f32),
        ],
        compiler_params=params(1),
        cost_estimate=pl.CostEstimate(
            flops=8 * 128 * rows * width,
            bytes_accessed=6 * rows * width,
            transcendentals=rows * width,
        ),
    )(info, grad, raw, scale, gain, *tables)


def feed_kernel(
    grid,
    span,
    split,
    info_ref,
    place_ref,
    tok_ref,
    heads_ref,
    cot_ref,
    *rest,
):
    pieces, rest = rest[:8], rest[8:]
    out_ref, hidden_ref, mid_ref, dgu_ref, dmid_ref, dheads_ref, dots_ref, *rest = rest
    w_out, w_gu, w_down, out_sems, gu_sems, down_sems = rest
    a, b = split
    out_loads = lambda: loads(grid, place_ref, pieces, w_out, out_sems, (0, a))
    gu_loads = lambda: loads(grid, place_ref, pieces, w_gu, gu_sems, (2 * a, 2 * a + b))
    down_loads = lambda: loads(grid, place_ref, pieces, w_down, down_sems, (a, 2 * a))

    @pl.when(pl.program_id(0) == 0)
    def _():
        load_all(out_loads() + gu_loads() + down_loads())

    rows = tok_ref.shape[0]
    middle = tok_ref[...].astype(f32) + mm(heads_ref[...], w_out[...], NT)
    middle_low = middle.astype(bf16)
    mid_ref[...] = middle_low
    scale = lax.rsqrt(jnp.mean(middle * middle, axis=-1, keepdims=True) + norm_eps)
    gate_up = mm(middle_low, w_gu[...]) * scale
    half = gate_up.shape[1] // 2
    gate, up = gate_up[:, :half], gate_up[:, half:]
    sig = 1.0 / (1.0 + jnp.exp(-gate))
    silu = gate * sig
    hidden = silu * up
    hidden_low = hidden.astype(bf16)
    out_ref[...] = (middle + mm(hidden_low, w_down[...], NT)).astype(bf16)

    first = pl.program_id(0) * (rows // span)
    count = rows // span
    longest = info_ref[1 + first]
    for k in range(1, count):
        longest = jnp.maximum(longest, info_ref[1 + first + k])
    alive = info_ref[0] < longest

    @pl.when(alive)
    def _():
        position = lax.broadcasted_iota(jnp.int32, (span, 1), 0) + info_ref[0]
        valid = jnp.concatenate(
            [(position < info_ref[1 + first + k]).astype(f32) for k in range(count)], axis=0
        )
        hidden_ref[...] = (hidden * valid).astype(bf16)
        cot = cot_ref[...].astype(f32) * valid
        grad_hidden = mm(cot.astype(bf16), w_down[...])
        grad_gate = grad_hidden * up * (sig * (1.0 + gate * (1.0 - sig))) * scale
        grad_up = grad_hidden * silu * scale
        grad_gu = jnp.concatenate([grad_gate.astype(bf16), grad_up.astype(bf16)], axis=1)
        dgu_ref[...] = grad_gu
        back = mm(grad_gu, w_gu[...], NT)
        unit = middle * scale
        grad_mid = cot + back - unit * jnp.mean(back * unit, axis=-1, keepdims=True)
        grad_mid = grad_mid.astype(bf16)
        dmid_ref[...] = grad_mid
        grad_heads = mm(grad_mid, w_out[...]).astype(bf16)
        dheads_ref[...] = grad_heads
        ones = group_matrix(64, 1.0)
        for slab in range(a // 128):
            lanes = slice(128 * slab, 128 * slab + 128)
            product = grad_heads[:, lanes].astype(f32) * heads_ref[:, lanes].astype(f32)
            dots_ref[:, lanes] = split_lanes(-group_sum(product, ones))

    @pl.when(jnp.logical_not(alive))
    def _():
        for ref in (hidden_ref, dgu_ref, dmid_ref, dheads_ref, dots_ref):
            ref[...] = jnp.zeros(ref.shape, ref.dtype)


def feed(grid, info, tokens, heads, cotangent, pieces, split, span):
    rows, width = tokens.shape
    a, b = split
    tile = max(span, min(256, rows))
    block = lambda n: pl.BlockSpec((tile, n), lambda i, *_: (i, 0))
    shape = lambda n: jax.ShapeDtypeStruct((rows, n), bf16)
    n = n_loads(grid)
    outs = (width, a, width, b, width, a, a)
    macs = width * (2 * a + b)
    return pl.pallas_call(
        functools.partial(feed_kernel, grid, span, split),
        grid_spec=pltpu.PrefetchScalarGridSpec(
            num_scalar_prefetch=2,
            grid=(rows // tile,),
            in_specs=[block(width), block(a), block(width)] + [any_spec] * 8,
            out_specs=[block(n) for n in outs],
            scratch_shapes=[
                pltpu.VMEM((width, a), bf16),
                pltpu.VMEM((width, b), bf16),
                pltpu.VMEM((width, a), bf16),
                pltpu.SemaphoreType.DMA((n,)),
                pltpu.SemaphoreType.DMA((n,)),
                pltpu.SemaphoreType.DMA((n,)),
            ],
        ),
        out_shape=[shape(n) for n in outs],
        compiler_params=params(1),
        cost_estimate=pl.CostEstimate(
            flops=6 * rows * macs,
            bytes_accessed=2 * (rows * (sum(outs) + 2 * width + a) + macs),
            transcendentals=rows * a,
        ),
    )(info, grid.place, tokens, heads, cotangent, *pieces)


def load_all(copies):
    for copy in copies:
        copy.start()
    for copy in copies:
        copy.wait()


def query_back_kernel(grid, info_ref, place_ref, grad_ref, *rest):
    pieces, (out_ref, weight, sems) = rest[:2], rest[2:]

    @pl.when(pl.program_id(0) == 0)
    def _():
        load_all(loads(grid, place_ref, pieces, weight, sems))

    @pl.when(info_ref[0] < info_ref[1 + pl.program_id(0)])
    def _():
        out_ref[...] = mm(grad_ref[...], weight[...], NT)


def query_back(grid, info, grad, pieces, width, span):
    rows, inner = grad.shape
    return pl.pallas_call(
        functools.partial(query_back_kernel, grid),
        grid_spec=pltpu.PrefetchScalarGridSpec(
            num_scalar_prefetch=2,
            grid=(rows // span,),
            in_specs=[pl.BlockSpec((span, inner), lambda i, *_: (i, 0))] + [any_spec] * 2,
            out_specs=pl.BlockSpec((span, width), lambda i, *_: (i, 0)),
            scratch_shapes=[
                pltpu.VMEM((width, inner), bf16),
                pltpu.SemaphoreType.DMA((n_loads(grid),)),
            ],
        ),
        out_shape=jax.ShapeDtypeStruct((rows, width), f32),
        compiler_params=params(1),
        cost_estimate=pl.CostEstimate(
            flops=2 * rows * width * inner,
            bytes_accessed=2 * (rows * (2 * width + inner) + width * inner),
            transcendentals=0,
        ),
    )(info, grid.place, grad, *pieces)


def last_kernel(grid, info_ref, place_ref, tok_ref, grad_ref, back_ref, dmid_ref, scale_ref, *rest):
    pieces, (out_ref, weight, sems) = rest[:2], rest[2:]

    @pl.when(pl.program_id(0) == 0)
    def _():
        load_all(loads(grid, place_ref, pieces, weight, sems))

    alive = info_ref[0] < info_ref[1 + pl.program_id(0)]

    @pl.when(alive)
    def _():
        back = back_ref[...] + mm(grad_ref[...], weight[...], NT)
        unit = tok_ref[...].astype(f32) * scale_ref[:, :1]
        grad = dmid_ref[...].astype(f32) + back
        grad = grad - unit * jnp.mean(back * unit, axis=-1, keepdims=True)
        out_ref[...] = grad.astype(bf16)

    @pl.when(jnp.logical_not(alive))
    def _():
        out_ref[...] = jnp.zeros(out_ref.shape, out_ref.dtype)


def last(grid, info, tokens, grad_kv, back, grad_mid, scale, pieces, span):
    rows, width = tokens.shape
    block = lambda a: pl.BlockSpec((span, a.shape[1]), lambda i, *_: (i, 0))
    inner = grad_kv.shape[1]
    args = (tokens, grad_kv, back, grad_mid, scale)
    return pl.pallas_call(
        functools.partial(last_kernel, grid),
        grid_spec=pltpu.PrefetchScalarGridSpec(
            num_scalar_prefetch=2,
            grid=(rows // span,),
            in_specs=[block(a) for a in args] + [any_spec] * 2,
            out_specs=block(tokens),
            scratch_shapes=[
                pltpu.VMEM((width, inner), bf16),
                pltpu.SemaphoreType.DMA((n_loads(grid),)),
            ],
        ),
        out_shape=jax.ShapeDtypeStruct(tokens.shape, bf16),
        compiler_params=params(1),
        cost_estimate=pl.CostEstimate(
            flops=2 * rows * width * inner,
            bytes_accessed=2 * (rows * (5 * width + inner) + width * inner),
            transcendentals=0,
        ),
    )(info, grid.place, *args, *pieces)


def weight_kernel(grid, shard, span, n_pairs, place_ref, info_ref, *refs):
    lefts, rights = refs[:n_pairs], refs[n_pairs : 2 * n_pairs]
    mine_ref, theirs_ref, acc = refs[2 * n_pairs :]
    core = place_ref[2]
    middle = grid.depth // 2
    n_seqs = lefts[0].shape[0] // span
    shortest = info_ref[1]
    for seq in range(1, n_seqs):
        shortest = jnp.minimum(shortest, info_ref[1 + seq])
    all_alive = info_ref[0] < shortest
    column = 0
    for left, right in zip(lefts, rights):
        width = right.shape[1]

        @pl.when(all_alive)
        def _(left=left, right=right, width=width):
            acc[:, :width] = mm(left[...], right[...], TN)

        @pl.when(jnp.logical_not(all_alive))
        def _(left=left, right=right, width=width):
            first_alive = info_ref[0] < info_ref[1]

            @pl.when(first_alive)
            def _():
                acc[:, :width] = mm(left[:span, :], right[:span, :], TN)

            @pl.when(jnp.logical_not(first_alive))
            def _():
                acc[:, :width] = jnp.zeros((acc.shape[0], width), f32)

            for seq in range(1, n_seqs):
                rows = slice(seq * span, (seq + 1) * span)

                @pl.when(info_ref[0] < info_ref[1 + seq])
                def _(rows=rows):
                    acc[:, :width] += mm(left[rows, :], right[rows, :], TN)

        for level in range(grid.depth):
            half, at = level // middle, level % middle
            for whose, ref in ((core, mine_ref), (1 - core, theirs_ref)):
                start = pl.multiple_of((level * 2 + whose) * shard, shard)
                ref[half, 0, at, :, column : column + width] = acc[
                    pl.ds(start, shard), :width
                ].astype(bf16)
        column += width


def weight_grad(grid, info, span, *pairs):
    lefts, rights = [p[0] for p in pairs], [p[1] for p in pairs]
    rows, features = lefts[0].shape
    widths = [r.shape[1] for r in rights]
    total = sum(widths)
    part = features // grid.rows
    shard = part // grid.seqs
    middle = grid.depth // 2
    shape = jax.ShapeDtypeStruct((2, grid.rows, middle, shard, total), bf16)
    piece = pl.BlockSpec((2, 1, middle, shard, total), lambda i, *_: (0, i, 0, 0, 0))
    return pl.pallas_call(
        functools.partial(weight_kernel, grid, shard, span, len(pairs)),
        grid_spec=pltpu.PrefetchScalarGridSpec(
            num_scalar_prefetch=2,
            grid=(grid.rows,),
            in_specs=[pl.BlockSpec((rows, part), lambda i, place, info: (0, place[0] ^ i))]
            * len(pairs)
            + [pl.BlockSpec(r.shape, lambda i, *_: (0, 0)) for r in rights],
            out_specs=[piece, piece],
            scratch_shapes=[pltpu.VMEM((part, max(widths)), f32)],
        ),
        out_shape=[shape, shape],
        compiler_params=params(1),
        cost_estimate=pl.CostEstimate(
            flops=2 * rows * features * total,
            bytes_accessed=2 * (rows * (features * len(pairs) + total) + features * total),
            transcendentals=0,
        ),
    )(grid.place, info, *lefts, *rights)


def shards(
    n_rows,
    n_seqs,
    tokens,
    lengths,
    cotangent,
    w_qkv,
    w_out,
    w_gateup,
    w_down,
    norm_attn,
    norm_ffn,
    q_gain,
    k_gain,
):
    grid = Grid(n_rows, n_seqs)
    seq_count, span_len, model_width = tokens.shape
    row_count = seq_count * span_len
    head_dim = q_gain.shape[0]
    half_dim = head_dim // 2
    query_width = w_out.shape[1]
    kv_width = (w_qkv.shape[1] - query_width) // 2
    log2_scale = math.log2(math.e) * head_dim ** (-0.5)

    offset = (grid.seq * span_len).astype(jnp.int32)
    positions = offset + jnp.arange(span_len, dtype=jnp.int32)
    inverse = theta_base ** (-jnp.arange(half_dim, dtype=f32) * 2.0 / head_dim)
    angles = positions.astype(f32)[:, None] * inverse[None, :]
    cosine, sine = jnp.cos(angles), jnp.sin(angles)
    nothing = jnp.zeros_like(sine)
    tables = (
        jnp.concatenate([cosine] * 4, axis=1),
        jnp.concatenate([-sine, nothing] * 2, axis=1),
        jnp.concatenate([nothing, sine] * 2, axis=1),
    )
    q_gain_f = jnp.concatenate([q_gain.astype(f32)] * 2)[None, :]
    k_gain_f = jnp.concatenate([k_gain.astype(f32)] * 2)[None, :]
    info = jnp.concatenate([offset[None], lengths])

    attn_gain = norm_attn.astype(f32)[:, None]
    ffn_gain = norm_ffn.astype(f32)[:, None]
    qkv_shard = (w_qkv.astype(f32) * attn_gain).astype(bf16)
    gateup_shard = (w_gateup.astype(f32) * ffn_gain).astype(bf16)

    order = Order()
    depth = grid.depth
    split = max(1, depth // 2)
    kv_steps = grid.ring(qkv_shard[:, query_width:])
    kv_own, kv_came = grid.spread(kv_steps)
    q_steps = grid.ring(qkv_shard[:, :query_width], [[kv_steps[1]], [kv_steps[-1]]])[:3]
    feed_steps = grid.ring(
        jnp.concatenate([w_out, w_down, gateup_shard], axis=1), [[kv_steps[2]], kv_came[-1]]
    )[:3]
    kv_pieces = grid.with_partner(kv_own, feed_steps[1], q_steps[1])

    rows_in = tokens.reshape(row_count, model_width)
    kv, k_raw, scale1 = project(grid, rows_in, kv_pieces, k_gain_f, tables, kv_width, head_dim)
    order.leave(kv)
    while len(feed_steps) < depth:
        feed_steps.append(grid.around(after(feed_steps[-1], kv)))
        q_steps.append(grid.around(after(q_steps[-1], kv)))
    q_own, q_came = grid.spread(q_steps, [[kv]] + [feed_steps[2:3]] * (len(grid.orders[0]) - 1))
    feed_own, feed_came = grid.spread(feed_steps, [q_came[-1]])
    kv = kv.reshape(seq_count, span_len, 2 * kv_width)
    reach = [kv]
    for _ in range(split):
        reach.append(grid.up(reach[-1]))
    q_pieces = grid.with_partner(q_own, reach[1], feed_steps[-1])
    q, q_raw = project(
        grid,
        order.enter(rows_in),
        q_pieces,
        q_gain_f * log2_scale,
        tables,
        query_width,
        head_dim,
        scale1,
    )
    order.leave(q)
    q = q.reshape(seq_count, span_len, query_width)
    bases = []
    for step in range(depth):
        level = grid.level - step
        start = jnp.stack([level * 2 + grid.core, level * 2 + 1 - grid.core]) * span_len
        bases.append(jnp.where(level >= 0, start, -1).astype(jnp.int32))
    reach[split - 1] = order.late(reach[split - 1])
    crossed = [grid.partner(own) for own in reach[:split]]
    order.pin(*feed_came[0])
    feed_held = [grid.partner(order.late(feed_own[k])) for k in (0, 2)]
    near = [c for pair in zip(reach, crossed) for c in pair]
    acc = attend(info, jnp.concatenate(bases[:split]), order.enter(q), near, None, False)
    order.leave(acc)
    for step in range(split, depth):
        final = step == depth - 1
        reach[step] = order.late(reach[step])
        if final:
            order.pin(*feed_came[-1], *feed_held)
            feed_found = [grid.partner(order.late(feed_own[k])) for k in (1, 3)]
        else:
            reach.append(grid.up(reach[step]))
            order.pin(reach[step])
        crossed.append(grid.partner(reach[step]))
        result = attend(
            info, bases[step], order.enter(q), [reach[step], crossed[step]], acc, final
        )
        acc = result
        order.leave(result[0] if final else acc)
    heads, logs = result
    attended = heads.reshape(row_count, query_width)
    feed_pieces = feed_own + [feed_held[0], feed_found[0], feed_held[1], feed_found[1]]

    flat_cot = cotangent.reshape(row_count, model_width)
    output, hidden, middle, grad_gu, grad_mid, grad_heads, dots = feed(
        grid,
        info,
        rows_in,
        attended,
        flat_cot,
        feed_pieces,
        (query_width, w_gateup.shape[1]),
        span_len,
    )
    order.leave(hidden)
    grad_heads = grad_heads.reshape(seq_count, span_len, query_width)
    dots = dots.reshape(seq_count, span_len, query_width)

    def advance(*sums):
        for each in sums:
            order.pin(*each.land())
            order.pin(*each.go())

    kv_flight = []

    def kv_sum_here(own, other):
        kv_flight[:] = [order.late(came) for came in kv_flight]
        here = own.astype(f32) + other.astype(f32)
        for came in kv_flight:
            here = here + came.astype(f32)
        return here.astype(bf16)

    def kv_hop(own, other):
        sent = order.late(kv_sum_here(own, other))
        order.pin(sent)
        order.kernel = sent
        kv_flight[:] = [grid.down(sent)]

    def back(steps, acc, final):
        chosen = [reach[k] for k in steps] + [crossed[k] for k in steps]
        starts = jnp.stack([bases[k] for k in steps], axis=1).reshape(-1)
        return attend_back(
            info, starts, order.enter(q), grad_heads, dots, logs, chosen, acc, final
        )

    feed_sum = Sum(
        grid,
        order,
        weight_grad(
            grid,
            info,
            span_len,
            (flat_cot, order.enter(hidden)),
            (middle, grad_gu),
            (grad_mid, attended),
        ),
    )
    order.leave(feed_sum.theirs)
    advance(feed_sum)
    far_own, far_theirs, acc_q = back(range(split, depth), None, False)
    order.leave(acc_q)
    far_came = grid.partner(far_theirs)
    kv_hop(far_own[-1], far_came[-1])
    advance(feed_sum)
    near_own, near_theirs, grad_q = back(range(split), acc_q, True)
    order.leave(grad_q)
    near_came = grid.partner(order.late(near_theirs))
    for step in reversed(range(split, depth - 1)):
        kv_hop(far_own[step - split], far_came[step - split])
    advance(feed_sum)
    grad_pq, gq = unproject(
        info,
        order.enter(grad_q.reshape(row_count, query_width)),
        q_raw,
        scale1,
        q_gain_f,
        tables,
        head_dim,
    )
    order.leave(grad_pq)
    q_sum = Sum(
        grid, order, weight_grad(grid, info, span_len, (rows_in, order.enter(grad_pq))), True
    )
    order.leave(q_sum.theirs)
    for step in reversed(range(1, split)):
        kv_hop(near_own[step], near_came[step])
    advance(feed_sum, q_sum)
    back_q = query_back(grid, info, order.enter(grad_pq), q_pieces, model_width, span_len)
    order.leave(back_q)
    advance(feed_sum, q_sum)
    grad_kv = kv_sum_here(near_own[0], near_came[0]).reshape(row_count, 2 * kv_width)
    grad_pkv, gk = unproject(
        info, order.enter(grad_kv), k_raw, scale1, k_gain_f, tables, head_dim
    )
    kv_sum = Sum(grid, order, weight_grad(grid, info, span_len, (rows_in, grad_pkv)), True)
    order.leave(kv_sum.theirs)
    gain_sum = Everywhere(grid, order, jnp.concatenate([gq[:1], gk[:1]], axis=0))
    advance(feed_sum, q_sum, kv_sum, gain_sum)
    grad_tokens = last(
        grid,
        info,
        rows_in,
        order.enter(grad_pkv),
        back_q,
        grad_mid,
        scale1,
        kv_pieces,
        span_len,
    )
    order.leave(grad_tokens)
    gains = gain_sum.finish()
    gains = gains[:, :head_dim] + gains[:, head_dim:]
    kv_total, q_total, feed_total = kv_sum.finish(), q_sum.finish(), feed_sum.finish()
    sum_qkv = jnp.concatenate([q_total, kv_total], axis=1)
    sum_down, sum_gateup = feed_total[:, :query_width], feed_total[:, query_width:-query_width]
    sum_out = feed_total[:, -query_width:]
    return (
        output.reshape(tokens.shape),
        grad_tokens.reshape(tokens.shape),
        sum_qkv * attn_gain,
        sum_out,
        sum_gateup * ffn_gain,
        sum_down,
        jnp.sum(sum_qkv * w_qkv.astype(f32), axis=1),
        jnp.sum(sum_gateup * w_gateup.astype(f32), axis=1),
        gains[0],
        gains[1],
    )


def solution(mesh):
    rows = P("row", "seq", None)
    weight = P(both, None)
    vector = P(both)
    return jax.shard_map(
        functools.partial(shards, mesh.shape["row"], mesh.shape["seq"]),
        mesh=mesh,
        in_specs=(rows, P("row"), rows, weight, weight, weight, weight, vector, vector, P(), P()),
        out_specs=(rows, rows, weight, weight, weight, weight, vector, vector, P(), P()),
        check_vma=False,
    )
```
